32 devices in a mesh: energy: 8 (over y, x, core), blk: 4 (over z).
Axes of the slice: x: 2, y: 2, z: 4, core: 2. Of those that a mesh axis runs over, the one named last changes fastest.
Arguments:
- lesser_green: bfloat16 [16, 4, 2, 384, 384], P('energy', 'blk'), may hold values from -4.1875 to 4.1875
- greater_green: bfloat16 [16, 4, 2, 384, 384], P('energy', 'blk'), may hold values from -4.1875 to 4.1875
- coulomb_blocks: bfloat16 [4, 3, 2, 384, 384], P('blk'), may hold values from -0.21875 to 0.21875
Outputs:
- lesser_sigma: bfloat16 [16, 4, 2, 384, 384], P('energy', 'blk')
- greater_sigma: bfloat16 [16, 4, 2, 384, 384], P('energy', 'blk')
The draws below stay inside these ranges and needn't reach their ends.
All inputs are finite; a program needn't handle non-finite values.
Results may differ from the reference program's by a relative error of at most 0.017.
Values may be sent and summed in bfloat16 or wider, within the bound.
No kernel may reach another device: no remote copies, remote signals or barrier semaphores. Data moves between devices by JAX's collectives and lax.ppermute only.
A program may use at most 128 MiB of HBM per device.

```python
import math
import jax
import jax.numpy as jnp
from jax import lax

M = 384
NE = 16
BLOCKS = 4


def shard_levels(own_key, shape, split, low, high):
    loudness = 1.0
    for dim, parts in split:
        draws = jax.random.uniform(jax.random.fold_in(jax.random.fold_in(own_key, 6), dim), (parts,), jnp.float32, low / len(split), high / len(split))
        loudness = loudness * jnp.repeat(jnp.exp(draws), shape[dim] // parts).reshape((-1,) + (1,) * (len(shape) - 1 - dim))
    return loudness


def bell_draw(stream_key, extent, spread, limit, shards=(), dtype=jnp.bfloat16):
    entries = spread * jax.random.normal(stream_key, extent, jnp.float32)
    if shards:
        entries = entries * shard_levels(stream_key, extent, shards, -0.22, 0.18)
    return jnp.clip(entries, -limit, limit).astype(dtype)


def setup_inputs(seed: int = 0) -> dict:
    streams_of = jax.random.split(jax.random.key(seed), 4)
    lesser_green = bell_draw(streams_of[0], (NE, BLOCKS, 2, M, M), 0.7, 4.1875, ((0, 8), (1, 4)))
    greater_green = bell_draw(streams_of[1], (NE, BLOCKS, 2, M, M), 0.7, 4.1875, ((0, 8), (1, 4)))
    coulomb_blocks = bell_draw(streams_of[2], (BLOCKS, 3, 2, M, M), (2 * M) ** -0.5, 0.21875, ((0, 4),))
    return {"lesser_green": lesser_green, "greater_green": greater_green, "coulomb_blocks": coulomb_blocks}


top_precision = lax.Precision.HIGHEST

def as_complex(pair):
    return pair[:, 0].astype(jnp.float32) + 1j * pair[:, 1].astype(jnp.float32)

def as_pair(values):
    return jnp.stack([jnp.real(values), jnp.imag(values)], axis=1).astype(jnp.bfloat16)

def product(first, second, form):
    return jnp.einsum(form, first, second, precision=top_precision)

def rounded(values):
    return lax.optimization_barrier(values.astype(jnp.bfloat16)).astype(jnp.float32)

def congruence(coupling, polar):
    coul_re = coupling[0].astype(jnp.float32)
    coul_im = coupling[1].astype(jnp.float32)
    pol_re = polar[:, 0].astype(jnp.float32)
    pol_im = polar[:, 1].astype(jnp.float32)
    left_re = rounded(product(coul_re, pol_re, 'ij,ejk->eik') - product(coul_im, pol_im, 'ij,ejk->eik'))
    left_im = rounded(product(coul_re, pol_im, 'ij,ejk->eik') + product(coul_im, pol_re, 'ij,ejk->eik'))
    right_re = product(left_re, coul_re, 'eik,jk->eij') + product(left_im, coul_im, 'eik,jk->eij')
    right_im = product(left_im, coul_re, 'eik,jk->eij') - product(left_re, coul_im, 'eik,jk->eij')
    return (right_re, right_im)

def reference(lesser_green, greater_green, coulomb_blocks):
    length = 2 * NE
    factor = 1.0 / math.sqrt(NE)
    less_specs = []
    great_specs = []
    pol_less = []
    pol_great = []
    for block in range(BLOCKS):
        less_spec = jnp.fft.fft(as_complex(lesser_green[:, block]), n=length, axis=0)
        great_spec = jnp.fft.fft(as_complex(greater_green[:, block]), n=length, axis=0)
        less_specs.append(less_spec)
        great_specs.append(great_spec)
        cross = less_spec * jnp.conj(great_spec)
        pol_less.append(as_pair(-factor * jnp.fft.ifft(cross, axis=0)[:NE]))
        pol_great.append(as_pair(-factor * jnp.fft.ifft(jnp.conj(cross), axis=0)[:NE]))
    outputs = []
    for kind_list, spec_list in ((pol_less, less_specs), (pol_great, great_specs)):
        stacked = jnp.stack(kind_list, axis=1)
        padded = jnp.pad(stacked, ((0, 0), (1, 1), (0, 0), (0, 0), (0, 0)))
        sigma_list = []
        for block in range(BLOCKS):
            total_re = jnp.zeros((NE, M, M), jnp.float32)
            total_im = jnp.zeros((NE, M, M), jnp.float32)
            for offset in range(3):
                right_re, right_im = congruence(coulomb_blocks[block, offset], padded[:, block + offset])
                total_re = total_re + right_re
                total_im = total_im + right_im
            screen = as_complex(jnp.stack([total_re, total_im], axis=1).astype(jnp.bfloat16))
            screen_spec = jnp.fft.fft(screen, n=length, axis=0)
            sigma = factor * jnp.fft.ifft(spec_list[block] * screen_spec, axis=0)[:NE]
            sigma_list.append(as_pair(sigma))
        outputs.append(jnp.stack(sigma_list, axis=1))
    return (outputs[0], outputs[1])
```

```python
import functools
import math

import jax
import jax.numpy as jnp
from jax import lax
from jax.experimental import pallas as pl
from jax.experimental.pallas import tpu as pltpu
from jax.sharding import PartitionSpec as P

f32 = jnp.float32
bf16 = jnp.bfloat16


def swap(value, distance):
    count = lax.axis_size("energy")
    return lax.ppermute(value, "energy", [(i, i ^ distance) for i in range(count)])


def shift(value, step):
    count = lax.axis_size("blk")
    pairs = [(i, i + step) for i in range(count) if 0 <= i + step < count]
    return lax.ppermute(value, "blk", pairs)


def row_block(rows):
    for size in (16, 8):
        if rows % size == 0:
            return size
    return rows


def out_like(shape):
    return jax.ShapeDtypeStruct(shape, bf16)


def vpu_cost(total, elements, moved):
    return pl.CostEstimate(
        flops=3 * total * (total + 1) * elements, bytes_accessed=2 * moved, transcendentals=0
    )


def tiles(rows, cols, body):
    lanes = 128 if cols % 128 == 0 else cols
    sub = 8 if rows % 8 == 0 else rows
    across = cols // lanes

    def step(t, carry):
        r = pl.multiple_of(lax.div(t, across) * sub, sub)
        c = pl.multiple_of(lax.rem(t, across) * lanes, lanes)
        body((pl.ds(r, sub), pl.ds(c, lanes)))
        return carry

    lax.fori_loop(0, (rows // sub) * across, step, 0)


def correlate_kernel(slots, inner, where, mine, sib, *rest):
    outs, (x_scr, y_scr, o_scr) = rest[:slots], rest[slots:]
    chip, core = where[0], where[1]
    total = 2 * inner * slots
    rows, cols = mine.shape[-2:]
    for j in range(slots):
        for side, source in enumerate((mine, sib)):
            half = core if side == 0 else 1 - core
            for i in range(inner):
                e = (2 * (chip ^ j) + half) * inner + i
                a = source[j, i, core, 0].astype(f32)
                b = source[j, i, core, 1].astype(f32)
                x_scr[0, e], x_scr[1, e], x_scr[2, e] = a, b, a + b
                a = source[j, i, 1 - core, 0].astype(f32)
                b = source[j, i, 1 - core, 1].astype(f32)
                y_scr[0, e], y_scr[1, e], y_scr[2, e] = a, b, a - b
    factor = -1.0 / math.sqrt(total)
    width = 4

    def body(at):
        for base in range(0, total, width):
            lags = range(base, min(base + width, total))
            sums = {}
            window = {}
            for e in range(total - base):
                y = [y_scr[(p, e) + at] for p in range(3)]
                for w in lags:
                    if e + w >= total:
                        continue
                    if e + w not in window:
                        window[e + w] = [x_scr[(p, e + w) + at] for p in range(3)]
                    terms = [window[e + w][p] * y[p] for p in range(3)]
                    sums[w] = [s + t for s, t in zip(sums[w], terms)] if w in sums else terms
                window.pop(e + base, None)
            for w in lags:
                first, second, third = sums[w]
                o_scr[(w, 0) + at] = factor * (first + second)
                o_scr[(w, 1) + at] = factor * (third - first + second)

    tiles(rows, cols, body)
    per = 2 * inner
    for j in range(slots):
        for i in range(per):
            outs[j][i] = o_scr[(chip ^ j) * per + i].astype(bf16)


def correlate(where, mine, sib):
    slots, inner, _, _, rows, cols = mine.shape
    total = 2 * inner * slots
    block = row_block(rows)
    in_spec = pl.BlockSpec((slots, inner, 2, 2, block, cols), lambda r, s: (0, 0, 0, 0, r, 0))
    out_spec = pl.BlockSpec((2 * inner, 2, block, cols), lambda r, s: (0, 0, r, 0))
    return pl.pallas_call(
        functools.partial(correlate_kernel, slots, inner),
        out_shape=[out_like((2 * inner, 2, rows, cols))] * slots,
        grid_spec=pltpu.PrefetchScalarGridSpec(
            num_scalar_prefetch=1,
            grid=(rows // block,),
            in_specs=[in_spec, in_spec],
            out_specs=[out_spec] * slots,
            scratch_shapes=[
                pltpu.VMEM((3, total, block, cols), f32),
                pltpu.VMEM((3, total, block, cols), f32),
                pltpu.VMEM((total, 2, block, cols), f32),
            ],
        ),
        compiler_params=pltpu.CompilerParams(vmem_limit_bytes=32 * 2**20),
        cost_estimate=vpu_cost(total, rows * cols, 2 * 3 * mine.size),
    )(where, mine, sib)


def sigma_kernel(slots, inner, chunks, where, mine, sib, *rest):
    screens = rest[: slots * chunks]
    outs = rest[slots * chunks : slots * chunks + slots]
    x_scr, y_scr, o_scr = rest[slots * chunks + slots :]
    chip, core = where[0], where[1]
    total = 2 * inner * slots
    rows, cols = mine.shape[-2:]
    per = 2 * inner
    each = per // chunks
    for j in range(slots):
        for side, source in enumerate((mine, sib)):
            half = core if side == 0 else 1 - core
            for i in range(inner):
                e = (2 * (chip ^ j) + half) * inner + i
                a = source[j, i, 0, 0].astype(f32)
                b = source[j, i, 0, 1].astype(f32)
                x_scr[0, e], x_scr[1, e], x_scr[2, e] = a, b, a + b
        for m in range(chunks):
            source = screens[m * slots + j]
            for i in range(each):
                w = (chip ^ j) * per + m * each + i
                a = source[i, 0].astype(f32)
                b = source[i, 1].astype(f32)
                y_scr[0, w], y_scr[1, w], y_scr[2, w] = a, b, a + b
    factor = 1.0 / math.sqrt(total)
    width = 4

    def body(at):
        for base in range(0, total, width):
            energies = range(base, min(base + width, total))
            sums = {}
            window = {}
            for w in range(base + width):
                if w >= total:
                    continue
                y = [y_scr[(p, w) + at] for p in range(3)]
                for e in energies:
                    if e < w:
                        continue
                    if e - w not in window:
                        window[e - w] = [x_scr[(p, e - w) + at] for p in range(3)]
                    terms = [window[e - w][p] * y[p] for p in range(3)]
                    sums[e] = [s + t for s, t in zip(sums[e], terms)] if e in sums else terms
                window.pop(base + width - 1 - w, None)
            for e in energies:
                first, second, third = sums[e]
                o_scr[(e, 0) + at] = factor * (first - second)
                o_scr[(e, 1) + at] = factor * (third - first - second)

    tiles(rows, cols, body)
    for j in range(slots):
        for side in range(2):
            half = core if side == 0 else 1 - core
            for i in range(inner):
                e = (2 * (chip ^ j) + half) * inner + i
                outs[j][side, i] = o_scr[e].astype(bf16)


def self_energy(where, mine, sib, screens, part):
    slots, inner, _, _, rows, cols = mine.shape
    chunks = len(screens)
    flat = [piece for chunk in screens for piece in chunk]
    each = flat[0].shape[0]
    total = 2 * inner * slots
    block = row_block(rows)
    steps = rows // block
    green_spec = pl.BlockSpec(
        (slots, inner, 1, 2, block, cols), lambda r, s: (0, 0, s[1], 0, r, 0)
    )
    screen_spec = pl.BlockSpec((each, 2, block, cols), lambda r, s: (0, 0, part * steps + r, 0))
    out_spec = pl.BlockSpec((2, inner, 2, block, cols), lambda r, s: (0, 0, 0, r, 0))
    return pl.pallas_call(
        functools.partial(sigma_kernel, slots, inner, chunks),
        out_shape=[out_like((2, inner, 2, rows, cols))] * slots,
        grid_spec=pltpu.PrefetchScalarGridSpec(
            num_scalar_prefetch=1,
            grid=(steps,),
            in_specs=[green_spec, green_spec] + [screen_spec] * len(flat),
            out_specs=[out_spec] * slots,
            scratch_shapes=[
                pltpu.VMEM((3, total, block, cols), f32),
                pltpu.VMEM((3, total, block, cols), f32),
                pltpu.VMEM((total, 2, block, cols), f32),
            ],
        ),
        compiler_params=pltpu.CompilerParams(vmem_limit_bytes=32 * 2**20),
        cost_estimate=vpu_cost(total, rows * cols, 3 * mine.size),
    )(where, mine, sib, *flat)


def screen_kernel(slots, low, own, high, left_ref, right_ref, *rest):
    outs, (pol, left) = rest[:slots], rest[slots:]
    each, depth, m = own.shape
    group = m // slots
    for o, source in enumerate((low, own, high)):
        for i in range(each):
            pol[:, i * m : (i + 1) * m] = source[i]
        product = jnp.dot(left_ref[o], pol[...], preferred_element_type=f32).astype(bf16)
        for i in range(each):
            for part in range(2):
                left[i, :, (2 * o + part) * m : (2 * o + part + 1) * m] = product[
                    part * m : (part + 1) * m, i * m : (i + 1) * m
                ]
    for i in range(each):
        result = jnp.dot(left[i], right_ref[...], preferred_element_type=f32).astype(bf16)
        for j in range(slots):
            for part in range(2):
                outs[j][i, part] = result[
                    j * group : (j + 1) * group, part * m : (part + 1) * m
                ]


def screen(low, own, high, left_matrix, right_matrix, slots):
    each, depth, m = own.shape
    group = m // slots
    vmem = pl.BlockSpec(memory_space=pltpu.VMEM)
    flops = 2 * each * (3 * depth * depth * m + 3 * m * depth * depth)
    moved = 2 * (3 * own.size + left_matrix.size + right_matrix.size + 2 * each * m * m)
    return pl.pallas_call(
        functools.partial(screen_kernel, slots),
        out_shape=[out_like((each, 2, group, m))] * slots,
        in_specs=[vmem] * 5,
        out_specs=[vmem] * slots,
        scratch_shapes=[pltpu.VMEM((depth, each * m), bf16), pltpu.VMEM((each, m, 3 * depth), bf16)],
        compiler_params=pltpu.CompilerParams(vmem_limit_bytes=40 * 2**20),
        cost_estimate=pl.CostEstimate(flops=flops, bytes_accessed=moved, transcendentals=0),
    )(low, own, high, left_matrix, right_matrix)


def collect_kernel(slots, parts, inner, group, where, *rest):
    count = slots * parts
    own, other = rest[:count], rest[count : count + parts]
    less, great, sems = rest[count + parts :]
    chip, core = where[0], where[1]
    rows = group // parts

    def gather(own_out, other_out):
        copies = []
        for h in range(parts):
            for j in range(slots):
                start = pl.multiple_of((chip ^ j) * group + h * rows, rows)
                for kind, (source, target) in enumerate(
                    ((own[h * slots + j].at[0], own_out), (other[h].at[j], other_out))
                ):
                    copies.append(
                        pltpu.make_async_copy(
                            source,
                            target.at[:, 0, :, pl.ds(start, rows), :],
                            sems.at[kind, h * slots + j],
                        )
                    )
        for copy in copies:
            copy.start()
        for copy in copies:
            copy.wait()

    @pl.when(core == 0)
    def _():
        gather(less, great)

    @pl.when(core != 0)
    def _():
        gather(great, less)


def collect(where, own, other, inner, m):
    parts, slots = len(own), len(own[0])
    flat = [piece for pieces in own for piece in pieces]
    anywhere = pl.BlockSpec(memory_space=pl.ANY)
    shape = (inner, 1, 2, m, m)
    return pl.pallas_call(
        functools.partial(collect_kernel, slots, parts, inner, m // slots),
        out_shape=[out_like(shape)] * 2,
        in_specs=[pl.BlockSpec(memory_space=pltpu.SMEM)] + [anywhere] * (len(flat) + parts),
        out_specs=[anywhere] * 2,
        scratch_shapes=[pltpu.SemaphoreType.DMA((2, slots * parts))],
        cost_estimate=pl.CostEstimate(flops=0, bytes_accessed=8 * inner * m * m * 2, transcendentals=0),
    )(where, *flat, *other)


def coupling_matrices(coulomb, chip, slots, parts):
    count, _, m, _ = coulomb.shape
    group = m // slots
    rows = group // parts
    real, imag = coulomb[:, 0], coulomb[:, 1]
    place = lax.iota(jnp.int32, 2 * m)
    row = place % rows
    kind = place // rows % 2
    slot = place // (2 * rows) % slots
    part = place // (2 * rows * slots)
    natural = (slot ^ chip) * group + part * rows + row
    index = lax.iota(jnp.int32, m)[:, None]
    hit = index == natural[None, :]
    pick_re = jnp.where(hit & (kind == 0), 1.0, 0.0).astype(bf16)
    pick_im = jnp.where(hit & (kind == 1), 1.0, 0.0).astype(bf16)

    def ordered(matrix):
        pieces = [
            lax.dynamic_slice_in_dim(matrix, (chip ^ j) * group, group, axis=1) for j in range(slots)
        ]
        return jnp.concatenate(pieces, axis=1)

    real_rows, imag_rows = ordered(real), ordered(imag)
    stacked_re = jnp.concatenate([real_rows, imag_rows], axis=1)
    stacked_im = jnp.concatenate([-imag_rows, real_rows], axis=1)
    left = (
        jnp.einsum("oik,kl->oil", stacked_re, pick_re, preferred_element_type=f32)
        + jnp.einsum("oik,kl->oil", stacked_im, pick_im, preferred_element_type=f32)
    ).astype(bf16)
    real_t, imag_t = jnp.swapaxes(real, 1, 2), jnp.swapaxes(imag, 1, 2)
    right = jnp.concatenate(
        [
            jnp.concatenate([real_t, -imag_t], axis=2),
            jnp.concatenate([imag_t, real_t], axis=2),
        ],
        axis=1,
    ).reshape(count * 2 * m, 2 * m)
    return left, right


def local(lesser_green, greater_green, coulomb_blocks):
    pieces = lax.axis_size("energy")
    slots = pieces // 2
    inner, _, _, m, _ = lesser_green.shape
    group = m // slots
    parts = 2 if group % 32 == 0 else 1
    rows = group // parts
    chunks = 2
    per = 2 * inner
    each = per // chunks
    index = lax.axis_index("energy")
    chip, core = index // 2, index % 2
    where = jnp.stack([chip, core]).astype(jnp.int32)

    def green_piece(h, j):
        start = (chip ^ j) * group + h * rows
        return jnp.stack(
            [lax.dynamic_slice_in_dim(g[:, 0], start, rows, axis=2) for g in (lesser_green, greater_green)],
            axis=1,
        )

    mine, sib = [], []
    for h in range(parts):
        got = [green_piece(h, 0)] + [swap(green_piece(h, j), 2 * j) for j in range(1, slots)]
        mine.append(jnp.stack(got))
        sib.append(swap(mine[h], 1))

    left, right = coupling_matrices(coulomb_blocks[0], chip, slots, parts)

    pol = []
    for h in range(parts):
        found = correlate(where, mine[h], sib[h])
        pol.append([found[0]] + [swap(found[j], 2 * j) for j in range(1, slots)])

    screens = []
    for c in range(chunks):
        own = jnp.concatenate(
            [pol[h][j][c * each : (c + 1) * each] for h in range(parts) for j in range(slots)], axis=1
        ).reshape(each, 2 * m, m)
        low, high = shift(own, 1), shift(own, -1)
        found = screen(low, own, high, left, right, slots)
        screens.append([found[0]] + [swap(found[j], 2 * j) for j in range(1, slots)])

    own, other = [], []
    for h in range(parts):
        found = self_energy(where, mine[h], sib[h], screens, h)
        own.append([found[0]] + [swap(found[j], 2 * j) for j in range(1, slots)])
        other.append(swap(jnp.stack([piece[1] for piece in own[h]]), 1))
    return tuple(collect(where, own, other, inner, m))


def solution(mesh):
    return jax.shard_map(
        local,
        mesh=mesh,
        in_specs=(
            P("energy", "blk", None, None, None),
            P("energy", "blk", None, None, None),
            P("blk", None, None, None, None),
        ),
        out_specs=(P("energy", "blk", None, None, None), P("energy", "blk", None, None, None)),
        check_vma=False,
    )
```

```python
import functools
import math

import jax
import jax.numpy as jnp
from jax import lax
from jax.experimental import pallas as pl
from jax.experimental.pallas import tpu as pltpu
from jax.sharding import PartitionSpec as P

f32 = jnp.float32
bf16 = jnp.bfloat16


def swap(value, distance):
    count = lax.axis_size("energy")
    return lax.ppermute(value, "energy", [(i, i ^ distance) for i in range(count)])


def shift(value, step):
    count = lax.axis_size("blk")
    pairs = [(i, i + step) for i in range(count) if 0 <= i + step < count]
    return lax.ppermute(value, "blk", pairs)


def row_block(rows):
    for size in (16, 8):
        if rows % size == 0:
            return size
    return rows


def out_like(shape):
    return jax.ShapeDtypeStruct(shape, bf16)


def vpu_cost(total, elements, moved):
    return pl.CostEstimate(
        flops=3 * total * (total + 1) * elements, bytes_accessed=2 * moved, transcendentals=0
    )


def tiles(rows, cols, body):
    lanes = 128 if cols % 128 == 0 else cols
    sub = 8 if rows % 8 == 0 else rows
    across = cols // lanes

    def step(t, carry):
        r = pl.multiple_of(lax.div(t, across) * sub, sub)
        c = pl.multiple_of(lax.rem(t, across) * lanes, lanes)
        body((pl.ds(r, sub), pl.ds(c, lanes)))
        return carry

    lax.fori_loop(0, (rows // sub) * across, step, 0)


def correlate_kernel(slots, inner, where, mine, sib, *rest):
    outs, (x_scr, y_scr, o_scr) = rest[:slots], rest[slots:]
    chip, core = where[0], where[1]
    total = 2 * inner * slots
    rows, cols = mine.shape[-2:]
    for j in range(slots):
        for side, source in enumerate((mine, sib)):
            half = core if side == 0 else 1 - core
            for i in range(inner):
                e = (2 * (chip ^ j) + half) * inner + i
                a = source[j, i, core, 0].astype(f32)
                b = source[j, i, core, 1].astype(f32)
                x_scr[0, e], x_scr[1, e], x_scr[2, e] = a, b, a + b
                a = source[j, i, 1 - core, 0].astype(f32)
                b = source[j, i, 1 - core, 1].astype(f32)
                y_scr[0, e], y_scr[1, e], y_scr[2, e] = a, b, a - b
    factor = -1.0 / math.sqrt(total)
    width = 4

    def body(at):
        for base in range(0, total, width):
            lags = range(base, min(base + width, total))
            sums = {}
            window = {}
            for e in range(total - base):
                y = [y_scr[(p, e) + at] for p in range(3)]
                for w in lags:
                    if e + w >= total:
                        continue
                    if e + w not in window:
                        window[e + w] = [x_scr[(p, e + w) + at] for p in range(3)]
                    terms = [window[e + w][p] * y[p] for p in range(3)]
                    sums[w] = [s + t for s, t in zip(sums[w], terms)] if w in sums else terms
                window.pop(e + base, None)
            for w in lags:
                first, second, third = sums[w]
                o_scr[(w, 0) + at] = factor * (first + second)
                o_scr[(w, 1) + at] = factor * (third - first + second)

    tiles(rows, cols, body)
    per = 2 * inner
    for j in range(slots):
        for i in range(per):
            outs[j][i] = o_scr[(chip ^ j) * per + i].astype(bf16)


def correlate(where, mine, sib):
    slots, inner, _, _, rows, cols = mine.shape
    total = 2 * inner * slots
    block = row_block(rows)
    in_spec = pl.BlockSpec((slots, inner, 2, 2, block, cols), lambda r, s: (0, 0, 0, 0, r, 0))
    out_spec = pl.BlockSpec((2 * inner, 2, block, cols), lambda r, s: (0, 0, r, 0))
    return pl.pallas_call(
        functools.partial(correlate_kernel, slots, inner),
        out_shape=[out_like((2 * inner, 2, rows, cols))] * slots,
        grid_spec=pltpu.PrefetchScalarGridSpec(
            num_scalar_prefetch=1,
            grid=(rows // block,),
            in_specs=[in_spec, in_spec],
            out_specs=[out_spec] * slots,
            scratch_shapes=[
                pltpu.VMEM((3, total, block, cols), f32),
                pltpu.VMEM((3, total, block, cols), f32),
                pltpu.VMEM((total, 2, block, cols), f32),
            ],
        ),
        compiler_params=pltpu.CompilerParams(vmem_limit_bytes=32 * 2**20),
        cost_estimate=vpu_cost(total, rows * cols, 2 * 3 * mine.size),
    )(where, mine, sib)


def sigma_kernel(slots, inner, chunks, where, mine, sib, *rest):
    screens = rest[: slots * chunks]
    outs = rest[slots * chunks : slots * chunks + slots]
    x_scr, y_scr, o_scr = rest[slots * chunks + slots :]
    chip, core = where[0], where[1]
    total = 2 * inner * slots
    rows, cols = mine.shape[-2:]
    per = 2 * inner
    each = per // chunks
    for j in range(slots):
        for side, source in enumerate((mine, sib)):
            half = core if side == 0 else 1 - core
            for i in range(inner):
                e = (2 * (chip ^ j) + half) * inner + i
                a = source[j, i, 0, 0].astype(f32)
                b = source[j, i, 0, 1].astype(f32)
                x_scr[0, e], x_scr[1, e], x_scr[2, e] = a, b, a + b
        for m in range(chunks):
            source = screens[m * slots + j]
            for i in range(each):
                w = (chip ^ j) * per + m * each + i
                a = source[i, 0].astype(f32)
                b = source[i, 1].astype(f32)
                y_scr[0, w], y_scr[1, w], y_scr[2, w] = a, b, a + b
    factor = 1.0 / math.sqrt(total)
    width = 4

    def body(at):
        for base in range(0, total, width):
            energies = range(base, min(base + width, total))
            sums = {}
            window = {}
            for w in range(base + width):
                if w >= total:
                    continue
                y = [y_scr[(p, w) + at] for p in range(3)]
                for e in energies:
                    if e < w:
                        continue
                    if e - w not in window:
                        window[e - w] = [x_scr[(p, e - w) + at] for p in range(3)]
                    terms = [window[e - w][p] * y[p] for p in range(3)]
                    sums[e] = [s + t for s, t in zip(sums[e], terms)] if e in sums else terms
                window.pop(base + width - 1 - w, None)
            for e in energies:
                first, second, third = sums[e]
                o_scr[(e, 0) + at] = factor * (first - second)
                o_scr[(e, 1) + at] = factor * (third - first - second)

    tiles(rows, cols, body)
    for j in range(slots):
        for side in range(2):
            half = core if side == 0 else 1 - core
            for i in range(inner):
                e = (2 * (chip ^ j) + half) * inner + i
                outs[j][side, i] = o_scr[e].astype(bf16)


def self_energy(where, mine, sib, screens, part):
    slots, inner, _, _, rows, cols = mine.shape
    chunks = len(screens)
    flat = [piece for chunk in screens for piece in chunk]
    each = flat[0].shape[0]
    total = 2 * inner * slots
    block = row_block(rows)
    steps = rows // block
    green_spec = pl.BlockSpec(
        (slots, inner, 1, 2, block, cols), lambda r, s: (0, 0, s[1], 0, r, 0)
    )
    screen_spec = pl.BlockSpec((each, 2, block, cols), lambda r, s: (0, 0, part * steps + r, 0))
    out_spec = pl.BlockSpec((2, inner, 2, block, cols), lambda r, s: (0, 0, 0, r, 0))
    return pl.pallas_call(
        functools.partial(sigma_kernel, slots, inner, chunks),
        out_shape=[out_like((2, inner, 2, rows, cols))] * slots,
        grid_spec=pltpu.PrefetchScalarGridSpec(
            num_scalar_prefetch=1,
            grid=(steps,),
            in_specs=[green_spec, green_spec] + [screen_spec] * len(flat),
            out_specs=[out_spec] * slots,
            scratch_shapes=[
                pltpu.VMEM((3, total, block, cols), f32),
                pltpu.VMEM((3, total, block, cols), f32),
                pltpu.VMEM((total, 2, block, cols), f32),
            ],
        ),
        compiler_params=pltpu.CompilerParams(vmem_limit_bytes=32 * 2**20),
        cost_estimate=vpu_cost(total, rows * cols, 3 * mine.size),
    )(where, mine, sib, *flat)


def cut_kernel(slots, where, *rest):
    for j in range(slots):
        for kind in range(2):
            rest[2 * slots + j][0, kind] = rest[kind * slots + j][0, 0]


def cut(where, greens, part, slots, rows):
    inner, _, _, m, _ = greens[0].shape
    parts = m // (slots * rows)
    if rows % 16:
        return [
            jnp.stack(
                [
                    lax.dynamic_slice_in_dim(g[:, 0], ((where[0] ^ j) * parts + part) * rows, rows, axis=2)
                    for g in greens
                ],
                axis=1,
            )
            for j in range(slots)
        ]

    def block(j):
        return pl.BlockSpec(
            (1, 1, 2, rows, m), lambda e, s: (e, 0, 0, (s[0] ^ j) * parts + part, 0)
        )

    return pl.pallas_call(
        functools.partial(cut_kernel, slots),
        out_shape=[out_like((inner, 2, 2, rows, m))] * slots,
        grid_spec=pltpu.PrefetchScalarGridSpec(
            num_scalar_prefetch=1,
            grid=(inner,),
            in_specs=[block(j) for j in range(slots)] * 2,
            out_specs=[pl.BlockSpec((1, 2, 2, rows, m), lambda e, s: (e, 0, 0, 0, 0))] * slots,
        ),
        compiler_params=pltpu.CompilerParams(vmem_limit_bytes=16 * 2**20),
        cost_estimate=pl.CostEstimate(
            flops=0, bytes_accessed=16 * inner * slots * rows * m, transcendentals=0
        ),
    )(where, *([greens[0]] * slots), *([greens[1]] * slots))


def matrices_kernel(slots, where, coupling, left, right, *held):
    count, _, m, _ = coupling.shape
    group = m // slots
    chip = where[0]
    for o in range(count):
        real, imag = coupling[o, 0].astype(f32), coupling[o, 1].astype(f32)
        real_t, imag_t = real.T.astype(bf16), imag.T.astype(bf16)
        base = 2 * m * o
        right[base : base + m, :m] = real_t
        right[base : base + m, m:] = -imag_t
        right[base + m : base + 2 * m, :m] = imag_t
        right[base + m : base + 2 * m, m:] = real_t
        if held:
            held[0][0], held[0][1] = real, imag
            source = held[0]
        else:
            source = coupling.at[o]
        for j in range(slots):
            start = pl.multiple_of((chip ^ j) * group, group)
            real = source[0, pl.ds(start, group), :].astype(bf16)
            imag = source[1, pl.ds(start, group), :].astype(bf16)
            low = j * group
            left[o, low : low + group, :m] = real
            left[o, low : low + group, m:] = -imag
            left[o, m + low : m + low + group, :m] = imag
            left[o, m + low : m + low + group, m:] = real


def coupling_matrices(where, coulomb, slots):
    count, _, m, _ = coulomb.shape
    vmem = pl.BlockSpec(memory_space=pltpu.VMEM)
    held = [] if (m // slots) % 16 == 0 else [pltpu.VMEM((2, m, m), f32)]
    return pl.pallas_call(
        functools.partial(matrices_kernel, slots),
        out_shape=[out_like((count, 2 * m, 2 * m)), out_like((count * 2 * m, 2 * m))],
        in_specs=[pl.BlockSpec(memory_space=pltpu.SMEM), vmem],
        out_specs=[vmem, vmem],
        scratch_shapes=held,
        compiler_params=pltpu.CompilerParams(vmem_limit_bytes=24 * 2**20),
        cost_estimate=pl.CostEstimate(flops=0, bytes_accessed=20 * coulomb.size, transcendentals=0),
    )(where, coulomb)


def pack_kernel(pieces, *refs):
    for k in range(pieces):
        refs[pieces][k] = refs[k][...]


def pack(pieces, chunk, each):
    _, _, rows, m = pieces[0].shape
    count = len(pieces)
    block = (each, 2, rows, m)
    return pl.pallas_call(
        functools.partial(pack_kernel, count),
        out_shape=out_like((count,) + block),
        grid=(1,),
        in_specs=[pl.BlockSpec(block, lambda i: (chunk, 0, 0, 0))] * count,
        out_specs=pl.BlockSpec((count,) + block, lambda i: (0, 0, 0, 0, 0)),
        compiler_params=pltpu.CompilerParams(vmem_limit_bytes=16 * 2**20),
        cost_estimate=pl.CostEstimate(
            flops=0, bytes_accessed=8 * count * each * rows * m, transcendentals=0
        ),
    )(*pieces)


def screen_kernel(slots, parts, chunk, where, left_ref, right_ref, *rest):
    per_source = parts + 1
    sources = [rest[o * per_source : (o + 1) * per_source] for o in range(3)]
    outs = rest[3 * per_source : 3 * per_source + slots]
    pol, left = rest[3 * per_source + slots :]
    each, _, rows, m = sources[0][parts].shape[1:]
    group = m // slots
    chip = where[0]
    for o, source in enumerate(sources):
        for h in range(parts):
            for j in range(slots):
                for part in range(2):
                    start = part * m + (chip ^ j) * group + h * rows
                    start = pl.multiple_of(start, rows)
                    for i in range(each):
                        if j == 0:
                            piece = source[h][chunk * each + i, part]
                        else:
                            piece = source[parts][h * (slots - 1) + j - 1, i, part]
                        pol[o, i, pl.ds(start, rows), :] = piece.astype(pol.dtype)
    for o in range(3):
        both = jnp.concatenate([pol[o, i].astype(bf16) for i in range(each)], axis=1)
        product = jnp.dot(left_ref[o], both, preferred_element_type=f32).astype(bf16)
        for i in range(each):
            for part in range(2):
                left[i, :, (2 * o + part) * m : (2 * o + part + 1) * m] = product[
                    part * m : (part + 1) * m, i * m : (i + 1) * m
                ]
    for i in range(each):
        result = jnp.dot(left[i], right_ref[...], preferred_element_type=f32).astype(bf16)
        for j in range(slots):
            for part in range(2):
                outs[j][i, part] = result[
                    j * group : (j + 1) * group, part * m : (part + 1) * m
                ]


def screen(where, left_matrix, right_matrix, sources, chunk, slots):
    parts = len(sources[0]) - 1
    _, each, _, rows, m = sources[0][parts].shape
    group = m // slots
    vmem = pl.BlockSpec(memory_space=pltpu.VMEM)
    flops = 2 * each * (6 * 2 * m * 2 * m * m)
    moved = 2 * (3 * each * 2 * m * m + left_matrix.size + right_matrix.size + 2 * each * m * m)
    hold = bf16 if rows % 16 == 0 else f32
    flat = [piece for source in sources for piece in source]
    return pl.pallas_call(
        functools.partial(screen_kernel, slots, parts, chunk),
        out_shape=[out_like((each, 2, group, m))] * slots,
        in_specs=[pl.BlockSpec(memory_space=pltpu.SMEM)] + [vmem] * (2 + len(flat)),
        out_specs=[vmem] * slots,
        scratch_shapes=[
            pltpu.VMEM((3, each, 2 * m, m), hold),
            pltpu.VMEM((each, m, 6 * m), bf16),
        ],
        compiler_params=pltpu.CompilerParams(vmem_limit_bytes=44 * 2**20),
        cost_estimate=pl.CostEstimate(flops=flops, bytes_accessed=moved, transcendentals=0),
    )(where, left_matrix, right_matrix, *flat)


def collect_kernel(slots, parts, where, *rest):
    count = slots * parts
    own, other = rest[:count], rest[count : count + parts]
    less, great = rest[count + parts :]
    core = where[1]
    for k in range(count):

        @pl.when(pl.program_id(0) == k)
        def _(k=k):
            h, j = divmod(k, slots)
            mine, theirs = own[k][0], other[h][j]
            less[:, 0] = jnp.where(core == 0, mine, theirs)
            great[:, 0] = jnp.where(core == 0, theirs, mine)


def collect(where, own, other, inner, m):
    parts, slots = len(own), len(own[0])
    rows = m // (slots * parts)
    if rows % 16:
        target = jnp.zeros((2, inner, 1, 2, m, m), bf16)
        for h in range(parts):
            for j in range(slots):
                pair = jnp.stack([own[h][j][0], other[h][j]])
                pair = jnp.where(where[1] == 0, pair, pair[::-1])[:, :, None]
                start = ((where[0] ^ j) * parts + h) * rows
                target = lax.dynamic_update_slice_in_dim(target, pair, start, axis=4)
        return target[0], target[1]
    flat = [piece for pieces in own for piece in pieces]
    vmem = [
        pl.BlockSpec((1, inner, 2, rows, m), lambda i, s: (0, 0, 0, 0, 0)) for _ in flat
    ] + [pl.BlockSpec((slots, inner, 2, rows, m), lambda i, s: (0, 0, 0, 0, 0)) for _ in other]
    shape = (inner, 1, 2, m, m)
    target = pl.BlockSpec(
        (inner, 1, 2, rows, m),
        lambda i, s: (0, 0, 0, (s[0] ^ lax.rem(i, slots)) * parts + lax.div(i, slots), 0),
    )
    return pl.pallas_call(
        functools.partial(collect_kernel, slots, parts),
        out_shape=[out_like(shape)] * 2,
        grid_spec=pltpu.PrefetchScalarGridSpec(
            num_scalar_prefetch=1,
            grid=(parts * slots,),
            in_specs=vmem,
            out_specs=[target] * 2,
        ),
        compiler_params=pltpu.CompilerParams(vmem_limit_bytes=24 * 2**20),
        cost_estimate=pl.CostEstimate(
            flops=0, bytes_accessed=16 * inner * m * m, transcendentals=0
        ),
    )(where, *flat, *other)


def local(lesser_green, greater_green, coulomb_blocks):
    pieces = lax.axis_size("energy")
    slots = pieces // 2
    inner, _, _, m, _ = lesser_green.shape
    group = m // slots
    parts = 2 if group % 32 == 0 else 1
    rows = group // parts
    chunks = 2
    each = 2 * inner // chunks
    index = lax.axis_index("energy")
    where = jnp.stack([index // 2, index % 2]).astype(jnp.int32)
    others = range(1, slots)

    mine, sib = [], []
    for h in range(parts):
        found = cut(where, (lesser_green, greater_green), h, slots, rows)
        mine.append(jnp.stack([found[0]] + [swap(found[j], 2 * j) for j in others]))
        sib.append(swap(mine[h], 1))

    left, right = coupling_matrices(where, coulomb_blocks[0], slots)

    pol = []
    near = [[], [], []]
    for h in range(parts):
        found = correlate(where, mine[h], sib[h])
        near[0].append(shift(found[0], 1))
        near[1].append(found[0])
        near[2].append(shift(found[0], -1))
        pol.append([swap(found[j], 2 * j) for j in others])

    screens = []
    for c in range(chunks):
        far = pack([piece for received in pol for piece in received], c, each)
        sources = [near[0] + [shift(far, 1)], near[1] + [far], near[2] + [shift(far, -1)]]
        found = screen(where, left, right, sources, c, slots)
        screens.append([found[0]] + [swap(found[j], 2 * j) for j in others])

    own, other = [], []
    for h in range(parts):
        found = self_energy(where, mine[h], sib[h], screens, h)
        own.append([found[0]] + [swap(found[j], 2 * j) for j in others])
        other.append(swap(jnp.stack([piece[1] for piece in own[h]]), 1))
    return tuple(collect(where, own, other, inner, m))


def solution(mesh):
    return jax.shard_map(
        local,
        mesh=mesh,
        in_specs=(
            P("energy", "blk", None, None, None),
            P("energy", "blk", None, None, None),
            P("blk", None, None, None, None),
        ),
        out_specs=(P("energy", "blk", None, None, None), P("energy", "blk", None, None, None)),
        check_vma=False,
    )
```

```python
import functools
import math

import jax
import jax.numpy as jnp
from jax import lax
from jax.experimental import pallas as pl
from jax.experimental.pallas import tpu as pltpu
from jax.sharding import PartitionSpec as P

f32 = jnp.float32
bf16 = jnp.bfloat16


def swap(value, distance):
    count = lax.axis_size("energy")
    return lax.ppermute(value, "energy", [(i, i ^ distance) for i in range(count)])


def shift(value, step):
    count = lax.axis_size("blk")
    pairs = [(i, i + step) for i in range(count) if 0 <= i + step < count]
    return lax.ppermute(value, "blk", pairs)


def row_block(rows):
    for size in (16, 8):
        if rows % size == 0:
            return size
    return rows


def out_like(shape):
    return jax.ShapeDtypeStruct(shape, bf16)


def vpu_cost(total, elements, moved):
    return pl.CostEstimate(
        flops=3 * total * (total + 1) * elements, bytes_accessed=2 * moved, transcendentals=0
    )


def tiles(rows, cols, body):
    lanes = 128 if cols % 128 == 0 else cols
    sub = 8 if rows % 8 == 0 else rows
    across = cols // lanes

    def step(t, carry):
        r = pl.multiple_of(lax.div(t, across) * sub, sub)
        c = pl.multiple_of(lax.rem(t, across) * lanes, lanes)
        body((pl.ds(r, sub), pl.ds(c, lanes)))
        return carry

    lax.fori_loop(0, (rows // sub) * across, step, 0)


def correlate_kernel(slots, inner, where, mine, sib, *rest):
    outs, (x_scr, y_scr, o_scr) = rest[:slots], rest[slots:]
    chip, core = where[0], where[1]
    total = 2 * inner * slots
    rows, cols = mine.shape[-2:]
    for j in range(slots):
        for side, source in enumerate((mine, sib)):
            half = core if side == 0 else 1 - core
            for i in range(inner):
                e = (2 * (chip ^ j) + half) * inner + i
                a = source[j, i, core, 0].astype(f32)
                b = source[j, i, core, 1].astype(f32)
                x_scr[0, e], x_scr[1, e], x_scr[2, e] = a, b, a + b
                a = source[j, i, 1 - core, 0].astype(f32)
                b = source[j, i, 1 - core, 1].astype(f32)
                y_scr[0, e], y_scr[1, e], y_scr[2, e] = a, b, a - b
    factor = -1.0 / math.sqrt(total)
    width = 4

    def body(at):
        for base in range(0, total, width):
            lags = range(base, min(base + width, total))
            sums = {}
            window = {}
            for e in range(total - base):
                y = [y_scr[(p, e) + at] for p in range(3)]
                for w in lags:
                    if e + w >= total:
                        continue
                    if e + w not in window:
                        window[e + w] = [x_scr[(p, e + w) + at] for p in range(3)]
                    terms = [window[e + w][p] * y[p] for p in range(3)]
                    sums[w] = [s + t for s, t in zip(sums[w], terms)] if w in sums else terms
                window.pop(e + base, None)
            for w in lags:
                first, second, third = sums[w]
                o_scr[(w, 0) + at] = factor * (first + second)
                o_scr[(w, 1) + at] = factor * (third - first + second)

    tiles(rows, cols, body)
    per = 2 * inner
    for j in range(slots):
        for i in range(per):
            outs[j][i] = o_scr[(chip ^ j) * per + i].astype(bf16)


def correlate(where, mine, sib):
    slots, inner, _, _, rows, cols = mine.shape
    total = 2 * inner * slots
    block = row_block(rows)
    in_spec = pl.BlockSpec((slots, inner, 2, 2, block, cols), lambda r, s: (0, 0, 0, 0, r, 0))
    out_spec = pl.BlockSpec((2 * inner, 2, block, cols), lambda r, s: (0, 0, r, 0))
    return pl.pallas_call(
        functools.partial(correlate_kernel, slots, inner),
        out_shape=[out_like((2 * inner, 2, rows, cols))] * slots,
        grid_spec=pltpu.PrefetchScalarGridSpec(
            num_scalar_prefetch=1,
            grid=(rows // block,),
            in_specs=[in_spec, in_spec],
            out_specs=[out_spec] * slots,
            scratch_shapes=[
                pltpu.VMEM((3, total, block, cols), f32),
                pltpu.VMEM((3, total, block, cols), f32),
                pltpu.VMEM((total, 2, block, cols), f32),
            ],
        ),
        compiler_params=pltpu.CompilerParams(vmem_limit_bytes=32 * 2**20),
        cost_estimate=vpu_cost(total, rows * cols, 2 * 3 * mine.size),
    )(where, mine, sib)


def sigma_kernel(slots, inner, chunks, where, mine, sib, *rest):
    screens = rest[: slots * chunks]
    outs = rest[slots * chunks : slots * chunks + slots]
    x_scr, y_scr, o_scr = rest[slots * chunks + slots :]
    chip, core = where[0], where[1]
    total = 2 * inner * slots
    rows, cols = mine.shape[-2:]
    per = 2 * inner
    each = per // chunks
    for j in range(slots):
        for side, source in enumerate((mine, sib)):
            half = core if side == 0 else 1 - core
            for i in range(inner):
                e = (2 * (chip ^ j) + half) * inner + i
                a = source[j, i, 0, 0].astype(f32)
                b = source[j, i, 0, 1].astype(f32)
                x_scr[0, e], x_scr[1, e], x_scr[2, e] = a, b, a + b
        for m in range(chunks):
            source = screens[m * slots + j]
            for i in range(each):
                w = (chip ^ j) * per + m * each + i
                a = source[i, 0].astype(f32)
                b = source[i, 1].astype(f32)
                y_scr[0, w], y_scr[1, w], y_scr[2, w] = a, b, a + b
    factor = 1.0 / math.sqrt(total)
    width = 4

    def body(at):
        for base in range(0, total, width):
            energies = range(base, min(base + width, total))
            sums = {}
            window = {}
            for w in range(base + width):
                if w >= total:
                    continue
                y = [y_scr[(p, w) + at] for p in range(3)]
                for e in energies:
                    if e < w:
                        continue
                    if e - w not in window:
                        window[e - w] = [x_scr[(p, e - w) + at] for p in range(3)]
                    terms = [window[e - w][p] * y[p] for p in range(3)]
                    sums[e] = [s + t for s, t in zip(sums[e], terms)] if e in sums else terms
                window.pop(base + width - 1 - w, None)
            for e in energies:
                first, second, third = sums[e]
                o_scr[(e, 0) + at] = factor * (first - second)
                o_scr[(e, 1) + at] = factor * (third - first - second)

    tiles(rows, cols, body)
    for j in range(slots):
        for side in range(2):
            half = core if side == 0 else 1 - core
            for i in range(inner):
                e = (2 * (chip ^ j) + half) * inner + i
                outs[j][side, i] = o_scr[e].astype(bf16)


def self_energy(where, mine, sib, screens, part):
    slots, inner, _, _, rows, cols = mine.shape
    chunks = len(screens)
    flat = [piece for chunk in screens for piece in chunk]
    each = flat[0].shape[0]
    total = 2 * inner * slots
    block = row_block(rows)
    steps = rows // block
    green_spec = pl.BlockSpec(
        (slots, inner, 1, 2, block, cols), lambda r, s: (0, 0, s[1], 0, r, 0)
    )
    screen_spec = pl.BlockSpec((each, 2, block, cols), lambda r, s: (0, 0, part * steps + r, 0))
    out_spec = pl.BlockSpec((2, inner, 2, block, cols), lambda r, s: (0, 0, 0, r, 0))
    return pl.pallas_call(
        functools.partial(sigma_kernel, slots, inner, chunks),
        out_shape=[out_like((2, inner, 2, rows, cols))] * slots,
        grid_spec=pltpu.PrefetchScalarGridSpec(
            num_scalar_prefetch=1,
            grid=(steps,),
            in_specs=[green_spec, green_spec] + [screen_spec] * len(flat),
            out_specs=[out_spec] * slots,
            scratch_shapes=[
                pltpu.VMEM((3, total, block, cols), f32),
                pltpu.VMEM((3, total, block, cols), f32),
                pltpu.VMEM((total, 2, block, cols), f32),
            ],
        ),
        compiler_params=pltpu.CompilerParams(vmem_limit_bytes=32 * 2**20),
        cost_estimate=vpu_cost(total, rows * cols, 3 * mine.size),
    )(where, mine, sib, *flat)


def cut_kernel(slots, where, *rest):
    for j in range(slots):
        for kind in range(2):
            rest[2 * slots + j][0, kind] = rest[kind * slots + j][0, 0]


def cut(where, greens, part, slots, rows):
    inner, _, _, m, _ = greens[0].shape
    parts = m // (slots * rows)
    if rows % 16:
        return [
            jnp.stack(
                [
                    lax.dynamic_slice_in_dim(g[:, 0], ((where[0] ^ j) * parts + part) * rows, rows, axis=2)
                    for g in greens
                ],
                axis=1,
            )
            for j in range(slots)
        ]

    def block(j):
        return pl.BlockSpec(
            (1, 1, 2, rows, m), lambda e, s: (e, 0, 0, (s[0] ^ j) * parts + part, 0)
        )

    return pl.pallas_call(
        functools.partial(cut_kernel, slots),
        out_shape=[out_like((inner, 2, 2, rows, m))] * slots,
        grid_spec=pltpu.PrefetchScalarGridSpec(
            num_scalar_prefetch=1,
            grid=(inner,),
            in_specs=[block(j) for j in range(slots)] * 2,
            out_specs=[pl.BlockSpec((1, 2, 2, rows, m), lambda e, s: (e, 0, 0, 0, 0))] * slots,
        ),
        compiler_params=pltpu.CompilerParams(vmem_limit_bytes=16 * 2**20),
        cost_estimate=pl.CostEstimate(
            flops=0, bytes_accessed=16 * inner * slots * rows * m, transcendentals=0
        ),
    )(where, *([greens[0]] * slots), *([greens[1]] * slots))


def matrices_kernel(slots, where, coupling, left, right, *held):
    count, _, m, _ = coupling.shape
    group = m // slots
    chip = where[0]
    for o in range(count):
        real, imag = coupling[o, 0].astype(f32), coupling[o, 1].astype(f32)
        real_t, imag_t = real.T.astype(bf16), imag.T.astype(bf16)
        base = 2 * m * o
        right[base : base + m, :m] = real_t
        right[base : base + m, m:] = -imag_t
        right[base + m : base + 2 * m, :m] = imag_t
        right[base + m : base + 2 * m, m:] = real_t
        if held:
            held[0][0], held[0][1] = real, imag
            source = held[0]
        else:
            source = coupling.at[o]
        for j in range(slots):
            start = pl.multiple_of((chip ^ j) * group, group)
            real = source[0, pl.ds(start, group), :].astype(bf16)
            imag = source[1, pl.ds(start, group), :].astype(bf16)
            low = j * group
            left[o, low : low + group, :m] = real
            left[o, low : low + group, m:] = -imag
            left[o, m + low : m + low + group, :m] = imag
            left[o, m + low : m + low + group, m:] = real


def coupling_matrices(where, coulomb, slots):
    count, _, m, _ = coulomb.shape
    vmem = pl.BlockSpec(memory_space=pltpu.VMEM)
    held = [] if (m // slots) % 16 == 0 else [pltpu.VMEM((2, m, m), f32)]
    return pl.pallas_call(
        functools.partial(matrices_kernel, slots),
        out_shape=[out_like((count, 2 * m, 2 * m)), out_like((count * 2 * m, 2 * m))],
        in_specs=[pl.BlockSpec(memory_space=pltpu.SMEM), vmem],
        out_specs=[vmem, vmem],
        scratch_shapes=held,
        compiler_params=pltpu.CompilerParams(vmem_limit_bytes=24 * 2**20),
        cost_estimate=pl.CostEstimate(flops=0, bytes_accessed=20 * coulomb.size, transcendentals=0),
    )(where, coulomb)


def pack_kernel(pieces, extra, *refs):
    for k in range(pieces):
        refs[pieces + extra][k] = refs[k][...]


def pack(pieces, chunk=0, each=None, after=()):
    count = len(pieces)
    shape = pieces[0].shape
    block = (each or shape[0],) + shape[1:]
    size = math.prod(block)
    rest = (0,) * (len(shape) - 1)
    return pl.pallas_call(
        functools.partial(pack_kernel, count, len(after)),
        out_shape=out_like((count,) + block),
        grid=(1,),
        in_specs=[pl.BlockSpec(block, lambda i: (chunk,) + rest)] * count
        + [pl.BlockSpec(memory_space=pl.ANY)] * len(after),
        out_specs=pl.BlockSpec((count,) + block, lambda i: (0, 0) + rest),
        compiler_params=pltpu.CompilerParams(vmem_limit_bytes=16 * 2**20),
        cost_estimate=pl.CostEstimate(flops=0, bytes_accessed=4 * count * size, transcendentals=0),
    )(*pieces, *after)


def screen_kernel(slots, parts, chunk, where, left_ref, right_ref, *rest):
    per_source = parts + 1
    sources = [rest[o * per_source : (o + 1) * per_source] for o in range(3)]
    outs = rest[3 * per_source : 3 * per_source + slots]
    pol, left = rest[3 * per_source + slots :]
    each, _, rows, m = sources[0][parts].shape[1:]
    group = m // slots
    chip = where[0]
    for o, source in enumerate(sources):
        for h in range(parts):
            for j in range(slots):
                for part in range(2):
                    start = part * m + (chip ^ j) * group + h * rows
                    start = pl.multiple_of(start, rows)
                    for i in range(each):
                        if j == 0:
                            piece = source[h][chunk * each + i, part]
                        else:
                            piece = source[parts][h * (slots - 1) + j - 1, i, part]
                        pol[o, i, pl.ds(start, rows), :] = piece.astype(pol.dtype)
    for o in range(3):
        both = jnp.concatenate([pol[o, i].astype(bf16) for i in range(each)], axis=1)
        product = jnp.dot(left_ref[o], both, preferred_element_type=f32).astype(bf16)
        for i in range(each):
            for part in range(2):
                left[i, :, (2 * o + part) * m : (2 * o + part + 1) * m] = product[
                    part * m : (part + 1) * m, i * m : (i + 1) * m
                ]
    for i in range(each):
        result = jnp.dot(left[i], right_ref[...], preferred_element_type=f32).astype(bf16)
        for j in range(slots):
            for part in range(2):
                outs[j][i, part] = result[
                    j * group : (j + 1) * group, part * m : (part + 1) * m
                ]


def screen(where, left_matrix, right_matrix, sources, chunk, slots):
    parts = len(sources[0]) - 1
    _, each, _, rows, m = sources[0][parts].shape
    group = m // slots
    vmem = pl.BlockSpec(memory_space=pltpu.VMEM)
    flops = 2 * each * (6 * 2 * m * 2 * m * m)
    moved = 2 * (3 * each * 2 * m * m + left_matrix.size + right_matrix.size + 2 * each * m * m)
    hold = bf16 if rows % 16 == 0 else f32
    flat = [piece for source in sources for piece in source]
    return pl.pallas_call(
        functools.partial(screen_kernel, slots, parts, chunk),
        out_shape=[out_like((each, 2, group, m))] * slots,
        in_specs=[pl.BlockSpec(memory_space=pltpu.SMEM)] + [vmem] * (2 + len(flat)),
        out_specs=[vmem] * slots,
        scratch_shapes=[
            pltpu.VMEM((3, each, 2 * m, m), hold),
            pltpu.VMEM((each, m, 6 * m), bf16),
        ],
        compiler_params=pltpu.CompilerParams(vmem_limit_bytes=44 * 2**20),
        cost_estimate=pl.CostEstimate(flops=flops, bytes_accessed=moved, transcendentals=0),
    )(where, left_matrix, right_matrix, *flat)


def collect_kernel(slots, parts, where, *rest):
    count = slots * parts
    own, other = rest[:count], rest[count : count + parts]
    less, great = rest[count + parts :]
    core = where[1]
    for k in range(count):

        @pl.when(pl.program_id(0) == k)
        def _(k=k):
            h, j = divmod(k, slots)
            mine, theirs = own[k][0], other[h][j]
            less[:, 0] = jnp.where(core == 0, mine, theirs)
            great[:, 0] = jnp.where(core == 0, theirs, mine)


def collect(where, own, other, inner, m):
    parts, slots = len(own), len(own[0])
    rows = m // (slots * parts)
    if rows % 16:
        target = jnp.zeros((2, inner, 1, 2, m, m), bf16)
        for h in range(parts):
            for j in range(slots):
                pair = jnp.stack([own[h][j][0], other[h][j]])
                pair = jnp.where(where[1] == 0, pair, pair[::-1])[:, :, None]
                start = ((where[0] ^ j) * parts + h) * rows
                target = lax.dynamic_update_slice_in_dim(target, pair, start, axis=4)
        return target[0], target[1]
    flat = [piece for pieces in own for piece in pieces]
    vmem = [
        pl.BlockSpec((1, inner, 2, rows, m), lambda i, s: (0, 0, 0, 0, 0)) for _ in flat
    ] + [pl.BlockSpec((slots, inner, 2, rows, m), lambda i, s: (0, 0, 0, 0, 0)) for _ in other]
    shape = (inner, 1, 2, m, m)
    target = pl.BlockSpec(
        (inner, 1, 2, rows, m),
        lambda i, s: (0, 0, 0, (s[0] ^ lax.rem(i, slots)) * parts + lax.div(i, slots), 0),
    )
    return pl.pallas_call(
        functools.partial(collect_kernel, slots, parts),
        out_shape=[out_like(shape)] * 2,
        grid_spec=pltpu.PrefetchScalarGridSpec(
            num_scalar_prefetch=1,
            grid=(parts * slots,),
            in_specs=vmem,
            out_specs=[target] * 2,
        ),
        compiler_params=pltpu.CompilerParams(vmem_limit_bytes=24 * 2**20),
        cost_estimate=pl.CostEstimate(
            flops=0, bytes_accessed=16 * inner * m * m, transcendentals=0
        ),
    )(where, *flat, *other)


def local(lesser_green, greater_green, coulomb_blocks):
    pieces = lax.axis_size("energy")
    slots = pieces // 2
    inner, _, _, m, _ = lesser_green.shape
    group = m // slots
    parts = 2 if group % 32 == 0 else 1
    rows = group // parts
    chunks = 2
    each = 2 * inner // chunks
    index = lax.axis_index("energy")
    where = jnp.stack([index // 2, index % 2]).astype(jnp.int32)
    others = range(1, slots)

    cuts = [cut(where, (lesser_green, greater_green), h, slots, rows) for h in range(parts)]
    greens = [[found[0]] + [swap(found[j], 2 * j) for j in others] for found in cuts]
    left, right = coupling_matrices(where, coulomb_blocks[0], slots)

    mine, sib, pol, after = [], [], [], []
    near = [[], [], []]
    for h in range(parts):
        mine.append(pack(greens[h], after=after))
        sib.append(swap(mine[h], 1))
        found = correlate(where, mine[h], sib[h])
        after = [found[0]]
        near[0].append(shift(found[0], 1))
        near[1].append(found[0])
        near[2].append(shift(found[0], -1))
        pol.append([swap(found[j], 2 * j) for j in others])

    screens = []
    after = near[0] + near[2]
    for c in range(chunks):
        far = pack([piece for received in pol for piece in received], c, each, after)
        after = [shift(far, 1), shift(far, -1)]
        sources = [near[0] + [after[0]], near[1] + [far], near[2] + [after[1]]]
        found = screen(where, left, right, sources, c, slots)
        screens.append([found[0]] + [swap(found[j], 2 * j) for j in others])

    own, other = [], []
    for h in range(parts):
        found = self_energy(where, mine[h], sib[h], screens, h)
        own.append([found[0]] + [swap(found[j], 2 * j) for j in others])
        other.append(swap(jnp.stack([piece[1] for piece in own[h]]), 1))
    return tuple(collect(where, own, other, inner, m))


def solution(mesh):
    return jax.shard_map(
        local,
        mesh=mesh,
        in_specs=(
            P("energy", "blk", None, None, None),
            P("energy", "blk", None, None, None),
            P("blk", None, None, None, None),
        ),
        out_specs=(P("energy", "blk", None, None, None), P("energy", "blk", None, None, None)),
        check_vma=False,
    )
```

```python
import functools
import math

import jax
import jax.numpy as jnp
from jax import lax
from jax.experimental import pallas as pl
from jax.experimental.pallas import tpu as pltpu
from jax.sharding import PartitionSpec as P

f32 = jnp.float32
bf16 = jnp.bfloat16


def swap(value, distance):
    count = lax.axis_size("energy")
    return lax.ppermute(value, "energy", [(i, i ^ distance) for i in range(count)])


def shift(value, step):
    count = lax.axis_size("blk")
    pairs = [(i, i + step) for i in range(count) if 0 <= i + step < count]
    return lax.ppermute(value, "blk", pairs)


def row_block(rows):
    for size in (16, 8):
        if rows % size == 0:
            return size
    return rows


def out_like(shape):
    return jax.ShapeDtypeStruct(shape, bf16)


def vpu_cost(total, elements, moved):
    return pl.CostEstimate(
        flops=3 * total * (total + 1) * elements, bytes_accessed=2 * moved, transcendentals=0
    )


def tiles(rows, cols, body):
    lanes = 128 if cols % 128 == 0 else cols
    sub = 8 if rows % 8 == 0 else rows
    across = cols // lanes

    def step(t, carry):
        r = pl.multiple_of(lax.div(t, across) * sub, sub)
        c = pl.multiple_of(lax.rem(t, across) * lanes, lanes)
        body((pl.ds(r, sub), pl.ds(c, lanes)))
        return carry

    lax.fori_loop(0, (rows // sub) * across, step, 0)


def correlate_kernel(slots, inner, where, mine, sib, *rest):
    outs, (x_scr, y_scr, o_scr) = rest[:slots], rest[slots:]
    chip, core = where[0], where[1]
    total = 2 * inner * slots
    rows, cols = mine.shape[-2:]
    for j in range(slots):
        for side, source in enumerate((mine, sib)):
            half = core if side == 0 else 1 - core
            for i in range(inner):
                e = (2 * (chip ^ j) + half) * inner + i
                a = source[j, i, core, 0].astype(f32)
                b = source[j, i, core, 1].astype(f32)
                x_scr[0, e], x_scr[1, e], x_scr[2, e] = a, b, a + b
                a = source[j, i, 1 - core, 0].astype(f32)
                b = source[j, i, 1 - core, 1].astype(f32)
                y_scr[0, e], y_scr[1, e], y_scr[2, e] = a, b, a - b
    factor = -1.0 / math.sqrt(total)
    width = 4

    def body(at):
        for base in range(0, total, width):
            lags = range(base, min(base + width, total))
            sums = {}
            window = {}
            for e in range(total - base):
                y = [y_scr[(p, e) + at] for p in range(3)]
                for w in lags:
                    if e + w >= total:
                        continue
                    if e + w not in window:
                        window[e + w] = [x_scr[(p, e + w) + at] for p in range(3)]
                    terms = [window[e + w][p] * y[p] for p in range(3)]
                    sums[w] = [s + t for s, t in zip(sums[w], terms)] if w in sums else terms
                window.pop(e + base, None)
            for w in lags:
                first, second, third = sums[w]
                o_scr[(w, 0) + at] = factor * (first + second)
                o_scr[(w, 1) + at] = factor * (third - first + second)

    tiles(rows, cols, body)
    per = 2 * inner
    for j in range(slots):
        for i in range(per):
            outs[j][i] = o_scr[(chip ^ j) * per + i].astype(bf16)


def correlate(where, mine, sib):
    slots, inner, _, _, rows, cols = mine.shape
    total = 2 * inner * slots
    block = row_block(rows)
    in_spec = pl.BlockSpec((slots, inner, 2, 2, block, cols), lambda r, s: (0, 0, 0, 0, r, 0))
    out_spec = pl.BlockSpec((2 * inner, 2, block, cols), lambda r, s: (0, 0, r, 0))
    return pl.pallas_call(
        functools.partial(correlate_kernel, slots, inner),
        name="correlate",
        out_shape=[out_like((2 * inner, 2, rows, cols))] * slots,
        grid_spec=pltpu.PrefetchScalarGridSpec(
            num_scalar_prefetch=1,
            grid=(rows // block,),
            in_specs=[in_spec, in_spec],
            out_specs=[out_spec] * slots,
            scratch_shapes=[
                pltpu.VMEM((3, total, block, cols), f32),
                pltpu.VMEM((3, total, block, cols), f32),
                pltpu.VMEM((total, 2, block, cols), f32),
            ],
        ),
        compiler_params=pltpu.CompilerParams(vmem_limit_bytes=32 * 2**20),
        cost_estimate=vpu_cost(total, rows * cols, 2 * 3 * mine.size),
    )(where, mine, sib)


def sigma_kernel(slots, inner, chunks, where, mine, sib, *rest):
    screens = rest[: slots * chunks]
    outs = rest[slots * chunks : slots * chunks + slots]
    x_scr, y_scr, o_scr = rest[slots * chunks + slots :]
    chip, core = where[0], where[1]
    total = 2 * inner * slots
    rows, cols = mine.shape[-2:]
    per = 2 * inner
    each = per // chunks
    for j in range(slots):
        for side, source in enumerate((mine, sib)):
            half = core if side == 0 else 1 - core
            for i in range(inner):
                e = (2 * (chip ^ j) + half) * inner + i
                a = source[j, i, 0, 0].astype(f32)
                b = source[j, i, 0, 1].astype(f32)
                x_scr[0, e], x_scr[1, e], x_scr[2, e] = a, b, a + b
        for m in range(chunks):
            source = screens[m * slots + j]
            for i in range(each):
                w = (chip ^ j) * per + m * each + i
                a = source[i, 0].astype(f32)
                b = source[i, 1].astype(f32)
                y_scr[0, w], y_scr[1, w], y_scr[2, w] = a, b, a + b
    factor = 1.0 / math.sqrt(total)
    width = 4

    def body(at):
        for base in range(0, total, width):
            energies = range(base, min(base + width, total))
            sums = {}
            window = {}
            for w in range(base + width):
                if w >= total:
                    continue
                y = [y_scr[(p, w) + at] for p in range(3)]
                for e in energies:
                    if e < w:
                        continue
                    if e - w not in window:
                        window[e - w] = [x_scr[(p, e - w) + at] for p in range(3)]
                    terms = [window[e - w][p] * y[p] for p in range(3)]
                    sums[e] = [s + t for s, t in zip(sums[e], terms)] if e in sums else terms
                window.pop(base + width - 1 - w, None)
            for e in energies:
                first, second, third = sums[e]
                o_scr[(e, 0) + at] = factor * (first - second)
                o_scr[(e, 1) + at] = factor * (third - first - second)

    tiles(rows, cols, body)
    for j in range(slots):
        for side in range(2):
            half = core if side == 0 else 1 - core
            for i in range(inner):
                e = (2 * (chip ^ j) + half) * inner + i
                outs[j][side, i] = o_scr[e].astype(bf16)


def self_energy(where, mine, sib, screens, part):
    slots, inner, _, _, rows, cols = mine.shape
    chunks = len(screens)
    flat = [piece for chunk in screens for piece in chunk]
    each = flat[0].shape[0]
    total = 2 * inner * slots
    block = row_block(rows)
    steps = rows // block
    green_spec = pl.BlockSpec(
        (slots, inner, 1, 2, block, cols), lambda r, s: (0, 0, s[1], 0, r, 0)
    )
    screen_spec = pl.BlockSpec((each, 2, block, cols), lambda r, s: (0, 0, part * steps + r, 0))
    out_spec = pl.BlockSpec((2, inner, 2, block, cols), lambda r, s: (0, 0, 0, r, 0))
    return pl.pallas_call(
        functools.partial(sigma_kernel, slots, inner, chunks),
        name="sigma",
        out_shape=[out_like((2, inner, 2, rows, cols))] * slots,
        grid_spec=pltpu.PrefetchScalarGridSpec(
            num_scalar_prefetch=1,
            grid=(steps,),
            in_specs=[green_spec, green_spec] + [screen_spec] * len(flat),
            out_specs=[out_spec] * slots,
            scratch_shapes=[
                pltpu.VMEM((3, total, block, cols), f32),
                pltpu.VMEM((3, total, block, cols), f32),
                pltpu.VMEM((total, 2, block, cols), f32),
            ],
        ),
        compiler_params=pltpu.CompilerParams(vmem_limit_bytes=32 * 2**20),
        cost_estimate=vpu_cost(total, rows * cols, 3 * mine.size),
    )(where, mine, sib, *flat)


def cut_kernel(slots, where, *rest):
    for j in range(slots):
        for kind in range(2):
            rest[2 * slots + j][0, kind] = rest[kind * slots + j][0, 0]


def cut(where, greens, slots):
    inner, _, _, m, _ = greens[0].shape
    group = m // slots
    if group % 16:
        return [
            jnp.stack(
                [
                    lax.dynamic_slice_in_dim(g[:, 0], (where[0] ^ j) * group, group, axis=2)
                    for g in greens
                ],
                axis=1,
            )
            for j in range(slots)
        ]

    def block(j):
        return pl.BlockSpec((1, 1, 2, group, m), lambda e, s: (e, 0, 0, s[0] ^ j, 0))

    return pl.pallas_call(
        functools.partial(cut_kernel, slots),
        name="cut_rows",
        out_shape=[out_like((inner, 2, 2, group, m))] * slots,
        grid_spec=pltpu.PrefetchScalarGridSpec(
            num_scalar_prefetch=1,
            grid=(inner,),
            in_specs=[block(j) for j in range(slots)] * 2,
            out_specs=[pl.BlockSpec((1, 2, 2, group, m), lambda e, s: (e, 0, 0, 0, 0))] * slots,
        ),
        compiler_params=pltpu.CompilerParams(vmem_limit_bytes=56 * 2**20),
        cost_estimate=pl.CostEstimate(flops=0, bytes_accessed=16 * inner * m * m, transcendentals=0),
    )(where, *([greens[0]] * slots), *([greens[1]] * slots))


def matrices_kernel(slots, where, coupling, left, right, *held):
    count, _, m, _ = coupling.shape
    group = m // slots
    chip = where[0]
    for o in range(count):
        real, imag = coupling[o, 0].astype(f32), coupling[o, 1].astype(f32)
        real_t, imag_t = real.T.astype(bf16), imag.T.astype(bf16)
        base = 2 * m * o
        right[base : base + m, :m] = real_t
        right[base : base + m, m:] = -imag_t
        right[base + m : base + 2 * m, :m] = imag_t
        right[base + m : base + 2 * m, m:] = real_t
        if held:
            held[0][0], held[0][1] = real, imag
            source = held[0]
        else:
            source = coupling.at[o]
        for j in range(slots):
            start = pl.multiple_of((chip ^ j) * group, group)
            real = source[0, pl.ds(start, group), :].astype(bf16)
            imag = source[1, pl.ds(start, group), :].astype(bf16)
            low = j * group
            left[o, low : low + group, :m] = real
            left[o, low : low + group, m:] = -imag
            left[o, m + low : m + low + group, :m] = imag
            left[o, m + low : m + low + group, m:] = real


def coupling_matrices(where, coulomb, slots):
    count, _, m, _ = coulomb.shape
    vmem = pl.BlockSpec(memory_space=pltpu.VMEM)
    held = [] if (m // slots) % 16 == 0 else [pltpu.VMEM((2, m, m), f32)]
    return pl.pallas_call(
        functools.partial(matrices_kernel, slots),
        name="coupling",
        out_shape=[out_like((count, 2 * m, 2 * m)), out_like((count * 2 * m, 2 * m))],
        in_specs=[pl.BlockSpec(memory_space=pltpu.SMEM), vmem],
        out_specs=[vmem, vmem],
        scratch_shapes=held,
        compiler_params=pltpu.CompilerParams(vmem_limit_bytes=24 * 2**20),
        cost_estimate=pl.CostEstimate(flops=0, bytes_accessed=20 * coulomb.size, transcendentals=0),
    )(where, coulomb)


def pack_kernel(pieces, extra, *refs):
    for k in range(pieces):
        refs[pieces + extra][k] = refs[k][...]


def pack(pieces, block=None, index=None, after=()):
    count = len(pieces)
    block = block or pieces[0].shape
    index = index or (0,) * len(block)
    size = math.prod(block)
    return pl.pallas_call(
        functools.partial(pack_kernel, count, len(after)),
        name="pack",
        out_shape=out_like((count,) + block),
        grid=(1,),
        in_specs=[pl.BlockSpec(block, lambda i: index)] * count
        + [pl.BlockSpec(memory_space=pl.ANY)] * len(after),
        out_specs=pl.BlockSpec((count,) + block, lambda i: (0,) * (1 + len(block))),
        compiler_params=pltpu.CompilerParams(vmem_limit_bytes=16 * 2**20),
        cost_estimate=pl.CostEstimate(flops=0, bytes_accessed=4 * count * size, transcendentals=0),
    )(*pieces, *after)


def screen_kernel(slots, parts, chunk, each, where, left_ref, right_ref, *rest):
    per_source = 2 * parts
    sources = [rest[o * per_source : (o + 1) * per_source] for o in range(3)]
    outs = rest[3 * per_source : 3 * per_source + slots]
    pol, left = rest[3 * per_source + slots :]
    rows, m = sources[0][0].shape[2:]
    group = m // slots
    chip = where[0]
    for o, source in enumerate(sources):
        for h in range(parts):
            for j in range(slots):
                for part in range(2):
                    start = part * m + (chip ^ j) * group + h * rows
                    start = pl.multiple_of(start, rows)
                    for i in range(each):
                        if j == 0:
                            piece = source[h][chunk * each + i, part]
                        else:
                            far = source[parts + h]
                            lag = i if far.shape[1] == each else chunk * each + i
                            piece = far[j - 1, lag, part]
                        pol[o, i, pl.ds(start, rows), :] = piece.astype(pol.dtype)
    for o in range(3):
        both = jnp.concatenate([pol[o, i].astype(bf16) for i in range(each)], axis=1)
        product = jnp.dot(left_ref[o], both, preferred_element_type=f32).astype(bf16)
        for i in range(each):
            for part in range(2):
                left[i, :, (2 * o + part) * m : (2 * o + part + 1) * m] = product[
                    part * m : (part + 1) * m, i * m : (i + 1) * m
                ]
    for i in range(each):
        result = jnp.dot(left[i], right_ref[...], preferred_element_type=f32).astype(bf16)
        for j in range(slots):
            for part in range(2):
                outs[j][i, part] = result[
                    j * group : (j + 1) * group, part * m : (part + 1) * m
                ]


def screen(where, left_matrix, right_matrix, sources, chunk, each, slots):
    parts = len(sources[0]) // 2
    _, _, rows, m = sources[0][0].shape
    group = m // slots
    vmem = pl.BlockSpec(memory_space=pltpu.VMEM)
    flops = 2 * each * (6 * 2 * m * 2 * m * m)
    moved = 2 * (3 * each * 2 * m * m + left_matrix.size + right_matrix.size + 2 * each * m * m)
    hold = bf16 if rows % 16 == 0 else f32
    flat = [piece for source in sources for piece in source]
    return pl.pallas_call(
        functools.partial(screen_kernel, slots, parts, chunk, each),
        name="screen",
        out_shape=[out_like((each, 2, group, m))] * slots,
        in_specs=[pl.BlockSpec(memory_space=pltpu.SMEM)] + [vmem] * (2 + len(flat)),
        out_specs=[vmem] * slots,
        scratch_shapes=[
            pltpu.VMEM((3, each, 2 * m, m), hold),
            pltpu.VMEM((each, m, 6 * m), bf16),
        ],
        compiler_params=pltpu.CompilerParams(vmem_limit_bytes=44 * 2**20),
        cost_estimate=pl.CostEstimate(flops=flops, bytes_accessed=moved, transcendentals=0),
    )(where, left_matrix, right_matrix, *flat)


def collect_kernel(slots, parts, where, *rest):
    count = slots * parts
    own, other = rest[:count], rest[count : count + parts]
    less, great = rest[count + parts :]
    core = where[1]
    for k in range(count):

        @pl.when(pl.program_id(0) == k)
        def _(k=k):
            h, j = divmod(k, slots)
            mine, theirs = own[k][0], other[h][j]
            less[:, 0] = jnp.where(core == 0, mine, theirs)
            great[:, 0] = jnp.where(core == 0, theirs, mine)


def collect(where, own, other, inner, m):
    parts, slots = len(own), len(own[0])
    rows = m // (slots * parts)
    if rows % 16:
        target = jnp.zeros((2, inner, 1, 2, m, m), bf16)
        for h in range(parts):
            for j in range(slots):
                pair = jnp.stack([own[h][j][0], other[h][j]])
                pair = jnp.where(where[1] == 0, pair, pair[::-1])[:, :, None]
                start = ((where[0] ^ j) * parts + h) * rows
                target = lax.dynamic_update_slice_in_dim(target, pair, start, axis=4)
        return target[0], target[1]
    flat = [piece for pieces in own for piece in pieces]
    vmem = [
        pl.BlockSpec((1, inner, 2, rows, m), lambda i, s: (0, 0, 0, 0, 0)) for _ in flat
    ] + [pl.BlockSpec((slots, inner, 2, rows, m), lambda i, s: (0, 0, 0, 0, 0)) for _ in other]
    shape = (inner, 1, 2, m, m)
    target = pl.BlockSpec(
        (inner, 1, 2, rows, m),
        lambda i, s: (0, 0, 0, (s[0] ^ lax.rem(i, slots)) * parts + lax.div(i, slots), 0),
    )
    return pl.pallas_call(
        functools.partial(collect_kernel, slots, parts),
        name="collect",
        out_shape=[out_like(shape)] * 2,
        grid_spec=pltpu.PrefetchScalarGridSpec(
            num_scalar_prefetch=1,
            grid=(parts * slots,),
            in_specs=vmem,
            out_specs=[target] * 2,
        ),
        compiler_params=pltpu.CompilerParams(vmem_limit_bytes=24 * 2**20),
        cost_estimate=pl.CostEstimate(
            flops=0, bytes_accessed=16 * inner * m * m, transcendentals=0
        ),
    )(where, *flat, *other)


def local(lesser_green, greater_green, coulomb_blocks):
    pieces = lax.axis_size("energy")
    slots = pieces // 2
    inner, _, _, m, _ = lesser_green.shape
    group = m // slots
    parts = 2 if group % 32 == 0 else 1
    rows = group // parts
    chunks = 2
    each = 2 * inner // chunks
    index = lax.axis_index("energy")
    where = jnp.stack([index // 2, index % 2]).astype(jnp.int32)
    others = range(1, slots)

    found = cut(where, (lesser_green, greater_green), slots)
    greens = [found[0]] + [swap(found[j], 2 * j) for j in others]
    left, right = coupling_matrices(where, coulomb_blocks[0], slots)

    mine, sib, pol, after = [], [], [], []
    shape = (inner, 2, 2, rows, m)
    near = [[], [], []]
    for h in range(parts):
        mine.append(pack(greens, shape, (0, 0, 0, h, 0), after))
        sib.append(swap(mine[h], 1))
        after = mine[:]
    for h in range(parts):
        found = correlate(where, mine[h], sib[h])
        near[0].append(shift(found[0], 1))
        near[1].append(found[0])
        near[2].append(shift(found[0], -1))
        pol.append([swap(found[j], 2 * j) for j in others])

    early = [[], [], []]
    for h in range(parts - 1):
        far = pack(pol[h], after=near[0][: h + 1] + near[2][: h + 1] + near[1][h + 1 :])
        early[0].append(shift(far, 1))
        early[1].append(far)
        early[2].append(shift(far, -1))
    screens = []
    after = near[0] + near[2]
    for c in range(chunks):
        far = pack(pol[-1], (each, 2, rows, m), (c, 0, 0, 0), after)
        late = [shift(far, 1), far, shift(far, -1)]
        after = early[0] + early[2] + [far] if c == 0 and parts > 1 else [late[0], late[2]]
        sources = [near[o] + early[o] + [late[o]] for o in range(3)]
        found = screen(where, left, right, sources, c, each, slots)
        screens.append([found[0]] + [swap(found[j], 2 * j) for j in others])

    own, other = [], []
    for h in range(parts):
        found = self_energy(where, mine[h], sib[h], screens, h)
        own.append([found[0]] + [swap(found[j], 2 * j) for j in others])
        other.append(swap(jnp.stack([piece[1] for piece in own[h]]), 1))
    return tuple(collect(where, own, other, inner, m))


def solution(mesh):
    return jax.shard_map(
        local,
        mesh=mesh,
        in_specs=(
            P("energy", "blk", None, None, None),
            P("energy", "blk", None, None, None),
            P("blk", None, None, None, None),
        ),
        out_specs=(P("energy", "blk", None, None, None), P("energy", "blk", None, None, None)),
        check_vma=False,
    )
```

```python
import functools
import math

import jax
import jax.numpy as jnp
from jax import lax
from jax.experimental import pallas as pl
from jax.experimental.pallas import tpu as pltpu
from jax.sharding import PartitionSpec as P

f32 = jnp.float32
bf16 = jnp.bfloat16


def swap(value, distance):
    count = lax.axis_size("energy")
    return lax.ppermute(value, "energy", [(i, i ^ distance) for i in range(count)])


def shift(value, step):
    count = lax.axis_size("blk")
    pairs = [(i, i + step) for i in range(count) if 0 <= i + step < count]
    return lax.ppermute(value, "blk", pairs)


def row_block(rows):
    for size in (16, 8):
        if rows % size == 0:
            return size
    return rows


def out_like(shape):
    return jax.ShapeDtypeStruct(shape, bf16)


def vpu_cost(total, elements, moved):
    return pl.CostEstimate(
        flops=3 * total * (total + 1) * elements, bytes_accessed=2 * moved, transcendentals=0
    )


def tiles(rows, cols, body):
    lanes = 128 if cols % 128 == 0 else cols
    sub = 8 if rows % 8 == 0 else rows
    across = cols // lanes

    def step(t, carry):
        r = pl.multiple_of(lax.div(t, across) * sub, sub)
        c = pl.multiple_of(lax.rem(t, across) * lanes, lanes)
        body((pl.ds(r, sub), pl.ds(c, lanes)))
        return carry

    lax.fori_loop(0, (rows // sub) * across, step, 0)


def lag_of(total, slots, chunks, chunk, slot, i):
    return (chunks - 1 - chunk) * (total // chunks) + slot * (total // (chunks * slots)) + i


def load_greens(slots, inner, where, mine, sib, put):
    chip, core = where[0], where[1]
    for half, sources in ((core, mine), (1 - core, sib)):
        j = 0
        for source in sources:
            for k in range(source.shape[0]):
                for i in range(inner):
                    put((2 * (chip ^ j) + half) * inner + i, source, k, i)
                j += 1


def correlate_kernel(slots, inner, chunks, chunk, halves, extra, where, *rest):
    mine, sib = rest[:halves], rest[halves : 2 * halves]
    rest = rest[2 * halves + extra :]
    outs, (x_scr, y_scr, o_scr) = rest[:slots], rest[slots:]
    chip, core = where[0], where[1]
    total = 2 * inner * slots
    rows, cols = mine[0].shape[-2:]

    def put(e, source, k, i):
        a = source[k, i, core, 0].astype(f32)
        b = source[k, i, core, 1].astype(f32)
        x_scr[0, e], x_scr[1, e], x_scr[2, e] = a, b, a + b
        a = source[k, i, 1 - core, 0].astype(f32)
        b = source[k, i, 1 - core, 1].astype(f32)
        y_scr[0, e], y_scr[1, e], y_scr[2, e] = a, b, a - b

    load_greens(slots, inner, where, mine, sib, put)
    factor = -1.0 / math.sqrt(total)
    width = 4
    first_lag = lag_of(total, slots, chunks, chunk, 0, 0)
    last_lag = first_lag + total // chunks

    def body(at):
        for base in range(first_lag, last_lag, width):
            lags = range(base, min(base + width, last_lag))
            sums = {}
            window = {}
            for e in range(total - base):
                y = [y_scr[(p, e) + at] for p in range(3)]
                for w in lags:
                    if e + w >= total:
                        continue
                    if e + w not in window:
                        window[e + w] = [x_scr[(p, e + w) + at] for p in range(3)]
                    terms = [window[e + w][p] * y[p] for p in range(3)]
                    sums[w] = [s + t for s, t in zip(sums[w], terms)] if w in sums else terms
                window.pop(e + base, None)
            for w in lags:
                first, second, third = sums[w]
                o_scr[(w - first_lag, 0) + at] = factor * (first + second)
                o_scr[(w - first_lag, 1) + at] = factor * (third - first + second)

    tiles(rows, cols, body)
    each = 2 * inner // chunks
    for j in range(slots):
        for i in range(each):
            outs[j][i] = o_scr[(chip ^ j) * each + i].astype(bf16)


def correlate(where, mine, sib, chunks, chunk, after):
    _, inner, _, _, rows, cols = mine[0].shape
    slots = sum(piece.shape[0] for piece in mine)
    total = 2 * inner * slots
    each = 2 * inner // chunks
    block = row_block(rows)
    in_specs = [
        pl.BlockSpec((piece.shape[0], inner, 2, 2, block, cols), lambda r, s: (0, 0, 0, 0, r, 0))
        for piece in (*mine, *sib)
    ]
    out_spec = pl.BlockSpec((each, 2, block, cols), lambda r, s: (0, 0, r, 0))
    return pl.pallas_call(
        functools.partial(correlate_kernel, slots, inner, chunks, chunk, len(mine), len(after)),
        name="correlate",
        out_shape=[out_like((each, 2, rows, cols))] * slots,
        grid_spec=pltpu.PrefetchScalarGridSpec(
            num_scalar_prefetch=1,
            grid=(rows // block,),
            in_specs=in_specs + [pl.BlockSpec(memory_space=pl.ANY)] * len(after),
            out_specs=[out_spec] * slots,
            scratch_shapes=[
                pltpu.VMEM((3, total, block, cols), f32),
                pltpu.VMEM((3, total, block, cols), f32),
                pltpu.VMEM((total // chunks, 2, block, cols), f32),
            ],
        ),
        compiler_params=pltpu.CompilerParams(vmem_limit_bytes=32 * 2**20),
        cost_estimate=vpu_cost(total, rows * cols // chunks, 4 * total * rows * cols),
    )(where, *mine, *sib, *after)


def sigma_kernel(slots, inner, chunks, halves, where, *rest):
    mine, sib = rest[:halves], rest[halves : 2 * halves]
    rest = rest[2 * halves :]
    screens = rest[: slots * chunks]
    outs = rest[slots * chunks : slots * chunks + slots]
    x_scr, y_scr, o_scr = rest[slots * chunks + slots :]
    chip, core = where[0], where[1]
    total = 2 * inner * slots
    rows, cols = mine[0].shape[-2:]
    each = 2 * inner // chunks

    def put(e, source, k, i):
        a = source[k, i, 0, 0].astype(f32)
        b = source[k, i, 0, 1].astype(f32)
        x_scr[0, e], x_scr[1, e], x_scr[2, e] = a, b, a + b

    load_greens(slots, inner, where, mine, sib, put)
    for j in range(slots):
        for chunk in range(chunks):
            source = screens[chunk * slots + j]
            for i in range(each):
                w = lag_of(total, slots, chunks, chunk, chip ^ j, i)
                a = source[i, 0].astype(f32)
                b = source[i, 1].astype(f32)
                y_scr[0, w], y_scr[1, w], y_scr[2, w] = a, b, a + b
    factor = 1.0 / math.sqrt(total)
    width = 4

    def body(at):
        for base in range(0, total, width):
            energies = range(base, min(base + width, total))
            sums = {}
            window = {}
            for w in range(min(base + width, total)):
                y = [y_scr[(p, w) + at] for p in range(3)]
                for e in energies:
                    if e < w:
                        continue
                    if e - w not in window:
                        window[e - w] = [x_scr[(p, e - w) + at] for p in range(3)]
                    terms = [window[e - w][p] * y[p] for p in range(3)]
                    sums[e] = [s + t for s, t in zip(sums[e], terms)] if e in sums else terms
                window.pop(base + width - 1 - w, None)
            for e in energies:
                first, second, third = sums[e]
                o_scr[(e, 0) + at] = factor * (first - second)
                o_scr[(e, 1) + at] = factor * (third - first - second)

    tiles(rows, cols, body)
    for j in range(slots):
        for side in range(2):
            half = core if side == 0 else 1 - core
            for i in range(inner):
                e = (2 * (chip ^ j) + half) * inner + i
                outs[j][side, i] = o_scr[e].astype(bf16)


def self_energy(where, mine, sib, screens, part, rows):
    _, inner, _, _, _, cols = mine[0].shape
    slots = sum(piece.shape[0] for piece in mine)
    chunks = len(screens)
    flat = [piece for chunk in screens for piece in chunk]
    each = flat[0].shape[0]
    total = 2 * inner * slots
    block = row_block(rows)
    steps = rows // block
    green_specs = [
        pl.BlockSpec(
            (piece.shape[0], inner, 1, 2, block, cols),
            lambda r, s: (0, 0, s[1], 0, part * steps + r, 0),
        )
        for piece in (*mine, *sib)
    ]
    screen_spec = pl.BlockSpec((each, 2, block, cols), lambda r, s: (0, 0, part * steps + r, 0))
    out_spec = pl.BlockSpec((2, inner, 2, block, cols), lambda r, s: (0, 0, 0, r, 0))
    return pl.pallas_call(
        functools.partial(sigma_kernel, slots, inner, chunks, len(mine)),
        name="sigma",
        out_shape=[out_like((2, inner, 2, rows, cols))] * slots,
        grid_spec=pltpu.PrefetchScalarGridSpec(
            num_scalar_prefetch=1,
            grid=(steps,),
            in_specs=green_specs + [screen_spec] * len(flat),
            out_specs=[out_spec] * slots,
            scratch_shapes=[
                pltpu.VMEM((3, total, block, cols), f32),
                pltpu.VMEM((3, total, block, cols), f32),
                pltpu.VMEM((total, 2, block, cols), f32),
            ],
        ),
        compiler_params=pltpu.CompilerParams(vmem_limit_bytes=32 * 2**20),
        cost_estimate=vpu_cost(total, rows * cols, 6 * total * rows * cols),
    )(where, *mine, *sib, *flat)


def cut_kernel(slots, where, *rest):
    for j in range(slots):
        for kind in range(2):
            rest[2 * slots + j][0, kind] = rest[kind * slots + j][0, 0]


def cut(where, greens, slots):
    inner, _, _, m, _ = greens[0].shape
    group = m // slots
    if group % 16:
        return [
            jnp.stack(
                [
                    lax.dynamic_slice_in_dim(g[:, 0], (where[0] ^ j) * group, group, axis=2)
                    for g in greens
                ],
                axis=1,
            )
            for j in range(slots)
        ]

    def block(j):
        return pl.BlockSpec((1, 1, 2, group, m), lambda e, s: (e, 0, 0, s[0] ^ j, 0))

    return pl.pallas_call(
        functools.partial(cut_kernel, slots),
        name="cut_rows",
        out_shape=[out_like((inner, 2, 2, group, m))] * slots,
        grid_spec=pltpu.PrefetchScalarGridSpec(
            num_scalar_prefetch=1,
            grid=(inner,),
            in_specs=[block(j) for j in range(slots)] * 2,
            out_specs=[pl.BlockSpec((1, 2, 2, group, m), lambda e, s: (e, 0, 0, 0, 0))] * slots,
        ),
        compiler_params=pltpu.CompilerParams(vmem_limit_bytes=56 * 2**20),
        cost_estimate=pl.CostEstimate(flops=0, bytes_accessed=16 * inner * m * m, transcendentals=0),
    )(where, *([greens[0]] * slots), *([greens[1]] * slots))


def matrices_kernel(slots, where, coupling, left, right, *held):
    count, _, m, _ = coupling.shape
    group = m // slots
    chip = where[0]
    for o in range(count):
        real, imag = coupling[o, 0].astype(f32), coupling[o, 1].astype(f32)
        real_t, imag_t = real.T.astype(bf16), imag.T.astype(bf16)
        base = 2 * m * o
        right[base : base + m, :m] = real_t
        right[base : base + m, m:] = -imag_t
        right[base + m : base + 2 * m, :m] = imag_t
        right[base + m : base + 2 * m, m:] = real_t
        if held:
            held[0][0], held[0][1] = real, imag
            source = held[0]
        else:
            source = coupling.at[o]
        for j in range(slots):
            start = pl.multiple_of((chip ^ j) * group, group)
            real = source[0, pl.ds(start, group), :].astype(bf16)
            imag = source[1, pl.ds(start, group), :].astype(bf16)
            low = j * group
            left[o, low : low + group, :m] = real
            left[o, low : low + group, m:] = -imag
            left[o, m + low : m + low + group, :m] = imag
            left[o, m + low : m + low + group, m:] = real


def coupling_matrices(where, coulomb, slots):
    count, _, m, _ = coulomb.shape
    vmem = pl.BlockSpec(memory_space=pltpu.VMEM)
    held = [] if (m // slots) % 16 == 0 else [pltpu.VMEM((2, m, m), f32)]
    return pl.pallas_call(
        functools.partial(matrices_kernel, slots),
        name="coupling",
        out_shape=[out_like((count, 2 * m, 2 * m)), out_like((count * 2 * m, 2 * m))],
        in_specs=[pl.BlockSpec(memory_space=pltpu.SMEM), vmem],
        out_specs=[vmem, vmem],
        scratch_shapes=held,
        compiler_params=pltpu.CompilerParams(vmem_limit_bytes=24 * 2**20),
        cost_estimate=pl.CostEstimate(flops=0, bytes_accessed=20 * coulomb.size, transcendentals=0),
    )(where, coulomb)


def pack_kernel(pieces, extra, *refs):
    for k in range(pieces):
        refs[pieces + extra][k] = refs[k][...]


def pack(pieces, block=None, index=None, after=()):
    count = len(pieces)
    block = block or pieces[0].shape
    index = index or (0,) * len(block)
    size = math.prod(block)
    return pl.pallas_call(
        functools.partial(pack_kernel, count, len(after)),
        name="pack",
        out_shape=out_like((count,) + block),
        grid=(1,),
        in_specs=[pl.BlockSpec(block, lambda i: index)] * count
        + [pl.BlockSpec(memory_space=pl.ANY)] * len(after),
        out_specs=pl.BlockSpec((count,) + block, lambda i: (0,) * (1 + len(block))),
        compiler_params=pltpu.CompilerParams(vmem_limit_bytes=16 * 2**20),
        cost_estimate=pl.CostEstimate(flops=0, bytes_accessed=4 * count * size, transcendentals=0),
    )(*pieces, *after)


def screen_kernel(slots, neighbours, each, final, where, left_ref, right_ref, *rest):
    count = len(neighbours)
    sources, rest = rest[: 2 * count], rest[2 * count :]
    if final:
        start_ref, rest = rest[0], rest[1:]
    outs, (pol, left) = rest[:-2], rest[-2:]
    rows, m = sources[0].shape[2:]
    chip = where[0]
    for n in range(count):
        near, far = sources[2 * n], sources[2 * n + 1]
        for j in range(slots):
            for part in range(2):
                start = pl.multiple_of(part * m + (chip ^ j) * rows, rows)
                for i in range(each):
                    piece = near[i, part] if j == 0 else far[j - 1, i, part]
                    pol[n, i, pl.ds(start, rows), :] = piece.astype(pol.dtype)
    for n, o in enumerate(neighbours):
        both = jnp.concatenate([pol[n, i].astype(bf16) for i in range(each)], axis=1)
        product = jnp.dot(left_ref[o], both, preferred_element_type=f32).astype(bf16)
        for i in range(each):
            for part in range(2):
                left[i, :, (2 * n + part) * m : (2 * n + part + 1) * m] = product[
                    part * m : (part + 1) * m, i * m : (i + 1) * m
                ]
    for i in range(each):
        result = start_ref[i] if final else None
        for n, o in enumerate(neighbours):
            term = jnp.dot(
                left[i, :, 2 * n * m : 2 * (n + 1) * m],
                right_ref[2 * o * m : 2 * (o + 1) * m, :],
                preferred_element_type=f32,
            )
            result = term if result is None else result + term
        if not final:
            outs[0][i] = result
            continue
        result = result.astype(bf16)
        for j in range(slots):
            for part in range(2):
                outs[j][i, part] = result[j * rows : (j + 1) * rows, part * m : (part + 1) * m]


def screen(where, left_matrix, right_matrix, sources, neighbours, slots, start=None):
    each, _, rows, m = sources[0].shape
    count = len(neighbours)
    vmem = pl.BlockSpec(memory_space=pltpu.VMEM)
    flops = 16 * each * count * m * m * m
    moved = 4 * each * m * m * (count + 1) + 2 * (left_matrix.size + right_matrix.size)
    hold = bf16 if rows % 16 == 0 else f32
    final = start is not None
    if final:
        shapes = [out_like((each, 2, rows, m))] * slots
    else:
        shapes = [jax.ShapeDtypeStruct((each, m, 2 * m), f32)]
    operands = list(sources) + ([start] if final else [])
    found = pl.pallas_call(
        functools.partial(screen_kernel, slots, neighbours, each, final),
        name="screen",
        out_shape=shapes,
        in_specs=[pl.BlockSpec(memory_space=pltpu.SMEM)] + [vmem] * (2 + len(operands)),
        out_specs=[vmem] * len(shapes),
        scratch_shapes=[
            pltpu.VMEM((count, each, 2 * m, m), hold),
            pltpu.VMEM((each, m, 2 * count * m), bf16),
        ],
        compiler_params=pltpu.CompilerParams(vmem_limit_bytes=44 * 2**20),
        cost_estimate=pl.CostEstimate(flops=flops, bytes_accessed=moved, transcendentals=0),
    )(where, left_matrix, right_matrix, *operands)
    return found if final else found[0]


def collect_kernel(slots, parts, where, *rest):
    count = slots * parts
    own, other = rest[:count], rest[count : count + parts]
    less, great = rest[count + parts :]
    core = where[1]
    for k in range(count):

        @pl.when(pl.program_id(0) == k)
        def _(k=k):
            h, j = divmod(k, slots)
            mine, theirs = own[k][0], other[h][j]
            less[:, 0] = jnp.where(core == 0, mine, theirs)
            great[:, 0] = jnp.where(core == 0, theirs, mine)


def collect(where, own, other, inner, m):
    parts, slots = len(own), len(own[0])
    rows = m // (slots * parts)
    if rows % 16:
        target = jnp.zeros((2, inner, 1, 2, m, m), bf16)
        for h in range(parts):
            for j in range(slots):
                pair = jnp.stack([own[h][j][0], other[h][j]])
                pair = jnp.where(where[1] == 0, pair, pair[::-1])[:, :, None]
                start = ((where[0] ^ j) * parts + h) * rows
                target = lax.dynamic_update_slice_in_dim(target, pair, start, axis=4)
        return target[0], target[1]
    flat = [piece for pieces in own for piece in pieces]
    vmem = [
        pl.BlockSpec((1, inner, 2, rows, m), lambda i, s: (0, 0, 0, 0, 0)) for _ in flat
    ] + [pl.BlockSpec((slots, inner, 2, rows, m), lambda i, s: (0, 0, 0, 0, 0)) for _ in other]
    shape = (inner, 1, 2, m, m)
    target = pl.BlockSpec(
        (inner, 1, 2, rows, m),
        lambda i, s: (0, 0, 0, (s[0] ^ lax.rem(i, slots)) * parts + lax.div(i, slots), 0),
    )
    return pl.pallas_call(
        functools.partial(collect_kernel, slots, parts),
        name="collect",
        out_shape=[out_like(shape)] * 2,
        grid_spec=pltpu.PrefetchScalarGridSpec(
            num_scalar_prefetch=1,
            grid=(parts * slots,),
            in_specs=vmem,
            out_specs=[target] * 2,
        ),
        compiler_params=pltpu.CompilerParams(vmem_limit_bytes=24 * 2**20),
        cost_estimate=pl.CostEstimate(
            flops=0, bytes_accessed=16 * inner * m * m, transcendentals=0
        ),
    )(where, *flat, *other)


def local(lesser_green, greater_green, coulomb_blocks):
    pieces = lax.axis_size("energy")
    slots = pieces // 2
    inner, _, _, m, _ = lesser_green.shape
    group = m // slots
    parts = 2 if group % 32 == 0 else 1
    rows = group // parts
    chunks = 2
    index = lax.axis_index("energy")
    where = jnp.stack([index // 2, index % 2]).astype(jnp.int32)
    others = range(1, slots)

    found = cut(where, (lesser_green, greater_green), slots)
    greens = [found[0]] + [swap(found[j], 2 * j) for j in others]
    left, right = coupling_matrices(where, coulomb_blocks[0], slots)

    middle = (slots + 1) // 2
    mine = [pack(greens[:middle])]
    sib = [swap(mine[0], 1)]
    mine.append(pack(greens[middle:], after=sib[:]))
    sib.append(swap(mine[1], 1))

    pol, near, after = [], [], []
    for c in range(chunks):
        found = correlate(where, mine, sib, chunks, c, after)
        after = [found[0]]
        near.append([shift(found[0], 1), found[0], shift(found[0], -1)])
        pol.append([swap(found[j], 2 * j) for j in others])

    screens = []
    after = [near[-1][1]]
    for c in range(chunks):
        far = pack(pol[c], after=after + [near[c][0], near[c][2]])
        after = [shift(far, 1), shift(far, -1)]
        crossed = [near[c][0], after[0], near[c][2], after[1]]
        start = screen(where, left, right, [near[c][1], far], (1,), slots)
        found = screen(where, left, right, crossed, (0, 2), slots, start)
        screens.append([found[0]] + [swap(found[j], 2 * j) for j in others])

    own, other = [], []
    for h in range(parts):
        found = self_energy(where, mine, sib, screens, h, rows)
        own.append([found[0]] + [swap(found[j], 2 * j) for j in others])
        other.append(swap(jnp.stack([piece[1] for piece in own[h]]), 1))
    return tuple(collect(where, own, other, inner, m))


def solution(mesh):
    return jax.shard_map(
        local,
        mesh=mesh,
        in_specs=(
            P("energy", "blk", None, None, None),
            P("energy", "blk", None, None, None),
            P("blk", None, None, None, None),
        ),
        out_specs=(P("energy", "blk", None, None, None), P("energy", "blk", None, None, None)),
        check_vma=False,
    )
```

```python
import functools
import math

import jax
import jax.numpy as jnp
from jax import lax
from jax.experimental import pallas as pl
from jax.experimental.pallas import tpu as pltpu
from jax.sharding import PartitionSpec as P

f32 = jnp.float32
bf16 = jnp.bfloat16


def swap(value, distance):
    count = lax.axis_size("energy")
    return lax.ppermute(value, "energy", [(i, i ^ distance) for i in range(count)])


def shift(value, step):
    count = lax.axis_size("blk")
    pairs = [(i, i + step) for i in range(count) if 0 <= i + step < count]
    return lax.ppermute(value, "blk", pairs)


def row_block(rows):
    for size in (16, 8):
        if rows % size == 0:
            return size
    return rows


def out_like(shape):
    return jax.ShapeDtypeStruct(shape, bf16)


def vpu_cost(total, elements, moved):
    return pl.CostEstimate(
        flops=3 * total * (total + 1) * elements, bytes_accessed=2 * moved, transcendentals=0
    )


def tiles(rows, cols, body):
    lanes = 128 if cols % 128 == 0 else cols
    sub = 8 if rows % 8 == 0 else rows
    across = cols // lanes

    def step(t, carry):
        r = pl.multiple_of(lax.div(t, across) * sub, sub)
        c = pl.multiple_of(lax.rem(t, across) * lanes, lanes)
        body((pl.ds(r, sub), pl.ds(c, lanes)))
        return carry

    lax.fori_loop(0, (rows // sub) * across, step, 0)


def lag_of(total, slots, chunks, chunk, slot, i):
    return (chunks - 1 - chunk) * (total // chunks) + slot * (total // (chunks * slots)) + i


def load_greens(slots, inner, where, mine, sib, put):
    chip, core = where[0], where[1]
    for half, sources in ((core, mine), (1 - core, sib)):
        j = 0
        for source in sources:
            for k in range(source.shape[0]):
                for i in range(inner):
                    put((2 * (chip ^ j) + half) * inner + i, source, k, i)
                j += 1


def correlate_kernel(slots, inner, chunks, chunk, halves, extra, where, *rest):
    mine, sib = rest[:halves], rest[halves : 2 * halves]
    rest = rest[2 * halves + extra :]
    outs, (x_scr, y_scr, o_scr) = rest[:slots], rest[slots:]
    chip, core = where[0], where[1]
    total = 2 * inner * slots
    rows, cols = mine[0].shape[-2:]

    def put(e, source, k, i):
        a = source[k, i, core, 0].astype(f32)
        b = source[k, i, core, 1].astype(f32)
        x_scr[0, e], x_scr[1, e], x_scr[2, e] = a, b, a + b
        a = source[k, i, 1 - core, 0].astype(f32)
        b = source[k, i, 1 - core, 1].astype(f32)
        y_scr[0, e], y_scr[1, e], y_scr[2, e] = a, b, a - b

    load_greens(slots, inner, where, mine, sib, put)
    factor = -1.0 / math.sqrt(total)
    width = 4
    first_lag = lag_of(total, slots, chunks, chunk, 0, 0)
    last_lag = first_lag + total // chunks

    def body(at):
        for base in range(first_lag, last_lag, width):
            lags = range(base, min(base + width, last_lag))
            sums = {}
            window = {}
            for e in range(total - base):
                y = [y_scr[(p, e) + at] for p in range(3)]
                for w in lags:
                    if e + w >= total:
                        continue
                    if e + w not in window:
                        window[e + w] = [x_scr[(p, e + w) + at] for p in range(3)]
                    terms = [window[e + w][p] * y[p] for p in range(3)]
                    sums[w] = [s + t for s, t in zip(sums[w], terms)] if w in sums else terms
                window.pop(e + base, None)
            for w in lags:
                first, second, third = sums[w]
                o_scr[(w - first_lag, 0) + at] = factor * (first + second)
                o_scr[(w - first_lag, 1) + at] = factor * (third - first + second)

    tiles(rows, cols, body)
    each = 2 * inner // chunks
    for j in range(slots):
        for i in range(each):
            outs[j][i] = o_scr[(chip ^ j) * each + i].astype(bf16)


def correlate(where, mine, sib, chunks, chunk, after):
    _, inner, _, _, rows, cols = mine[0].shape
    slots = sum(piece.shape[0] for piece in mine)
    total = 2 * inner * slots
    each = 2 * inner // chunks
    block = row_block(rows)
    in_specs = [
        pl.BlockSpec((piece.shape[0], inner, 2, 2, block, cols), lambda r, s: (0, 0, 0, 0, r, 0))
        for piece in (*mine, *sib)
    ]
    out_spec = pl.BlockSpec((each, 2, block, cols), lambda r, s: (0, 0, r, 0))
    return pl.pallas_call(
        functools.partial(correlate_kernel, slots, inner, chunks, chunk, len(mine), len(after)),
        name="correlate",
        out_shape=[out_like((each, 2, rows, cols))] * slots,
        grid_spec=pltpu.PrefetchScalarGridSpec(
            num_scalar_prefetch=1,
            grid=(rows // block,),
            in_specs=in_specs + [pl.BlockSpec(memory_space=pl.ANY)] * len(after),
            out_specs=[out_spec] * slots,
            scratch_shapes=[
                pltpu.VMEM((3, total, block, cols), f32),
                pltpu.VMEM((3, total, block, cols), f32),
                pltpu.VMEM((total // chunks, 2, block, cols), f32),
            ],
        ),
        compiler_params=pltpu.CompilerParams(vmem_limit_bytes=32 * 2**20),
        cost_estimate=vpu_cost(total, rows * cols // chunks, 4 * total * rows * cols),
    )(where, *mine, *sib, *after)


def sigma_kernel(slots, inner, chunks, halves, where, *rest):
    mine, sib = rest[:halves], rest[halves : 2 * halves]
    rest = rest[2 * halves :]
    screens = rest[: slots * chunks]
    outs = rest[slots * chunks : slots * chunks + slots]
    x_scr, y_scr, o_scr = rest[slots * chunks + slots :]
    chip, core = where[0], where[1]
    total = 2 * inner * slots
    rows, cols = mine[0].shape[-2:]
    each = 2 * inner // chunks

    def put(e, source, k, i):
        a = source[k, i, 0, 0].astype(f32)
        b = source[k, i, 0, 1].astype(f32)
        x_scr[0, e], x_scr[1, e], x_scr[2, e] = a, b, a + b

    load_greens(slots, inner, where, mine, sib, put)
    for j in range(slots):
        for chunk in range(chunks):
            source = screens[chunk * slots + j]
            for i in range(each):
                w = lag_of(total, slots, chunks, chunk, chip ^ j, i)
                a = source[i, 0].astype(f32)
                b = source[i, 1].astype(f32)
                y_scr[0, w], y_scr[1, w], y_scr[2, w] = a, b, a + b
    factor = 1.0 / math.sqrt(total)
    width = 4

    def body(at):
        for base in range(0, total, width):
            energies = range(base, min(base + width, total))
            sums = {}
            window = {}
            for w in range(min(base + width, total)):
                y = [y_scr[(p, w) + at] for p in range(3)]
                for e in energies:
                    if e < w:
                        continue
                    if e - w not in window:
                        window[e - w] = [x_scr[(p, e - w) + at] for p in range(3)]
                    terms = [window[e - w][p] * y[p] for p in range(3)]
                    sums[e] = [s + t for s, t in zip(sums[e], terms)] if e in sums else terms
                window.pop(base + width - 1 - w, None)
            for e in energies:
                first, second, third = sums[e]
                o_scr[(e, 0) + at] = factor * (first - second)
                o_scr[(e, 1) + at] = factor * (third - first - second)

    tiles(rows, cols, body)
    for j in range(slots):
        for side in range(2):
            half = core if side == 0 else 1 - core
            for i in range(inner):
                e = (2 * (chip ^ j) + half) * inner + i
                outs[j][side, i] = o_scr[e].astype(bf16)


def self_energy(where, mine, sib, screens, part, rows):
    _, inner, _, _, _, cols = mine[0].shape
    slots = sum(piece.shape[0] for piece in mine)
    chunks = len(screens)
    flat = [piece for chunk in screens for piece in chunk]
    each = flat[0].shape[0]
    total = 2 * inner * slots
    block = row_block(rows)
    steps = rows // block
    green_specs = [
        pl.BlockSpec(
            (piece.shape[0], inner, 1, 2, block, cols),
            lambda r, s: (0, 0, s[1], 0, part * steps + r, 0),
        )
        for piece in (*mine, *sib)
    ]
    screen_spec = pl.BlockSpec((each, 2, block, cols), lambda r, s: (0, 0, part * steps + r, 0))
    out_spec = pl.BlockSpec((2, inner, 2, block, cols), lambda r, s: (0, 0, 0, r, 0))
    return pl.pallas_call(
        functools.partial(sigma_kernel, slots, inner, chunks, len(mine)),
        name="sigma",
        out_shape=[out_like((2, inner, 2, rows, cols))] * slots,
        grid_spec=pltpu.PrefetchScalarGridSpec(
            num_scalar_prefetch=1,
            grid=(steps,),
            in_specs=green_specs + [screen_spec] * len(flat),
            out_specs=[out_spec] * slots,
            scratch_shapes=[
                pltpu.VMEM((3, total, block, cols), f32),
                pltpu.VMEM((3, total, block, cols), f32),
                pltpu.VMEM((total, 2, block, cols), f32),
            ],
        ),
        compiler_params=pltpu.CompilerParams(vmem_limit_bytes=32 * 2**20),
        cost_estimate=vpu_cost(total, rows * cols, 6 * total * rows * cols),
    )(where, *mine, *sib, *flat)


def cut_kernel(slots, where, *rest):
    for j in range(slots):
        for kind in range(2):
            rest[2 * slots + j][0, kind] = rest[kind * slots + j][0, 0]


def cut(where, greens, slots):
    inner, _, _, m, _ = greens[0].shape
    group = m // slots
    if group % 16:
        return [
            jnp.stack(
                [
                    lax.dynamic_slice_in_dim(g[:, 0], (where[0] ^ j) * group, group, axis=2)
                    for g in greens
                ],
                axis=1,
            )
            for j in range(slots)
        ]

    def block(j):
        return pl.BlockSpec((1, 1, 2, group, m), lambda e, s: (e, 0, 0, s[0] ^ j, 0))

    return pl.pallas_call(
        functools.partial(cut_kernel, slots),
        name="cut_rows",
        out_shape=[out_like((inner, 2, 2, group, m))] * slots,
        grid_spec=pltpu.PrefetchScalarGridSpec(
            num_scalar_prefetch=1,
            grid=(inner,),
            in_specs=[block(j) for j in range(slots)] * 2,
            out_specs=[pl.BlockSpec((1, 2, 2, group, m), lambda e, s: (e, 0, 0, 0, 0))] * slots,
        ),
        compiler_params=pltpu.CompilerParams(vmem_limit_bytes=56 * 2**20),
        cost_estimate=pl.CostEstimate(flops=0, bytes_accessed=16 * inner * m * m, transcendentals=0),
    )(where, *([greens[0]] * slots), *([greens[1]] * slots))


def matrices_kernel(slots, where, coupling, left, right, *held):
    count, _, m, _ = coupling.shape
    group = m // slots
    chip = where[0]
    for o in range(count):
        real, imag = coupling[o, 0].astype(f32), coupling[o, 1].astype(f32)
        real_t, imag_t = real.T.astype(bf16), imag.T.astype(bf16)
        base = 2 * m * o
        right[base : base + m, :m] = real_t
        right[base : base + m, m:] = -imag_t
        right[base + m : base + 2 * m, :m] = imag_t
        right[base + m : base + 2 * m, m:] = real_t
        if held:
            held[0][0], held[0][1] = real, imag
            source = held[0]
        else:
            source = coupling.at[o]
        for j in range(slots):
            start = pl.multiple_of((chip ^ j) * group, group)
            real = source[0, pl.ds(start, group), :].astype(bf16)
            imag = source[1, pl.ds(start, group), :].astype(bf16)
            low = j * group
            left[o, low : low + group, :m] = real
            left[o, low : low + group, m:] = -imag
            left[o, m + low : m + low + group, :m] = imag
            left[o, m + low : m + low + group, m:] = real


def coupling_matrices(where, coulomb, slots):
    count, _, m, _ = coulomb.shape
    vmem = pl.BlockSpec(memory_space=pltpu.VMEM)
    held = [] if (m // slots) % 16 == 0 else [pltpu.VMEM((2, m, m), f32)]
    return pl.pallas_call(
        functools.partial(matrices_kernel, slots),
        name="coupling",
        out_shape=[out_like((count, 2 * m, 2 * m)), out_like((count * 2 * m, 2 * m))],
        in_specs=[pl.BlockSpec(memory_space=pltpu.SMEM), vmem],
        out_specs=[vmem, vmem],
        scratch_shapes=held,
        compiler_params=pltpu.CompilerParams(vmem_limit_bytes=24 * 2**20),
        cost_estimate=pl.CostEstimate(flops=0, bytes_accessed=20 * coulomb.size, transcendentals=0),
    )(where, coulomb)


def pack_kernel(pieces, extra, *refs):
    for k in range(pieces):
        refs[pieces + extra][k] = refs[k][...]


def pack(pieces, block=None, index=None, after=()):
    count = len(pieces)
    block = block or pieces[0].shape
    index = index or (0,) * len(block)
    size = math.prod(block)
    return pl.pallas_call(
        functools.partial(pack_kernel, count, len(after)),
        name="pack",
        out_shape=out_like((count,) + block),
        grid=(1,),
        in_specs=[pl.BlockSpec(block, lambda i: index)] * count
        + [pl.BlockSpec(memory_space=pl.ANY)] * len(after),
        out_specs=pl.BlockSpec((count,) + block, lambda i: (0,) * (1 + len(block))),
        compiler_params=pltpu.CompilerParams(vmem_limit_bytes=16 * 2**20),
        cost_estimate=pl.CostEstimate(flops=0, bytes_accessed=4 * count * size, transcendentals=0),
    )(*pieces, *after)


def screen_kernel(slots, neighbours, each, final, where, left_ref, right_ref, *rest):
    count = len(neighbours)
    sources, rest = rest[: 2 * count], rest[2 * count :]
    if final:
        start_ref, rest = rest[0], rest[1:]
    outs, (pol, left) = rest[:-2], rest[-2:]
    rows, m = sources[0].shape[2:]
    chip = where[0]
    for n in range(count):
        near, far = sources[2 * n], sources[2 * n + 1]
        for j in range(slots):
            for part in range(2):
                start = pl.multiple_of(part * m + (chip ^ j) * rows, rows)
                for i in range(each):
                    piece = near[i, part] if j == 0 else far[j - 1, i, part]
                    pol[n, i, pl.ds(start, rows), :] = piece.astype(pol.dtype)
    for n, o in enumerate(neighbours):
        both = jnp.concatenate([pol[n, i].astype(bf16) for i in range(each)], axis=1)
        product = jnp.dot(left_ref[o], both, preferred_element_type=f32).astype(bf16)
        for i in range(each):
            for part in range(2):
                left[i, :, (2 * n + part) * m : (2 * n + part + 1) * m] = product[
                    part * m : (part + 1) * m, i * m : (i + 1) * m
                ]
    for i in range(each):
        result = start_ref[i] if final else None
        for n, o in enumerate(neighbours):
            term = jnp.dot(
                left[i, :, 2 * n * m : 2 * (n + 1) * m],
                right_ref[2 * o * m : 2 * (o + 1) * m, :],
                preferred_element_type=f32,
            )
            result = term if result is None else result + term
        if not final:
            outs[0][i] = result
            continue
        result = result.astype(bf16)
        for j in range(slots):
            for part in range(2):
                outs[j][i, part] = result[j * rows : (j + 1) * rows, part * m : (part + 1) * m]


def screen(where, left_matrix, right_matrix, sources, neighbours, slots, start=None):
    each, _, rows, m = sources[0].shape
    count = len(neighbours)
    vmem = pl.BlockSpec(memory_space=pltpu.VMEM)
    flops = 16 * each * count * m * m * m
    moved = 4 * each * m * m * (count + 1) + 2 * (left_matrix.size + right_matrix.size)
    hold = bf16 if rows % 16 == 0 else f32
    final = start is not None
    if final:
        shapes = [out_like((each, 2, rows, m))] * slots
    else:
        shapes = [jax.ShapeDtypeStruct((each, m, 2 * m), f32)]
    operands = list(sources) + ([start] if final else [])
    found = pl.pallas_call(
        functools.partial(screen_kernel, slots, neighbours, each, final),
        name="screen",
        out_shape=shapes,
        in_specs=[pl.BlockSpec(memory_space=pltpu.SMEM)] + [vmem] * (2 + len(operands)),
        out_specs=[vmem] * len(shapes),
        scratch_shapes=[
            pltpu.VMEM((count, each, 2 * m, m), hold),
            pltpu.VMEM((each, m, 2 * count * m), bf16),
        ],
        compiler_params=pltpu.CompilerParams(vmem_limit_bytes=44 * 2**20),
        cost_estimate=pl.CostEstimate(flops=flops, bytes_accessed=moved, transcendentals=0),
    )(where, left_matrix, right_matrix, *operands)
    return found if final else found[0]


def collect_kernel(slots, parts, where, *rest):
    count = slots * parts
    own, other = rest[:count], rest[count : count + parts]
    less, great = rest[count + parts :]
    core = where[1]
    for k in range(count):

        @pl.when(pl.program_id(0) == k)
        def _(k=k):
            h, j = divmod(k, slots)
            mine, theirs = own[k][0], other[h][j]
            less[:, 0] = jnp.where(core == 0, mine, theirs)
            great[:, 0] = jnp.where(core == 0, theirs, mine)


def collect(where, own, other, inner, m):
    parts, slots = len(own), len(own[0])
    rows = m // (slots * parts)
    if rows % 16:
        target = jnp.zeros((2, inner, 1, 2, m, m), bf16)
        for h in range(parts):
            for j in range(slots):
                pair = jnp.stack([own[h][j][0], other[h][j]])
                pair = jnp.where(where[1] == 0, pair, pair[::-1])[:, :, None]
                start = ((where[0] ^ j) * parts + h) * rows
                target = lax.dynamic_update_slice_in_dim(target, pair, start, axis=4)
        return target[0], target[1]
    flat = [piece for pieces in own for piece in pieces]
    vmem = [
        pl.BlockSpec((1, inner, 2, rows, m), lambda i, s: (0, 0, 0, 0, 0)) for _ in flat
    ] + [pl.BlockSpec((slots, inner, 2, rows, m), lambda i, s: (0, 0, 0, 0, 0)) for _ in other]
    shape = (inner, 1, 2, m, m)
    target = pl.BlockSpec(
        (inner, 1, 2, rows, m),
        lambda i, s: (0, 0, 0, (s[0] ^ lax.rem(i, slots)) * parts + lax.div(i, slots), 0),
    )
    return pl.pallas_call(
        functools.partial(collect_kernel, slots, parts),
        name="collect",
        out_shape=[out_like(shape)] * 2,
        grid_spec=pltpu.PrefetchScalarGridSpec(
            num_scalar_prefetch=1,
            grid=(parts * slots,),
            in_specs=vmem,
            out_specs=[target] * 2,
        ),
        compiler_params=pltpu.CompilerParams(vmem_limit_bytes=24 * 2**20),
        cost_estimate=pl.CostEstimate(
            flops=0, bytes_accessed=16 * inner * m * m, transcendentals=0
        ),
    )(where, *flat, *other)


def local(lesser_green, greater_green, coulomb_blocks):
    pieces = lax.axis_size("energy")
    slots = pieces // 2
    inner, _, _, m, _ = lesser_green.shape
    group = m // slots
    parts = 2 if group % 32 == 0 else 1
    rows = group // parts
    chunks = 2
    index = lax.axis_index("energy")
    where = jnp.stack([index // 2, index % 2]).astype(jnp.int32)
    others = range(1, slots)

    found = cut(where, (lesser_green, greater_green), slots)
    greens = [found[0]] + [swap(found[j], 2 * j) for j in others]
    left, right = coupling_matrices(where, coulomb_blocks[0], slots)

    middle = (slots + 1) // 2
    mine = [pack(group) for group in (greens[middle:], greens[:middle])][::-1]
    sib = [swap(piece, 1) for piece in mine[::-1]][::-1]

    pol, near, after = [], [], []
    for c in range(chunks):
        found = correlate(where, mine, sib, chunks, c, after)
        after = [found[0]]
        near.append([shift(found[0], 1), found[0], shift(found[0], -1)])
        pol.append([swap(found[j], 2 * j) for j in others])

    screens = []
    after = [piece for triple in near for piece in (triple[0], triple[2])] + [near[-1][1]]
    for c in range(chunks):
        far = pack(pol[c], after=after)
        after = [shift(far, 1), shift(far, -1)]
        crossed = [near[c][0], after[0], near[c][2], after[1]]
        start = screen(where, left, right, [near[c][1], far], (1,), slots)
        found = screen(where, left, right, crossed, (0, 2), slots, start)
        screens.append([found[0]] + [swap(found[j], 2 * j) for j in others])

    own, other = [], []
    for h in range(parts):
        found = self_energy(where, mine, sib, screens, h, rows)
        own.append([found[0]] + [swap(found[j], 2 * j) for j in others])
        other.append(swap(jnp.stack([piece[1] for piece in own[h]]), 1))
    return tuple(collect(where, own, other, inner, m))


def solution(mesh):
    return jax.shard_map(
        local,
        mesh=mesh,
        in_specs=(
            P("energy", "blk", None, None, None),
            P("energy", "blk", None, None, None),
            P("blk", None, None, None, None),
        ),
        out_specs=(P("energy", "blk", None, None, None), P("energy", "blk", None, None, None)),
        check_vma=False,
    )
```

```python
import functools
import math

import jax
import jax.numpy as jnp
from jax import lax
from jax.experimental import pallas as pl
from jax.experimental.pallas import tpu as pltpu
from jax.sharding import PartitionSpec as P

f32 = jnp.float32
bf16 = jnp.bfloat16


def swap(value, distance):
    count = lax.axis_size("energy")
    return lax.ppermute(value, "energy", [(i, i ^ distance) for i in range(count)])


def trade(value, first):
    count = lax.axis_size("blk")
    lows = range(first, count - 1, 2)
    return lax.ppermute(value, "blk", [(i, i + 1) for i in lows] + [(i + 1, i) for i in lows])


def row_block(rows):
    for size in (16, 8):
        if rows % size == 0:
            return size
    return rows


def out_like(shape):
    return jax.ShapeDtypeStruct(shape, bf16)


def vpu_cost(total, elements, moved):
    return pl.CostEstimate(
        flops=3 * total * (total + 1) * elements, bytes_accessed=2 * moved, transcendentals=0
    )


def tiles(rows, cols, body):
    lanes = 128 if cols % 128 == 0 else cols
    sub = 8 if rows % 8 == 0 else rows
    across = cols // lanes

    def step(t, carry):
        r = pl.multiple_of(lax.div(t, across) * sub, sub)
        c = pl.multiple_of(lax.rem(t, across) * lanes, lanes)
        body((pl.ds(r, sub), pl.ds(c, lanes)))
        return carry

    lax.fori_loop(0, (rows // sub) * across, step, 0)


def lag_of(total, slots, chunks, chunk, slot, i):
    return (chunks - 1 - chunk) * (total // chunks) + slot * (total // (chunks * slots)) + i


def load_greens(slots, inner, where, mine, sib, put):
    chip, core = where[0], where[1]
    for half, sources in ((core, mine), (1 - core, sib)):
        j = 0
        for source in sources:
            for k in range(source.shape[0]):
                for i in range(inner):
                    put((2 * (chip ^ j) + half) * inner + i, source, k, i)
                j += 1


def correlate_kernel(slots, inner, chunks, chunk, halves, extra, where, *rest):
    mine, sib = rest[:halves], rest[halves : 2 * halves][::-1]
    rest = rest[2 * halves + extra :]
    outs, (x_scr, y_scr, o_scr) = rest[:slots], rest[slots:]
    chip, core = where[0], where[1]
    total = 2 * inner * slots
    rows, cols = mine[0].shape[-2:]

    def put(e, source, k, i):
        a = source[k, i, core, 0].astype(f32)
        b = source[k, i, core, 1].astype(f32)
        x_scr[0, e], x_scr[1, e], x_scr[2, e] = a, b, a + b
        a = source[k, i, 1 - core, 0].astype(f32)
        b = source[k, i, 1 - core, 1].astype(f32)
        y_scr[0, e], y_scr[1, e], y_scr[2, e] = a, b, a - b

    load_greens(slots, inner, where, mine, sib, put)
    factor = -1.0 / math.sqrt(total)
    width = 4
    first_lag = lag_of(total, slots, chunks, chunk, 0, 0)
    last_lag = first_lag + total // chunks

    def body(at):
        for base in range(first_lag, last_lag, width):
            lags = range(base, min(base + width, last_lag))
            sums = {}
            window = {}
            for e in range(total - base):
                y = [y_scr[(p, e) + at] for p in range(3)]
                for w in lags:
                    if e + w >= total:
                        continue
                    if e + w not in window:
                        window[e + w] = [x_scr[(p, e + w) + at] for p in range(3)]
                    terms = [window[e + w][p] * y[p] for p in range(3)]
                    sums[w] = [s + t for s, t in zip(sums[w], terms)] if w in sums else terms
                window.pop(e + base, None)
            for w in lags:
                first, second, third = sums[w]
                o_scr[(w - first_lag, 0) + at] = factor * (first + second)
                o_scr[(w - first_lag, 1) + at] = factor * (third - first + second)

    tiles(rows, cols, body)
    each = 2 * inner // chunks
    for j in range(slots):
        for i in range(each):
            outs[j][i] = o_scr[(chip ^ j) * each + i].astype(bf16)


def correlate(where, mine, sib, chunks, chunk, after):
    _, inner, _, _, rows, cols = mine[0].shape
    slots = sum(piece.shape[0] for piece in mine)
    total = 2 * inner * slots
    each = 2 * inner // chunks
    block = row_block(rows)
    in_specs = [
        pl.BlockSpec((piece.shape[0], inner, 2, 2, block, cols), lambda r, s: (0, 0, 0, 0, r, 0))
        for piece in (*mine, *sib[::-1])
    ]
    out_spec = pl.BlockSpec((each, 2, block, cols), lambda r, s: (0, 0, r, 0))
    return pl.pallas_call(
        functools.partial(correlate_kernel, slots, inner, chunks, chunk, len(mine), len(after)),
        name="correlate",
        out_shape=[out_like((each, 2, rows, cols))] * slots,
        grid_spec=pltpu.PrefetchScalarGridSpec(
            num_scalar_prefetch=1,
            grid=(rows // block,),
            in_specs=in_specs + [pl.BlockSpec(memory_space=pl.ANY)] * len(after),
            out_specs=[out_spec] * slots,
            scratch_shapes=[
                pltpu.VMEM((3, total, block, cols), f32),
                pltpu.VMEM((3, total, block, cols), f32),
                pltpu.VMEM((total // chunks, 2, block, cols), f32),
            ],
        ),
        compiler_params=pltpu.CompilerParams(vmem_limit_bytes=32 * 2**20),
        cost_estimate=vpu_cost(total, rows * cols // chunks, 4 * total * rows * cols),
    )(where, *mine, *sib[::-1], *after)


def sigma_kernel(slots, inner, chunks, halves, where, *rest):
    mine, sib = rest[:halves], rest[halves : 2 * halves][::-1]
    rest = rest[2 * halves :]
    screens = rest[: slots * chunks]
    outs = rest[slots * chunks : slots * chunks + slots]
    x_scr, y_scr, o_scr = rest[slots * chunks + slots :]
    chip, core = where[0], where[1]
    total = 2 * inner * slots
    rows, cols = mine[0].shape[-2:]
    each = 2 * inner // chunks

    def put(e, source, k, i):
        a = source[k, i, 0, 0].astype(f32)
        b = source[k, i, 0, 1].astype(f32)
        x_scr[0, e], x_scr[1, e], x_scr[2, e] = a, b, a + b

    load_greens(slots, inner, where, mine, sib, put)
    for j in range(slots):
        for chunk in range(chunks):
            source = screens[chunk * slots + j]
            for i in range(each):
                w = lag_of(total, slots, chunks, chunk, chip ^ j, i)
                a = source[i, 0].astype(f32)
                b = source[i, 1].astype(f32)
                y_scr[0, w], y_scr[1, w], y_scr[2, w] = a, b, a + b
    factor = 1.0 / math.sqrt(total)
    width = 4

    def body(at):
        for base in range(0, total, width):
            energies = range(base, min(base + width, total))
            sums = {}
            window = {}
            for w in range(min(base + width, total)):
                y = [y_scr[(p, w) + at] for p in range(3)]
                for e in energies:
                    if e < w:
                        continue
                    if e - w not in window:
                        window[e - w] = [x_scr[(p, e - w) + at] for p in range(3)]
                    terms = [window[e - w][p] * y[p] for p in range(3)]
                    sums[e] = [s + t for s, t in zip(sums[e], terms)] if e in sums else terms
                window.pop(base + width - 1 - w, None)
            for e in energies:
                first, second, third = sums[e]
                o_scr[(e, 0) + at] = factor * (first - second)
                o_scr[(e, 1) + at] = factor * (third - first - second)

    tiles(rows, cols, body)
    for j in range(slots):
        for side in range(2):
            half = core if side == 0 else 1 - core
            for i in range(inner):
                e = (2 * (chip ^ j) + half) * inner + i
                outs[j][side, i] = o_scr[e].astype(bf16)


def self_energy(where, mine, sib, screens, part, rows):
    _, inner, _, _, _, cols = mine[0].shape
    slots = sum(piece.shape[0] for piece in mine)
    chunks = len(screens)
    flat = [piece for chunk in screens for piece in chunk]
    each = flat[0].shape[0]
    total = 2 * inner * slots
    block = row_block(rows)
    steps = rows // block
    green_specs = [
        pl.BlockSpec(
            (piece.shape[0], inner, 1, 2, block, cols),
            lambda r, s: (0, 0, s[1], 0, part * steps + r, 0),
        )
        for piece in (*mine, *sib[::-1])
    ]
    screen_spec = pl.BlockSpec((each, 2, block, cols), lambda r, s: (0, 0, part * steps + r, 0))
    out_spec = pl.BlockSpec((2, inner, 2, block, cols), lambda r, s: (0, 0, 0, r, 0))
    return pl.pallas_call(
        functools.partial(sigma_kernel, slots, inner, chunks, len(mine)),
        name="sigma",
        out_shape=[out_like((2, inner, 2, rows, cols))] * slots,
        grid_spec=pltpu.PrefetchScalarGridSpec(
            num_scalar_prefetch=1,
            grid=(steps,),
            in_specs=green_specs + [screen_spec] * len(flat),
            out_specs=[out_spec] * slots,
            scratch_shapes=[
                pltpu.VMEM((3, total, block, cols), f32),
                pltpu.VMEM((3, total, block, cols), f32),
                pltpu.VMEM((total, 2, block, cols), f32),
            ],
        ),
        compiler_params=pltpu.CompilerParams(vmem_limit_bytes=32 * 2**20),
        cost_estimate=vpu_cost(total, rows * cols, 6 * total * rows * cols),
    )(where, *mine, *sib[::-1], *flat)


def cut_kernel(count, where, *rest):
    for k in range(count):
        for kind in range(2):
            rest[2 * count + k][0, kind] = rest[kind * count + k][0, 0]


def cut(where, greens, slots, wanted):
    inner, _, _, m, _ = greens[0].shape
    group = m // slots
    count = len(wanted)
    if group % 16:
        return [
            jnp.stack(
                [
                    lax.dynamic_slice_in_dim(g[:, 0], (where[0] ^ j) * group, group, axis=2)
                    for g in greens
                ],
                axis=1,
            )
            for j in wanted
        ]

    def block(j):
        return pl.BlockSpec((1, 1, 2, group, m), lambda e, s: (e, 0, 0, s[0] ^ j, 0))

    return pl.pallas_call(
        functools.partial(cut_kernel, count),
        name="cut_rows",
        out_shape=[out_like((inner, 2, 2, group, m))] * count,
        grid_spec=pltpu.PrefetchScalarGridSpec(
            num_scalar_prefetch=1,
            grid=(inner,),
            in_specs=[block(j) for j in wanted] * 2,
            out_specs=[pl.BlockSpec((1, 2, 2, group, m), lambda e, s: (e, 0, 0, 0, 0))] * count,
        ),
        compiler_params=pltpu.CompilerParams(vmem_limit_bytes=56 * 2**20),
        cost_estimate=pl.CostEstimate(flops=0, bytes_accessed=16 * inner * count * group * m, transcendentals=0),
    )(where, *([greens[0]] * count), *([greens[1]] * count))


def matrices_kernel(slots, where, coupling, left, right, *held):
    count, _, m, _ = coupling.shape
    group = m // slots
    chip = where[0]
    for o in range(count):
        real, imag = coupling[o, 0].astype(f32), coupling[o, 1].astype(f32)
        real_t, imag_t = real.T.astype(bf16), imag.T.astype(bf16)
        right[o, :m, :m] = real_t
        right[o, :m, m:] = -imag_t
        right[o, m:, :m] = imag_t
        right[o, m:, m:] = real_t
        if held:
            held[0][0], held[0][1] = real, imag
            source = held[0]
        else:
            source = coupling.at[o]
        for j in range(slots):
            start = pl.multiple_of((chip ^ j) * group, group)
            real = source[0, pl.ds(start, group), :].astype(bf16)
            imag = source[1, pl.ds(start, group), :].astype(bf16)
            low = j * group
            left[o, low : low + group, :m] = real
            left[o, low : low + group, m:] = -imag
            left[o, m + low : m + low + group, :m] = imag
            left[o, m + low : m + low + group, m:] = real


def coupling_matrices(where, coulomb, slots):
    count, _, m, _ = coulomb.shape
    vmem = pl.BlockSpec(memory_space=pltpu.VMEM)
    held = [] if (m // slots) % 16 == 0 else [pltpu.VMEM((2, m, m), f32)]
    return pl.pallas_call(
        functools.partial(matrices_kernel, slots),
        name="coupling",
        out_shape=[out_like((count, 2 * m, 2 * m))] * 2,
        in_specs=[pl.BlockSpec(memory_space=pltpu.SMEM), vmem],
        out_specs=[vmem, vmem],
        scratch_shapes=held,
        compiler_params=pltpu.CompilerParams(vmem_limit_bytes=24 * 2**20),
        cost_estimate=pl.CostEstimate(flops=0, bytes_accessed=20 * coulomb.size, transcendentals=0),
    )(where, coulomb)


def pack_kernel(pieces, extra, *refs):
    for k in range(pieces):
        refs[pieces + extra][k] = refs[k][...]


def pack(pieces, block=None, index=None, after=()):
    count = len(pieces)
    block = block or pieces[0].shape
    index = index or (0,) * len(block)
    size = math.prod(block)
    return pl.pallas_call(
        functools.partial(pack_kernel, count, len(after)),
        name="pack",
        out_shape=out_like((count,) + block),
        grid=(1,),
        in_specs=[pl.BlockSpec(block, lambda i: index)] * count
        + [pl.BlockSpec(memory_space=pl.ANY)] * len(after),
        out_specs=pl.BlockSpec((count,) + block, lambda i: (0,) * (1 + len(block))),
        compiler_params=pltpu.CompilerParams(vmem_limit_bytes=16 * 2**20),
        cost_estimate=pl.CostEstimate(flops=0, bytes_accessed=4 * count * size, transcendentals=0),
    )(*pieces, *after)


def screen_kernel(slots, each, final, where, left_ref, right_ref, *rest):
    odd = where[2]
    neighbours = (2 - 2 * odd, 2 * odd) if final else (1,)
    count = len(neighbours)
    per_source = 2 if final else slots
    sources, rest = rest[: per_source * count], rest[per_source * count :]
    if final:
        start_ref, rest = rest[0], rest[1:]
    outs, (pol, left) = rest[:-2], rest[-2:]
    rows, m = sources[0].shape[2:]
    chip = where[0]
    for n in range(count):
        near, far = sources[per_source * n], sources[per_source * n + 1 : per_source * (n + 1)]
        for j in range(slots):
            for part in range(2):
                start = pl.multiple_of(part * m + (chip ^ j) * rows, rows)
                for i in range(each):
                    if j == 0:
                        piece = near[i, part]
                    else:
                        piece = far[0][j - 1, i, part] if final else far[j - 1][i, part]
                    pol[n, i, pl.ds(start, rows), :] = piece.astype(pol.dtype)
    for n, o in enumerate(neighbours):
        both = jnp.concatenate([pol[n, i].astype(bf16) for i in range(each)], axis=1)
        product = jnp.dot(left_ref[o], both, preferred_element_type=f32).astype(bf16)
        for i in range(each):
            for part in range(2):
                left[i, :, (2 * n + part) * m : (2 * n + part + 1) * m] = product[
                    part * m : (part + 1) * m, i * m : (i + 1) * m
                ]
    for i in range(each):
        result = start_ref[i] if final else None
        for n, o in enumerate(neighbours):
            term = jnp.dot(
                left[i, :, 2 * n * m : 2 * (n + 1) * m],
                right_ref[o],
                preferred_element_type=f32,
            )
            result = term if result is None else result + term
        if not final:
            outs[0][i] = result
            continue
        result = result.astype(bf16)
        for j in range(slots):
            for part in range(2):
                outs[j][i, part] = result[j * rows : (j + 1) * rows, part * m : (part + 1) * m]


def screen(where, left_matrix, right_matrix, sources, slots, start=None):
    each, _, rows, m = sources[0].shape
    count = 1 if start is None else 2
    vmem = pl.BlockSpec(memory_space=pltpu.VMEM)
    flops = 16 * each * count * m * m * m
    moved = 4 * each * m * m * (count + 1) + 2 * (left_matrix.size + right_matrix.size)
    hold = bf16 if rows % 16 == 0 else f32
    final = start is not None
    if final:
        shapes = [out_like((each, 2, rows, m))] * slots
    else:
        shapes = [jax.ShapeDtypeStruct((each, m, 2 * m), f32)]
    operands = list(sources) + ([start] if final else [])
    found = pl.pallas_call(
        functools.partial(screen_kernel, slots, each, final),
        name="screen",
        out_shape=shapes,
        in_specs=[pl.BlockSpec(memory_space=pltpu.SMEM)] + [vmem] * (2 + len(operands)),
        out_specs=[vmem] * len(shapes),
        scratch_shapes=[
            pltpu.VMEM((count, each, 2 * m, m), hold),
            pltpu.VMEM((each, m, 2 * count * m), bf16),
        ],
        compiler_params=pltpu.CompilerParams(vmem_limit_bytes=44 * 2**20),
        cost_estimate=pl.CostEstimate(flops=flops, bytes_accessed=moved, transcendentals=0),
    )(where, left_matrix, right_matrix, *operands)
    return found if final else found[0]


def collect_kernel(slots, parts, where, *rest):
    count = slots * parts
    own, other = rest[:count], rest[count : count + parts]
    less, great = rest[count + parts :]
    core = where[1]
    for k in range(count):

        @pl.when(pl.program_id(0) == k)
        def _(k=k):
            h, j = divmod(k, slots)
            mine, theirs = own[k][0], other[h][j]
            less[:, 0] = jnp.where(core == 0, mine, theirs)
            great[:, 0] = jnp.where(core == 0, theirs, mine)


def collect(where, own, other, inner, m):
    parts, slots = len(own), len(own[0])
    rows = m // (slots * parts)
    if rows % 16:
        target = jnp.zeros((2, inner, 1, 2, m, m), bf16)
        for h in range(parts):
            for j in range(slots):
                pair = jnp.stack([own[h][j][0], other[h][j]])
                pair = jnp.where(where[1] == 0, pair, pair[::-1])[:, :, None]
                start = ((where[0] ^ j) * parts + h) * rows
                target = lax.dynamic_update_slice_in_dim(target, pair, start, axis=4)
        return target[0], target[1]
    flat = [piece for pieces in own for piece in pieces]
    vmem = [
        pl.BlockSpec((1, inner, 2, rows, m), lambda i, s: (0, 0, 0, 0, 0)) for _ in flat
    ] + [pl.BlockSpec((slots, inner, 2, rows, m), lambda i, s: (0, 0, 0, 0, 0)) for _ in other]
    shape = (inner, 1, 2, m, m)
    target = pl.BlockSpec(
        (inner, 1, 2, rows, m),
        lambda i, s: (0, 0, 0, (s[0] ^ lax.rem(i, slots)) * parts + lax.div(i, slots), 0),
    )
    return pl.pallas_call(
        functools.partial(collect_kernel, slots, parts),
        name="collect",
        out_shape=[out_like(shape)] * 2,
        grid_spec=pltpu.PrefetchScalarGridSpec(
            num_scalar_prefetch=1,
            grid=(parts * slots,),
            in_specs=vmem,
            out_specs=[target] * 2,
        ),
        compiler_params=pltpu.CompilerParams(vmem_limit_bytes=24 * 2**20),
        cost_estimate=pl.CostEstimate(
            flops=0, bytes_accessed=16 * inner * m * m, transcendentals=0
        ),
    )(where, *flat, *other)


def local(lesser_green, greater_green, coulomb_blocks):
    pieces = lax.axis_size("energy")
    slots = pieces // 2
    inner, _, _, m, _ = lesser_green.shape
    group = m // slots
    parts = 2 if group % 32 == 0 else 1
    rows = group // parts
    chunks = 2
    index = lax.axis_index("energy")
    where = jnp.stack([index // 2, index % 2, lax.axis_index("blk") % 2]).astype(jnp.int32)
    others = range(1, slots)

    both = (lesser_green, greater_green)
    found = cut(where, both, slots, list(others))
    greens = [swap(found[j - 1], 2 * j) for j in others]
    greens = [*cut(where, both, slots, [0]), *greens]
    left, right = coupling_matrices(where, coulomb_blocks[0], slots)

    middle = (slots + 1) // 2
    mine = [pack(group) for group in (greens[:middle], greens[middle:])]
    sib = [swap(piece, 1) for piece in mine]

    pol, near, after = [], [], []
    for c in range(chunks):
        found = correlate(where, mine, sib, chunks, c, after)
        after = [found[0]]
        pol.append([swap(found[j], 2 * j) for j in others])
        near.append([trade(found[0], 0), found[0], trade(found[0], 1)])

    starts = [screen(where, left, right, [near[c][1], *pol[c]], slots) for c in range(chunks)]

    screens = []
    after = [piece for triple in near for piece in (triple[0], triple[2])] + [near[-1][1]]
    for c in range(chunks):
        far = pack(pol[c], after=after)
        crossed = [near[c][0], trade(far, 0), near[c][2], trade(far, 1)]
        after = crossed[1::2] + starts
        found = screen(where, left, right, crossed, slots, starts[c])
        screens.append([found[0]] + [swap(found[j], 2 * j) for j in others])

    own, other = [], []
    for h in range(parts):
        found = self_energy(where, mine, sib, screens, h, rows)
        own.append([found[0]] + [swap(found[j], 2 * j) for j in others])
        other.append(swap(jnp.stack([piece[1] for piece in own[h]]), 1))
    return tuple(collect(where, own, other, inner, m))


def solution(mesh):
    return jax.shard_map(
        local,
        mesh=mesh,
        in_specs=(
            P("energy", "blk", None, None, None),
            P("energy", "blk", None, None, None),
            P("blk", None, None, None, None),
        ),
        out_specs=(P("energy", "blk", None, None, None), P("energy", "blk", None, None, None)),
        check_vma=False,
    )
```

```python
import functools
import math

import jax
import jax.numpy as jnp
from jax import lax
from jax.experimental import pallas as pl
from jax.experimental.pallas import tpu as pltpu
from jax.sharding import PartitionSpec as P

f32 = jnp.float32
bf16 = jnp.bfloat16


def swap(value, distance):
    count = lax.axis_size("energy")
    return lax.ppermute(value, "energy", [(i, i ^ distance) for i in range(count)])


def trade(value, first):
    count = lax.axis_size("blk")
    lows = range(first, count - 1, 2)
    return lax.ppermute(value, "blk", [(i, i + 1) for i in lows] + [(i + 1, i) for i in lows])


def row_block(rows):
    for size in (16, 8):
        if rows % size == 0:
            return size
    return rows


def out_like(shape):
    return jax.ShapeDtypeStruct(shape, bf16)


def vpu_cost(total, elements, moved):
    return pl.CostEstimate(
        flops=3 * total * (total + 1) * elements, bytes_accessed=2 * moved, transcendentals=0
    )


def tiles(rows, cols, body):
    lanes = 128 if cols % 128 == 0 else cols
    sub = 8 if rows % 8 == 0 else rows
    across = cols // lanes

    def step(t, carry):
        r = pl.multiple_of(lax.div(t, across) * sub, sub)
        c = pl.multiple_of(lax.rem(t, across) * lanes, lanes)
        body((pl.ds(r, sub), pl.ds(c, lanes)))
        return carry

    lax.fori_loop(0, (rows // sub) * across, step, 0)


def lag_of(total, slots, chunks, chunk, slot, i):
    return (chunks - 1 - chunk) * (total // chunks) + slot * (total // (chunks * slots)) + i


def load_greens(slots, inner, where, mine, sib, put):
    chip, core = where[0], where[1]
    for half, sources in ((core, mine), (1 - core, sib)):
        j = 0
        for source in sources:
            for k in range(source.shape[0]):
                for i in range(inner):
                    put((2 * (chip ^ j) + half) * inner + i, source, k, i)
                j += 1


def correlate_kernel(slots, inner, chunks, chunk, halves, extra, where, *rest):
    mine, sib = rest[:halves], rest[halves : 2 * halves][::-1]
    rest = rest[2 * halves + extra :]
    outs, (x_scr, y_scr, o_scr) = rest[:slots], rest[slots:]
    chip, core = where[0], where[1]
    total = 2 * inner * slots
    rows, cols = mine[0].shape[-2:]

    def put(e, source, k, i):
        a = source[k, i, core, 0].astype(f32)
        b = source[k, i, core, 1].astype(f32)
        x_scr[0, e], x_scr[1, e], x_scr[2, e] = a, b, a + b
        a = source[k, i, 1 - core, 0].astype(f32)
        b = source[k, i, 1 - core, 1].astype(f32)
        y_scr[0, e], y_scr[1, e], y_scr[2, e] = a, b, a - b

    load_greens(slots, inner, where, mine, sib, put)
    factor = -1.0 / math.sqrt(total)
    width = 4
    first_lag = lag_of(total, slots, chunks, chunk, 0, 0)
    last_lag = first_lag + total // chunks

    def body(at):
        for base in range(first_lag, last_lag, width):
            lags = range(base, min(base + width, last_lag))
            sums = {}
            window = {}
            for e in range(total - base):
                y = [y_scr[(p, e) + at] for p in range(3)]
                for w in lags:
                    if e + w >= total:
                        continue
                    if e + w not in window:
                        window[e + w] = [x_scr[(p, e + w) + at] for p in range(3)]
                    terms = [window[e + w][p] * y[p] for p in range(3)]
                    sums[w] = [s + t for s, t in zip(sums[w], terms)] if w in sums else terms
                window.pop(e + base, None)
            for w in lags:
                first, second, third = sums[w]
                o_scr[(w - first_lag, 0) + at] = factor * (first + second)
                o_scr[(w - first_lag, 1) + at] = factor * (third - first + second)

    tiles(rows, cols, body)
    each = 2 * inner // chunks
    for j in range(slots):
        for i in range(each):
            outs[j][i] = o_scr[(chip ^ j) * each + i].astype(bf16)


def correlate(where, mine, sib, chunks, chunk, after):
    _, inner, _, _, rows, cols = mine[0].shape
    slots = sum(piece.shape[0] for piece in mine)
    total = 2 * inner * slots
    each = 2 * inner // chunks
    block = row_block(rows)
    in_specs = [
        pl.BlockSpec((piece.shape[0], inner, 2, 2, block, cols), lambda r, s: (0, 0, 0, 0, r, 0))
        for piece in (*mine, *sib[::-1])
    ]
    out_spec = pl.BlockSpec((each, 2, block, cols), lambda r, s: (0, 0, r, 0))
    return pl.pallas_call(
        functools.partial(correlate_kernel, slots, inner, chunks, chunk, len(mine), len(after)),
        name="correlate",
        out_shape=[out_like((each, 2, rows, cols))] * slots,
        grid_spec=pltpu.PrefetchScalarGridSpec(
            num_scalar_prefetch=1,
            grid=(rows // block,),
            in_specs=in_specs + [pl.BlockSpec(memory_space=pl.ANY)] * len(after),
            out_specs=[out_spec] * slots,
            scratch_shapes=[
                pltpu.VMEM((3, total, block, cols), f32),
                pltpu.VMEM((3, total, block, cols), f32),
                pltpu.VMEM((total // chunks, 2, block, cols), f32),
            ],
        ),
        compiler_params=pltpu.CompilerParams(vmem_limit_bytes=32 * 2**20),
        cost_estimate=vpu_cost(total, rows * cols // chunks, 4 * total * rows * cols),
    )(where, *mine, *sib[::-1], *after)


def sigma_kernel(slots, inner, chunks, halves, where, *rest):
    mine, sib = rest[:halves], rest[halves : 2 * halves][::-1]
    rest = rest[2 * halves :]
    screens = rest[: slots * chunks]
    outs = rest[slots * chunks : slots * chunks + slots]
    x_scr, y_scr, o_scr = rest[slots * chunks + slots :]
    chip, core = where[0], where[1]
    total = 2 * inner * slots
    rows, cols = mine[0].shape[-2:]
    each = 2 * inner // chunks

    def put(e, source, k, i):
        a = source[k, i, 0, 0].astype(f32)
        b = source[k, i, 0, 1].astype(f32)
        x_scr[0, e], x_scr[1, e], x_scr[2, e] = a, b, a + b

    load_greens(slots, inner, where, mine, sib, put)
    for j in range(slots):
        for chunk in range(chunks):
            source = screens[chunk * slots + j]
            for i in range(each):
                w = lag_of(total, slots, chunks, chunk, chip ^ j, i)
                a = source[i, 0].astype(f32)
                b = source[i, 1].astype(f32)
                y_scr[0, w], y_scr[1, w], y_scr[2, w] = a, b, a + b
    factor = 1.0 / math.sqrt(total)
    width = 4

    def body(at):
        for base in range(0, total, width):
            energies = range(base, min(base + width, total))
            sums = {}
            window = {}
            for w in range(min(base + width, total)):
                y = [y_scr[(p, w) + at] for p in range(3)]
                for e in energies:
                    if e < w:
                        continue
                    if e - w not in window:
                        window[e - w] = [x_scr[(p, e - w) + at] for p in range(3)]
                    terms = [window[e - w][p] * y[p] for p in range(3)]
                    sums[e] = [s + t for s, t in zip(sums[e], terms)] if e in sums else terms
                window.pop(base + width - 1 - w, None)
            for e in energies:
                first, second, third = sums[e]
                o_scr[(e, 0) + at] = factor * (first - second)
                o_scr[(e, 1) + at] = factor * (third - first - second)

    tiles(rows, cols, body)
    for j in range(slots):
        for side in range(2):
            half = core if side == 0 else 1 - core
            for i in range(inner):
                e = (2 * (chip ^ j) + half) * inner + i
                outs[j][side, i] = o_scr[e].astype(bf16)


def self_energy(where, mine, sib, screens, part, rows):
    _, inner, _, _, _, cols = mine[0].shape
    slots = sum(piece.shape[0] for piece in mine)
    chunks = len(screens)
    flat = [piece for chunk in screens for piece in chunk]
    each = flat[0].shape[0]
    total = 2 * inner * slots
    block = row_block(rows)
    steps = rows // block
    green_specs = [
        pl.BlockSpec(
            (piece.shape[0], inner, 1, 2, block, cols),
            lambda r, s: (0, 0, s[1], 0, part * steps + r, 0),
        )
        for piece in (*mine, *sib[::-1])
    ]
    screen_spec = pl.BlockSpec((each, 2, block, cols), lambda r, s: (0, 0, part * steps + r, 0))
    out_spec = pl.BlockSpec((2, inner, 2, block, cols), lambda r, s: (0, 0, 0, r, 0))
    return pl.pallas_call(
        functools.partial(sigma_kernel, slots, inner, chunks, len(mine)),
        name="sigma",
        out_shape=[out_like((2, inner, 2, rows, cols))] * slots,
        grid_spec=pltpu.PrefetchScalarGridSpec(
            num_scalar_prefetch=1,
            grid=(steps,),
            in_specs=green_specs + [screen_spec] * len(flat),
            out_specs=[out_spec] * slots,
            scratch_shapes=[
                pltpu.VMEM((3, total, block, cols), f32),
                pltpu.VMEM((3, total, block, cols), f32),
                pltpu.VMEM((total, 2, block, cols), f32),
            ],
        ),
        compiler_params=pltpu.CompilerParams(vmem_limit_bytes=32 * 2**20),
        cost_estimate=vpu_cost(total, rows * cols, 6 * total * rows * cols),
    )(where, *mine, *sib[::-1], *flat)


def cut_kernel(count, where, *rest):
    for k in range(count):
        for kind in range(2):
            rest[2 * count + k][0, kind] = rest[kind * count + k][0, 0]


def cut(where, greens, slots, wanted):
    inner, _, _, m, _ = greens[0].shape
    group = m // slots
    count = len(wanted)
    if group % 16:
        return [
            jnp.stack(
                [
                    lax.dynamic_slice_in_dim(g[:, 0], (where[0] ^ j) * group, group, axis=2)
                    for g in greens
                ],
                axis=1,
            )
            for j in wanted
        ]

    def block(j):
        return pl.BlockSpec((1, 1, 2, group, m), lambda e, s: (e, 0, 0, s[0] ^ j, 0))

    return pl.pallas_call(
        functools.partial(cut_kernel, count),
        name="cut_rows",
        out_shape=[out_like((inner, 2, 2, group, m))] * count,
        grid_spec=pltpu.PrefetchScalarGridSpec(
            num_scalar_prefetch=1,
            grid=(inner,),
            in_specs=[block(j) for j in wanted] * 2,
            out_specs=[pl.BlockSpec((1, 2, 2, group, m), lambda e, s: (e, 0, 0, 0, 0))] * count,
        ),
        compiler_params=pltpu.CompilerParams(vmem_limit_bytes=56 * 2**20),
        cost_estimate=pl.CostEstimate(flops=0, bytes_accessed=16 * inner * count * group * m, transcendentals=0),
    )(where, *([greens[0]] * count), *([greens[1]] * count))


def matrices_kernel(slots, where, coupling, left, right, *held):
    count, _, m, _ = coupling.shape
    group = m // slots
    chip = where[0]
    for o in range(count):
        real, imag = coupling[o, 0].astype(f32), coupling[o, 1].astype(f32)
        real_t, imag_t = real.T.astype(bf16), imag.T.astype(bf16)
        right[o, :m, :m] = real_t
        right[o, :m, m:] = -imag_t
        right[o, m:, :m] = imag_t
        right[o, m:, m:] = real_t
        if held:
            held[0][0], held[0][1] = real, imag
            source = held[0]
        else:
            source = coupling.at[o]
        for j in range(slots):
            start = pl.multiple_of((chip ^ j) * group, group)
            real = source[0, pl.ds(start, group), :].astype(bf16)
            imag = source[1, pl.ds(start, group), :].astype(bf16)
            low = j * group
            left[o, low : low + group, :m] = real
            left[o, low : low + group, m:] = -imag
            left[o, m + low : m + low + group, :m] = imag
            left[o, m + low : m + low + group, m:] = real


def coupling_matrices(where, coulomb, slots):
    count, _, m, _ = coulomb.shape
    vmem = pl.BlockSpec(memory_space=pltpu.VMEM)
    held = [] if (m // slots) % 16 == 0 else [pltpu.VMEM((2, m, m), f32)]
    return pl.pallas_call(
        functools.partial(matrices_kernel, slots),
        name="coupling",
        out_shape=[out_like((count, 2 * m, 2 * m))] * 2,
        in_specs=[pl.BlockSpec(memory_space=pltpu.SMEM), vmem],
        out_specs=[vmem, vmem],
        scratch_shapes=held,
        compiler_params=pltpu.CompilerParams(vmem_limit_bytes=24 * 2**20),
        cost_estimate=pl.CostEstimate(flops=0, bytes_accessed=20 * coulomb.size, transcendentals=0),
    )(where, coulomb)


def pack_kernel(pieces, extra, *refs):
    for k in range(pieces):
        refs[pieces + extra][k] = refs[k][...]


def pack(pieces, block=None, index=None, after=()):
    count = len(pieces)
    block = block or pieces[0].shape
    index = index or (0,) * len(block)
    size = math.prod(block)
    return pl.pallas_call(
        functools.partial(pack_kernel, count, len(after)),
        name="pack",
        out_shape=out_like((count,) + block),
        grid=(1,),
        in_specs=[pl.BlockSpec(block, lambda i: index)] * count
        + [pl.BlockSpec(memory_space=pl.ANY)] * len(after),
        out_specs=pl.BlockSpec((count,) + block, lambda i: (0,) * (1 + len(block))),
        compiler_params=pltpu.CompilerParams(vmem_limit_bytes=16 * 2**20),
        cost_estimate=pl.CostEstimate(flops=0, bytes_accessed=4 * count * size, transcendentals=0),
    )(*pieces, *after)


def screen_kernel(slots, each, final, where, left_ref, right_ref, *rest):
    odd = where[2]
    neighbours = (2 - 2 * odd, 2 * odd) if final else (1,)
    count = len(neighbours)
    per_source = 2 if final else slots
    sources, rest = rest[: per_source * count], rest[per_source * count :]
    if final:
        start_ref, rest = rest[0], rest[1:]
    outs, (pol, left) = rest[:-2], rest[-2:]
    rows, m = sources[0].shape[2:]
    chip = where[0]
    for n in range(count):
        near, far = sources[per_source * n], sources[per_source * n + 1 : per_source * (n + 1)]
        for j in range(slots):
            for part in range(2):
                start = pl.multiple_of(part * m + (chip ^ j) * rows, rows)
                for i in range(each):
                    if j == 0:
                        piece = near[i, part]
                    else:
                        piece = far[0][j - 1, i, part] if final else far[j - 1][i, part]
                    pol[n, i, pl.ds(start, rows), :] = piece.astype(pol.dtype)
    for n, o in enumerate(neighbours):
        both = jnp.concatenate([pol[n, i].astype(bf16) for i in range(each)], axis=1)
        product = jnp.dot(left_ref[o], both, preferred_element_type=f32).astype(bf16)
        for i in range(each):
            for part in range(2):
                left[i, :, (2 * n + part) * m : (2 * n + part + 1) * m] = product[
                    part * m : (part + 1) * m, i * m : (i + 1) * m
                ]
    for i in range(each):
        result = start_ref[i] if final else None
        for n, o in enumerate(neighbours):
            term = jnp.dot(
                left[i, :, 2 * n * m : 2 * (n + 1) * m],
                right_ref[o],
                preferred_element_type=f32,
            )
            result = term if result is None else result + term
        if not final:
            outs[0][i] = result
            continue
        result = result.astype(bf16)
        for j in range(slots):
            for part in range(2):
                outs[j][i, part] = result[j * rows : (j + 1) * rows, part * m : (part + 1) * m]


def screen(where, left_matrix, right_matrix, sources, slots, start=None):
    each, _, rows, m = sources[0].shape
    count = 1 if start is None else 2
    vmem = pl.BlockSpec(memory_space=pltpu.VMEM)
    flops = 16 * each * count * m * m * m
    moved = 4 * each * m * m * (count + 1) + 2 * (left_matrix.size + right_matrix.size)
    hold = bf16 if rows % 16 == 0 else f32
    final = start is not None
    if final:
        shapes = [out_like((each, 2, rows, m))] * slots
    else:
        shapes = [jax.ShapeDtypeStruct((each, m, 2 * m), f32)]
    operands = list(sources) + ([start] if final else [])
    found = pl.pallas_call(
        functools.partial(screen_kernel, slots, each, final),
        name="screen",
        out_shape=shapes,
        in_specs=[pl.BlockSpec(memory_space=pltpu.SMEM)] + [vmem] * (2 + len(operands)),
        out_specs=[vmem] * len(shapes),
        scratch_shapes=[
            pltpu.VMEM((count, each, 2 * m, m), hold),
            pltpu.VMEM((each, m, 2 * count * m), bf16),
        ],
        compiler_params=pltpu.CompilerParams(vmem_limit_bytes=44 * 2**20),
        cost_estimate=pl.CostEstimate(flops=flops, bytes_accessed=moved, transcendentals=0),
    )(where, left_matrix, right_matrix, *operands)
    return found if final else found[0]


def collect_kernel(slots, into, where, *rest):
    own, other = rest[:slots], rest[slots]
    less, great = rest[slots + 1 + into :]
    core = where[1]
    for j in range(slots):

        @pl.when(pl.program_id(0) == j)
        def _(j=j):
            mine, theirs = own[j][0], other[j]
            less[:, 0] = jnp.where(core == 0, mine, theirs)
            great[:, 0] = jnp.where(core == 0, theirs, mine)


def collect(where, own, other, part, parts, into):
    slots = len(own)
    _, inner, _, rows, m = own[0].shape
    shape = (inner, 1, 2, m, m)
    if rows % 16:
        target = jnp.stack(into) if into else jnp.zeros((2,) + shape, bf16)
        for j in range(slots):
            pair = jnp.stack([own[j][0], other[j]])
            pair = jnp.where(where[1] == 0, pair, pair[::-1])[:, :, None]
            start = ((where[0] ^ j) * parts + part) * rows
            target = lax.dynamic_update_slice_in_dim(target, pair, start, axis=4)
        return [target[0], target[1]]
    before = list(into or [])
    specs = [pl.BlockSpec((1, inner, 2, rows, m), lambda i, s: (0, 0, 0, 0, 0))] * slots
    specs += [pl.BlockSpec((slots, inner, 2, rows, m), lambda i, s: (0, 0, 0, 0, 0))]
    specs += [pl.BlockSpec(memory_space=pl.ANY)] * len(before)
    target = pl.BlockSpec(
        (inner, 1, 2, rows, m), lambda i, s: (0, 0, 0, (s[0] ^ i) * parts + part, 0)
    )
    return pl.pallas_call(
        functools.partial(collect_kernel, slots, len(before)),
        name="collect",
        out_shape=[out_like(shape)] * 2,
        grid_spec=pltpu.PrefetchScalarGridSpec(
            num_scalar_prefetch=1,
            grid=(slots,),
            in_specs=specs,
            out_specs=[target] * 2,
        ),
        input_output_aliases={slots + 2 + k: k for k in range(len(before))},
        compiler_params=pltpu.CompilerParams(vmem_limit_bytes=24 * 2**20),
        cost_estimate=pl.CostEstimate(
            flops=0, bytes_accessed=16 * inner * m * slots * rows, transcendentals=0
        ),
    )(where, *own, other, *before)


def local(lesser_green, greater_green, coulomb_blocks):
    pieces = lax.axis_size("energy")
    slots = pieces // 2
    inner, _, _, m, _ = lesser_green.shape
    group = m // slots
    parts = 2 if group % 32 == 0 else 1
    rows = group // parts
    chunks = 2
    index = lax.axis_index("energy")
    where = jnp.stack([index // 2, index % 2, lax.axis_index("blk") % 2]).astype(jnp.int32)
    others = range(1, slots)

    both = (lesser_green, greater_green)
    found = cut(where, both, slots, list(others))
    greens = [swap(found[j - 1], 2 * j) for j in others]
    greens = [*cut(where, both, slots, [0]), *greens]
    left, right = coupling_matrices(where, coulomb_blocks[0], slots)

    middle = (slots + 1) // 2
    mine = [pack(group) for group in (greens[:middle], greens[middle:])]
    sib = [swap(piece, 1) for piece in mine]

    pol, near, after = [], [], []
    for c in range(chunks):
        found = correlate(where, mine, sib, chunks, c, after)
        after = [found[0]]
        pol.append([swap(found[j], 2 * j) for j in others])
        near.append([trade(found[0], 0), found[0], trade(found[0], 1)])

    starts = [screen(where, left, right, [near[c][1], *pol[c]], slots) for c in range(chunks)]

    screens = []
    after = [piece for triple in near for piece in (triple[0], triple[2])] + [near[-1][1]]
    for c in range(chunks):
        far = pack(pol[c], after=after)
        crossed = [near[c][0], trade(far, 0), near[c][2], trade(far, 1)]
        after = [far, starts[0]]
        found = screen(where, left, right, crossed, slots, starts[c])
        screens.append([found[0]] + [swap(found[j], 2 * j) for j in others])

    into = None
    for h in range(parts):
        found = self_energy(where, mine, sib, screens, h, rows)
        own = [found[0]] + [swap(found[j], 2 * j) for j in others]
        other = swap(jnp.stack([piece[1] for piece in own]), 1)
        into = collect(where, own, other, h, parts, into)
    return tuple(into)


def solution(mesh):
    return jax.shard_map(
        local,
        mesh=mesh,
        in_specs=(
            P("energy", "blk", None, None, None),
            P("energy", "blk", None, None, None),
            P("blk", None, None, None, None),
        ),
        out_specs=(P("energy", "blk", None, None, None), P("energy", "blk", None, None, None)),
        check_vma=False,
    )
```

```python
import functools
import math

import jax
import jax.numpy as jnp
from jax import lax
from jax.experimental import pallas as pl
from jax.experimental.pallas import tpu as pltpu
from jax.sharding import PartitionSpec as P

f32 = jnp.float32
bf16 = jnp.bfloat16


def swap(value, distance):
    count = lax.axis_size("energy")
    return lax.ppermute(value, "energy", [(i, i ^ distance) for i in range(count)])


def trade(value, first):
    count = lax.axis_size("blk")
    lows = range(first, count - 1, 2)
    return lax.ppermute(value, "blk", [(i, i + 1) for i in lows] + [(i + 1, i) for i in lows])


def row_block(rows):
    for size in (16, 8):
        if rows % size == 0:
            return size
    return rows


def out_like(shape):
    return jax.ShapeDtypeStruct(shape, bf16)


def vpu_cost(total, elements, moved):
    return pl.CostEstimate(
        flops=3 * total * (total + 1) * elements, bytes_accessed=2 * moved, transcendentals=0
    )


def tiles(rows, cols, body):
    lanes = 128 if cols % 128 == 0 else cols
    sub = 8 if rows % 8 == 0 else rows
    across = cols // lanes

    def step(t, carry):
        r = pl.multiple_of(lax.div(t, across) * sub, sub)
        c = pl.multiple_of(lax.rem(t, across) * lanes, lanes)
        body((pl.ds(r, sub), pl.ds(c, lanes)))
        return carry

    lax.fori_loop(0, (rows // sub) * across, step, 0)


def lag_of(total, slots, chunks, chunk, slot, i):
    return (chunks - 1 - chunk) * (total // chunks) + slot * (total // (chunks * slots)) + i


def load_greens(slots, inner, where, mine, sib, put):
    chip, core = where[0], where[1]
    for half, sources in ((core, mine), (1 - core, sib)):
        j = 0
        for source in sources:
            for k in range(source.shape[0]):
                for i in range(inner):
                    put((2 * (chip ^ j) + half) * inner + i, source, k, i)
                j += 1


def correlate_kernel(slots, inner, chunks, chunk, halves, extra, where, *rest):
    mine, sib = rest[:halves], rest[halves : 2 * halves][::-1]
    rest = rest[2 * halves + extra :]
    outs, (x_scr, y_scr, o_scr) = rest[:slots], rest[slots:]
    chip, core = where[0], where[1]
    total = 2 * inner * slots
    rows, cols = mine[0].shape[-2:]

    def put(e, source, k, i):
        a = source[k, i, core, 0].astype(f32)
        b = source[k, i, core, 1].astype(f32)
        x_scr[0, e], x_scr[1, e], x_scr[2, e] = a, b, a + b
        a = source[k, i, 1 - core, 0].astype(f32)
        b = source[k, i, 1 - core, 1].astype(f32)
        y_scr[0, e], y_scr[1, e], y_scr[2, e] = a, b, a - b

    load_greens(slots, inner, where, mine, sib, put)
    factor = -1.0 / math.sqrt(total)
    width = 4
    first_lag = lag_of(total, slots, chunks, chunk, 0, 0)
    last_lag = first_lag + total // chunks

    def body(at):
        for base in range(first_lag, last_lag, width):
            lags = range(base, min(base + width, last_lag))
            sums = {}
            window = {}
            for e in range(total - base):
                y = [y_scr[(p, e) + at] for p in range(3)]
                for w in lags:
                    if e + w >= total:
                        continue
                    if e + w not in window:
                        window[e + w] = [x_scr[(p, e + w) + at] for p in range(3)]
                    terms = [window[e + w][p] * y[p] for p in range(3)]
                    sums[w] = [s + t for s, t in zip(sums[w], terms)] if w in sums else terms
                window.pop(e + base, None)
            for w in lags:
                first, second, third = sums[w]
                o_scr[(w - first_lag, 0) + at] = factor * (first + second)
                o_scr[(w - first_lag, 1) + at] = factor * (third - first + second)

    tiles(rows, cols, body)
    each = 2 * inner // chunks
    for j in range(slots):
        for i in range(each):
            outs[j][i] = o_scr[(chip ^ j) * each + i].astype(bf16)


def correlate(where, mine, sib, chunks, chunk, after):
    _, inner, _, _, rows, cols = mine[0].shape
    slots = sum(piece.shape[0] for piece in mine)
    total = 2 * inner * slots
    each = 2 * inner // chunks
    block = row_block(rows)
    in_specs = [
        pl.BlockSpec((piece.shape[0], inner, 2, 2, block, cols), lambda r, s: (0, 0, 0, 0, r, 0))
        for piece in (*mine, *sib[::-1])
    ]
    out_spec = pl.BlockSpec((each, 2, block, cols), lambda r, s: (0, 0, r, 0))
    return pl.pallas_call(
        functools.partial(correlate_kernel, slots, inner, chunks, chunk, len(mine), len(after)),
        name="correlate",
        out_shape=[out_like((each, 2, rows, cols))] * slots,
        grid_spec=pltpu.PrefetchScalarGridSpec(
            num_scalar_prefetch=1,
            grid=(rows // block,),
            in_specs=in_specs + [pl.BlockSpec(memory_space=pl.ANY)] * len(after),
            out_specs=[out_spec] * slots,
            scratch_shapes=[
                pltpu.VMEM((3, total, block, cols), f32),
                pltpu.VMEM((3, total, block, cols), f32),
                pltpu.VMEM((total // chunks, 2, block, cols), f32),
            ],
        ),
        compiler_params=pltpu.CompilerParams(vmem_limit_bytes=16 * 2**20),
        cost_estimate=vpu_cost(total, rows * cols // chunks, 4 * total * rows * cols),
    )(where, *mine, *sib[::-1], *after)


def sigma_kernel(slots, inner, chunks, halves, where, *rest):
    mine, sib = rest[:halves], rest[halves : 2 * halves][::-1]
    rest = rest[2 * halves :]
    screens = rest[: slots * chunks]
    outs = rest[slots * chunks : slots * chunks + slots]
    x_scr, y_scr, o_scr = rest[slots * chunks + slots :]
    chip, core = where[0], where[1]
    total = 2 * inner * slots
    rows, cols = mine[0].shape[-2:]
    each = 2 * inner // chunks

    def put(e, source, k, i):
        a = source[k, i, 0, 0].astype(f32)
        b = source[k, i, 0, 1].astype(f32)
        x_scr[0, e], x_scr[1, e], x_scr[2, e] = a, b, a + b

    load_greens(slots, inner, where, mine, sib, put)
    for j in range(slots):
        for chunk in range(chunks):
            source = screens[chunk * slots + j]
            for i in range(each):
                w = lag_of(total, slots, chunks, chunk, chip ^ j, i)
                a = source[i, 0].astype(f32)
                b = source[i, 1].astype(f32)
                y_scr[0, w], y_scr[1, w], y_scr[2, w] = a, b, a + b
    factor = 1.0 / math.sqrt(total)
    width = 4

    def body(at):
        for base in range(0, total, width):
            energies = range(base, min(base + width, total))
            sums = {}
            window = {}
            for w in range(min(base + width, total)):
                y = [y_scr[(p, w) + at] for p in range(3)]
                for e in energies:
                    if e < w:
                        continue
                    if e - w not in window:
                        window[e - w] = [x_scr[(p, e - w) + at] for p in range(3)]
                    terms = [window[e - w][p] * y[p] for p in range(3)]
                    sums[e] = [s + t for s, t in zip(sums[e], terms)] if e in sums else terms
                window.pop(base + width - 1 - w, None)
            for e in energies:
                first, second, third = sums[e]
                o_scr[(e, 0) + at] = factor * (first - second)
                o_scr[(e, 1) + at] = factor * (third - first - second)

    tiles(rows, cols, body)
    for j in range(slots):
        for side in range(2):
            half = core if side == 0 else 1 - core
            for i in range(inner):
                e = (2 * (chip ^ j) + half) * inner + i
                outs[j][side, i] = o_scr[e].astype(bf16)


def self_energy(where, mine, sib, screens, part, rows):
    _, inner, _, _, _, cols = mine[0].shape
    slots = sum(piece.shape[0] for piece in mine)
    chunks = len(screens)
    flat = [piece for chunk in screens for piece in chunk]
    each = flat[0].shape[0]
    total = 2 * inner * slots
    block = row_block(rows)
    steps = rows // block
    green_specs = [
        pl.BlockSpec(
            (piece.shape[0], inner, 1, 2, block, cols),
            lambda r, s: (0, 0, s[1], 0, part * steps + r, 0),
        )
        for piece in (*mine, *sib[::-1])
    ]
    screen_spec = pl.BlockSpec((each, 2, block, cols), lambda r, s: (0, 0, part * steps + r, 0))
    out_spec = pl.BlockSpec((2, inner, 2, block, cols), lambda r, s: (0, 0, 0, r, 0))
    return pl.pallas_call(
        functools.partial(sigma_kernel, slots, inner, chunks, len(mine)),
        name="sigma",
        out_shape=[out_like((2, inner, 2, rows, cols))] * slots,
        grid_spec=pltpu.PrefetchScalarGridSpec(
            num_scalar_prefetch=1,
            grid=(steps,),
            in_specs=green_specs + [screen_spec] * len(flat),
            out_specs=[out_spec] * slots,
            scratch_shapes=[
                pltpu.VMEM((3, total, block, cols), f32),
                pltpu.VMEM((3, total, block, cols), f32),
                pltpu.VMEM((total, 2, block, cols), f32),
            ],
        ),
        compiler_params=pltpu.CompilerParams(vmem_limit_bytes=16 * 2**20),
        cost_estimate=vpu_cost(total, rows * cols, 6 * total * rows * cols),
    )(where, *mine, *sib[::-1], *flat)


def cut_kernel(count, where, *rest):
    for k in range(count):
        for kind in range(2):
            rest[2 * count + k][0, kind] = rest[kind * count + k][0, 0]


def cut(where, greens, slots, wanted):
    inner, _, _, m, _ = greens[0].shape
    group = m // slots
    count = len(wanted)
    if group % 16:
        return [
            jnp.stack(
                [
                    lax.dynamic_slice_in_dim(g[:, 0], (where[0] ^ j) * group, group, axis=2)
                    for g in greens
                ],
                axis=1,
            )
            for j in wanted
        ]

    def block(j):
        return pl.BlockSpec((1, 1, 2, group, m), lambda e, s: (e, 0, 0, s[0] ^ j, 0))

    return pl.pallas_call(
        functools.partial(cut_kernel, count),
        name="cut_rows",
        out_shape=[out_like((inner, 2, 2, group, m))] * count,
        grid_spec=pltpu.PrefetchScalarGridSpec(
            num_scalar_prefetch=1,
            grid=(inner,),
            in_specs=[block(j) for j in wanted] * 2,
            out_specs=[pl.BlockSpec((1, 2, 2, group, m), lambda e, s: (e, 0, 0, 0, 0))] * count,
        ),
        compiler_params=pltpu.CompilerParams(vmem_limit_bytes=56 * 2**20),
        cost_estimate=pl.CostEstimate(flops=0, bytes_accessed=16 * inner * count * group * m, transcendentals=0),
    )(where, *([greens[0]] * count), *([greens[1]] * count))


def matrices_kernel(slots, where, coupling, left, right, *held):
    count, _, m, _ = coupling.shape
    group = m // slots
    chip = where[0]
    for o in range(count):
        real, imag = coupling[o, 0].astype(f32), coupling[o, 1].astype(f32)
        real_t, imag_t = real.T.astype(bf16), imag.T.astype(bf16)
        right[o, :m, :m] = real_t
        right[o, :m, m:] = -imag_t
        right[o, m:, :m] = imag_t
        right[o, m:, m:] = real_t
        if held:
            held[0][0], held[0][1] = real, imag
            source = held[0]
        else:
            source = coupling.at[o]
        for j in range(slots):
            start = pl.multiple_of((chip ^ j) * group, group)
            real = source[0, pl.ds(start, group), :].astype(bf16)
            imag = source[1, pl.ds(start, group), :].astype(bf16)
            low = j * group
            left[o, low : low + group, :m] = real
            left[o, low : low + group, m:] = -imag
            left[o, m + low : m + low + group, :m] = imag
            left[o, m + low : m + low + group, m:] = real


def coupling_matrices(where, coulomb, slots):
    count, _, m, _ = coulomb.shape
    vmem = pl.BlockSpec(memory_space=pltpu.VMEM)
    held = [] if (m // slots) % 16 == 0 else [pltpu.VMEM((2, m, m), f32)]
    return pl.pallas_call(
        functools.partial(matrices_kernel, slots),
        name="coupling",
        out_shape=[out_like((count, 2 * m, 2 * m))] * 2,
        in_specs=[pl.BlockSpec(memory_space=pltpu.SMEM), vmem],
        out_specs=[vmem, vmem],
        scratch_shapes=held,
        compiler_params=pltpu.CompilerParams(vmem_limit_bytes=20 * 2**20),
        cost_estimate=pl.CostEstimate(flops=0, bytes_accessed=20 * coulomb.size, transcendentals=0),
    )(where, coulomb)


def pack_kernel(pieces, extra, *refs):
    for k in range(pieces):
        refs[pieces + extra][k] = refs[k][...]


def pack(pieces, block=None, index=None, after=()):
    count = len(pieces)
    block = block or pieces[0].shape
    index = index or (0,) * len(block)
    size = math.prod(block)
    return pl.pallas_call(
        functools.partial(pack_kernel, count, len(after)),
        name="pack",
        out_shape=out_like((count,) + block),
        grid=(1,),
        in_specs=[pl.BlockSpec(block, lambda i: index)] * count
        + [pl.BlockSpec(memory_space=pl.ANY)] * len(after),
        out_specs=pl.BlockSpec((count,) + block, lambda i: (0,) * (1 + len(block))),
        compiler_params=pltpu.CompilerParams(vmem_limit_bytes=16 * 2**20),
        cost_estimate=pl.CostEstimate(flops=0, bytes_accessed=4 * count * size, transcendentals=0),
    )(*pieces, *after)


def screen_kernel(slots, each, final, where, left_ref, right_ref, *rest):
    odd = where[2]
    neighbours = (2 - 2 * odd, 2 * odd) if final else (1,)
    count = len(neighbours)
    per_source = 2 if final else slots
    sources, rest = rest[: per_source * count], rest[per_source * count :]
    if final:
        start_ref, rest = rest[0], rest[1:]
    outs, (pol, left) = rest[:-2], rest[-2:]
    rows, m = sources[0].shape[2:]
    chip = where[0]
    for n in range(count):
        near, far = sources[per_source * n], sources[per_source * n + 1 : per_source * (n + 1)]
        for j in range(slots):
            for part in range(2):
                start = pl.multiple_of(part * m + (chip ^ j) * rows, rows)
                for i in range(each):
                    if j == 0:
                        piece = near[i, part]
                    else:
                        piece = far[0][j - 1, i, part] if final else far[j - 1][i, part]
                    pol[n, i, pl.ds(start, rows), :] = piece.astype(pol.dtype)
    for n, o in enumerate(neighbours):
        both = jnp.concatenate([pol[n, i].astype(bf16) for i in range(each)], axis=1)
        product = jnp.dot(left_ref[o], both, preferred_element_type=f32).astype(bf16)
        for i in range(each):
            for part in range(2):
                left[i, :, (2 * n + part) * m : (2 * n + part + 1) * m] = product[
                    part * m : (part + 1) * m, i * m : (i + 1) * m
                ]
    for i in range(each):
        result = start_ref[i] if final else None
        for n, o in enumerate(neighbours):
            term = jnp.dot(
                left[i, :, 2 * n * m : 2 * (n + 1) * m],
                right_ref[o],
                preferred_element_type=f32,
            )
            result = term if result is None else result + term
        if not final:
            outs[0][i] = result
            continue
        result = result.astype(bf16)
        for j in range(slots):
            for part in range(2):
                outs[j][i, part] = result[j * rows : (j + 1) * rows, part * m : (part + 1) * m]


def screen(where, left_matrix, right_matrix, sources, slots, start=None):
    each, _, rows, m = sources[0].shape
    count = 1 if start is None else 2
    vmem = pl.BlockSpec(memory_space=pltpu.VMEM)
    flops = 16 * each * count * m * m * m
    moved = 4 * each * m * m * (count + 1) + 2 * (left_matrix.size + right_matrix.size)
    hold = bf16 if rows % 16 == 0 else f32
    final = start is not None
    if final:
        shapes = [out_like((each, 2, rows, m))] * slots
    else:
        shapes = [jax.ShapeDtypeStruct((each, m, 2 * m), f32)]
    operands = list(sources) + ([start] if final else [])
    found = pl.pallas_call(
        functools.partial(screen_kernel, slots, each, final),
        name="screen",
        out_shape=shapes,
        in_specs=[pl.BlockSpec(memory_space=pltpu.SMEM)] + [vmem] * (2 + len(operands)),
        out_specs=[vmem] * len(shapes),
        scratch_shapes=[
            pltpu.VMEM((count, each, 2 * m, m), hold),
            pltpu.VMEM((each, m, 2 * count * m), bf16),
        ],
        compiler_params=pltpu.CompilerParams(vmem_limit_bytes=28 * 2**20),
        cost_estimate=pl.CostEstimate(flops=flops, bytes_accessed=moved, transcendentals=0),
    )(where, left_matrix, right_matrix, *operands)
    return found if final else found[0]


def collect_kernel(slots, into, where, *rest):
    own, other = rest[:slots], rest[slots]
    less, great = rest[slots + 1 + into :]
    core = where[1]
    for j in range(slots):

        @pl.when(pl.program_id(0) == j)
        def _(j=j):
            mine, theirs = own[j][0], other[j]
            less[:, 0] = jnp.where(core == 0, mine, theirs)
            great[:, 0] = jnp.where(core == 0, theirs, mine)


def collect(where, own, other, part, parts, into):
    slots = len(own)
    _, inner, _, rows, m = own[0].shape
    shape = (inner, 1, 2, m, m)
    if rows % 16:
        target = jnp.stack(into) if into else jnp.zeros((2,) + shape, bf16)
        for j in range(slots):
            pair = jnp.stack([own[j][0], other[j]])
            pair = jnp.where(where[1] == 0, pair, pair[::-1])[:, :, None]
            start = ((where[0] ^ j) * parts + part) * rows
            target = lax.dynamic_update_slice_in_dim(target, pair, start, axis=4)
        return [target[0], target[1]]
    before = list(into or [])
    specs = [pl.BlockSpec((1, inner, 2, rows, m), lambda i, s: (0, 0, 0, 0, 0))] * slots
    specs += [pl.BlockSpec((slots, inner, 2, rows, m), lambda i, s: (0, 0, 0, 0, 0))]
    specs += [pl.BlockSpec(memory_space=pl.ANY)] * len(before)
    target = pl.BlockSpec(
        (inner, 1, 2, rows, m), lambda i, s: (0, 0, 0, (s[0] ^ i) * parts + part, 0)
    )
    return pl.pallas_call(
        functools.partial(collect_kernel, slots, len(before)),
        name="collect",
        out_shape=[out_like(shape)] * 2,
        grid_spec=pltpu.PrefetchScalarGridSpec(
            num_scalar_prefetch=1,
            grid=(slots,),
            in_specs=specs,
            out_specs=[target] * 2,
        ),
        input_output_aliases={slots + 2 + k: k for k in range(len(before))},
        compiler_params=pltpu.CompilerParams(vmem_limit_bytes=20 * 2**20),
        cost_estimate=pl.CostEstimate(
            flops=0, bytes_accessed=16 * inner * m * slots * rows, transcendentals=0
        ),
    )(where, *own, other, *before)


def local(lesser_green, greater_green, coulomb_blocks):
    pieces = lax.axis_size("energy")
    slots = pieces // 2
    inner, _, _, m, _ = lesser_green.shape
    group = m // slots
    parts = next((n for n in (3, 2) if group % (16 * n) == 0), 1)
    rows = group // parts
    chunks = 2
    index = lax.axis_index("energy")
    where = jnp.stack([index // 2, index % 2, lax.axis_index("blk") % 2]).astype(jnp.int32)
    others = range(1, slots)

    both = (lesser_green, greater_green)
    found = cut(where, both, slots, list(others))
    greens = [swap(found[j - 1], 2 * j) for j in others]
    greens = [*cut(where, both, slots, [0]), *greens]
    left, right = coupling_matrices(where, coulomb_blocks[0], slots)

    middle = (slots + 1) // 2
    mine = [pack(group) for group in (greens[:middle], greens[middle:])]
    sib = [swap(piece, 1) for piece in mine]

    pol, near, after = [], [], []
    for c in range(chunks):
        found = correlate(where, mine, sib, chunks, c, after)
        after = [found[0]]
        pol.append([swap(found[j], 2 * j) for j in others])
        near.append([trade(found[0], 0), found[0], trade(found[0], 1)])

    starts = [screen(where, left, right, [near[c][1], *pol[c]], slots) for c in range(chunks)]

    screens = []
    after = [piece for triple in near for piece in (triple[0], triple[2])] + [near[-1][1]]
    for c in range(chunks):
        far = pack(pol[c], after=after)
        crossed = [near[c][0], trade(far, 0), near[c][2], trade(far, 1)]
        after = [far, starts[0]]
        found = screen(where, left, right, crossed, slots, starts[c])
        screens.append([found[0]] + [swap(found[j], 2 * j) for j in others])

    into = None
    for h in range(parts):
        found = self_energy(where, mine, sib, screens, h, rows)
        own = [found[0]] + [swap(found[j], 2 * j) for j in others]
        other = swap(jnp.stack([piece[1] for piece in own]), 1)
        into = collect(where, own, other, h, parts, into)
    return tuple(into)


def solution(mesh):
    return jax.shard_map(
        local,
        mesh=mesh,
        in_specs=(
            P("energy", "blk", None, None, None),
            P("energy", "blk", None, None, None),
            P("blk", None, None, None, None),
        ),
        out_specs=(P("energy", "blk", None, None, None), P("energy", "blk", None, None, None)),
        check_vma=False,
    )
```

```python
import functools
import math

import jax
import jax.numpy as jnp
from jax import lax
from jax.experimental import pallas as pl
from jax.experimental.pallas import tpu as pltpu
from jax.sharding import PartitionSpec as P

f32 = jnp.float32
bf16 = jnp.bfloat16


def swap(value, distance):
    count = lax.axis_size("energy")
    return lax.ppermute(value, "energy", [(i, i ^ distance) for i in range(count)])


def trade(value, first):
    count = lax.axis_size("blk")
    lows = range(first, count - 1, 2)
    return lax.ppermute(value, "blk", [(i, i + 1) for i in lows] + [(i + 1, i) for i in lows])


def row_block(rows):
    for size in (16, 8):
        if rows % size == 0:
            return size
    return rows


def out_like(shape):
    return jax.ShapeDtypeStruct(shape, bf16)


def vpu_cost(total, elements, moved):
    return pl.CostEstimate(
        flops=3 * total * (total + 1) * elements, bytes_accessed=2 * moved, transcendentals=0
    )


def tiles(rows, cols, body):
    lanes = 128 if cols % 128 == 0 else cols
    sub = 8 if rows % 8 == 0 else rows
    across = cols // lanes

    def step(t, carry):
        r = pl.multiple_of(lax.div(t, across) * sub, sub)
        c = pl.multiple_of(lax.rem(t, across) * lanes, lanes)
        body((pl.ds(r, sub), pl.ds(c, lanes)))
        return carry

    lax.fori_loop(0, (rows // sub) * across, step, 0)


def lag_of(total, slots, chunks, chunk, slot, i):
    return (chunks - 1 - chunk) * (total // chunks) + slot * (total // (chunks * slots)) + i


def load_greens(slots, inner, where, mine, sib, put):
    chip, core = where[0], where[1]
    for half, sources in ((core, mine), (1 - core, sib)):
        j = 0
        for source in sources:
            for k in range(source.shape[0]):
                for i in range(inner):
                    put((2 * (chip ^ j) + half) * inner + i, source, k, i)
                j += 1


def correlate_kernel(slots, inner, chunks, chunk, halves, extra, where, *rest):
    mine, sib = rest[:halves], rest[halves : 2 * halves][::-1]
    rest = rest[2 * halves + extra :]
    outs, (x_scr, y_scr, o_scr) = rest[:slots], rest[slots:]
    chip, core = where[0], where[1]
    total = 2 * inner * slots
    rows, cols = mine[0].shape[-2:]

    def put(e, source, k, i):
        a = source[k, i, core, 0].astype(f32)
        b = source[k, i, core, 1].astype(f32)
        x_scr[0, e], x_scr[1, e], x_scr[2, e] = a, b, a + b
        a = source[k, i, 1 - core, 0].astype(f32)
        b = source[k, i, 1 - core, 1].astype(f32)
        y_scr[0, e], y_scr[1, e], y_scr[2, e] = a, b, a - b

    load_greens(slots, inner, where, mine, sib, put)
    factor = -1.0 / math.sqrt(total)
    width = 4
    first_lag = lag_of(total, slots, chunks, chunk, 0, 0)
    last_lag = first_lag + total // chunks

    def body(at):
        for base in range(first_lag, last_lag, width):
            lags = range(base, min(base + width, last_lag))
            sums = {}
            window = {}
            for e in range(total - base):
                y = [y_scr[(p, e) + at] for p in range(3)]
                for w in lags:
                    if e + w >= total:
                        continue
                    if e + w not in window:
                        window[e + w] = [x_scr[(p, e + w) + at] for p in range(3)]
                    terms = [window[e + w][p] * y[p] for p in range(3)]
                    sums[w] = [s + t for s, t in zip(sums[w], terms)] if w in sums else terms
                window.pop(e + base, None)
            for w in lags:
                first, second, third = sums[w]
                o_scr[(w - first_lag, 0) + at] = factor * (first + second)
                o_scr[(w - first_lag, 1) + at] = factor * (third - first + second)

    tiles(rows, cols, body)
    each = 2 * inner // chunks
    for j in range(slots):
        for i in range(each):
            outs[j][i] = o_scr[(chip ^ j) * each + i].astype(bf16)


def correlate(where, mine, sib, chunks, chunk, after):
    _, inner, _, _, rows, cols = mine[0].shape
    slots = sum(piece.shape[0] for piece in mine)
    total = 2 * inner * slots
    each = 2 * inner // chunks
    block = row_block(rows)
    in_specs = [
        pl.BlockSpec((piece.shape[0], inner, 2, 2, block, cols), lambda r, s: (0, 0, 0, 0, r, 0))
        for piece in (*mine, *sib[::-1])
    ]
    out_spec = pl.BlockSpec((each, 2, block, cols), lambda r, s: (0, 0, r, 0))
    return pl.pallas_call(
        functools.partial(correlate_kernel, slots, inner, chunks, chunk, len(mine), len(after)),
        name="correlate",
        out_shape=[out_like((each, 2, rows, cols))] * slots,
        grid_spec=pltpu.PrefetchScalarGridSpec(
            num_scalar_prefetch=1,
            grid=(rows // block,),
            in_specs=in_specs + [pl.BlockSpec(memory_space=pl.ANY)] * len(after),
            out_specs=[out_spec] * slots,
            scratch_shapes=[
                pltpu.VMEM((3, total, block, cols), f32),
                pltpu.VMEM((3, total, block, cols), f32),
                pltpu.VMEM((total // chunks, 2, block, cols), f32),
            ],
        ),
        compiler_params=pltpu.CompilerParams(vmem_limit_bytes=16 * 2**20),
        cost_estimate=vpu_cost(total, rows * cols // chunks, 4 * total * rows * cols),
    )(where, *mine, *sib[::-1], *after)


def sigma_kernel(slots, inner, chunks, halves, where, *rest):
    mine, sib = rest[:halves], rest[halves : 2 * halves][::-1]
    rest = rest[2 * halves :]
    screens = rest[: slots * chunks]
    outs = rest[slots * chunks : slots * chunks + slots]
    x_scr, y_scr, o_scr = rest[slots * chunks + slots :]
    chip, core = where[0], where[1]
    total = 2 * inner * slots
    rows, cols = mine[0].shape[-2:]
    each = 2 * inner // chunks

    def put(e, source, k, i):
        a = source[k, i, 0, 0].astype(f32)
        b = source[k, i, 0, 1].astype(f32)
        x_scr[0, e], x_scr[1, e], x_scr[2, e] = a, b, a + b

    load_greens(slots, inner, where, mine, sib, put)
    for j in range(slots):
        for chunk in range(chunks):
            source = screens[chunk * slots + j]
            for i in range(each):
                w = lag_of(total, slots, chunks, chunk, chip ^ j, i)
                a = source[i, 0].astype(f32)
                b = source[i, 1].astype(f32)
                y_scr[0, w], y_scr[1, w], y_scr[2, w] = a, b, a + b
    factor = 1.0 / math.sqrt(total)
    width = 4

    def body(at):
        for base in range(0, total, width):
            energies = range(base, min(base + width, total))
            sums = {}
            window = {}
            for w in range(min(base + width, total)):
                y = [y_scr[(p, w) + at] for p in range(3)]
                for e in energies:
                    if e < w:
                        continue
                    if e - w not in window:
                        window[e - w] = [x_scr[(p, e - w) + at] for p in range(3)]
                    terms = [window[e - w][p] * y[p] for p in range(3)]
                    sums[e] = [s + t for s, t in zip(sums[e], terms)] if e in sums else terms
                window.pop(base + width - 1 - w, None)
            for e in energies:
                first, second, third = sums[e]
                o_scr[(e, 0) + at] = factor * (first - second)
                o_scr[(e, 1) + at] = factor * (third - first - second)

    tiles(rows, cols, body)
    for j in range(slots):
        for side in range(2):
            half = core if side == 0 else 1 - core
            for i in range(inner):
                e = (2 * (chip ^ j) + half) * inner + i
                outs[j][side, i] = o_scr[e].astype(bf16)


def self_energy(where, mine, sib, screens, part, rows):
    _, inner, _, _, _, cols = mine[0].shape
    slots = sum(piece.shape[0] for piece in mine)
    chunks = len(screens)
    flat = [piece for chunk in screens for piece in chunk]
    each = flat[0].shape[0]
    total = 2 * inner * slots
    block = row_block(rows)
    steps = rows // block
    green_specs = [
        pl.BlockSpec(
            (piece.shape[0], inner, 1, 2, block, cols),
            lambda r, s: (0, 0, s[1], 0, part * steps + r, 0),
        )
        for piece in (*mine, *sib[::-1])
    ]
    screen_spec = pl.BlockSpec((each, 2, block, cols), lambda r, s: (0, 0, part * steps + r, 0))
    out_spec = pl.BlockSpec((2, inner, 2, block, cols), lambda r, s: (0, 0, 0, r, 0))
    return pl.pallas_call(
        functools.partial(sigma_kernel, slots, inner, chunks, len(mine)),
        name="sigma",
        out_shape=[out_like((2, inner, 2, rows, cols))] * slots,
        grid_spec=pltpu.PrefetchScalarGridSpec(
            num_scalar_prefetch=1,
            grid=(steps,),
            in_specs=green_specs + [screen_spec] * len(flat),
            out_specs=[out_spec] * slots,
            scratch_shapes=[
                pltpu.VMEM((3, total, block, cols), f32),
                pltpu.VMEM((3, total, block, cols), f32),
                pltpu.VMEM((total, 2, block, cols), f32),
            ],
        ),
        compiler_params=pltpu.CompilerParams(vmem_limit_bytes=16 * 2**20),
        cost_estimate=vpu_cost(total, rows * cols, 6 * total * rows * cols),
    )(where, *mine, *sib[::-1], *flat)


def cut_kernel(count, where, *rest):
    for k in range(count):
        for kind in range(2):
            rest[2 * count + k][0, kind] = rest[kind * count + k][0, 0]


def cut(where, greens, slots, wanted):
    inner, _, _, m, _ = greens[0].shape
    group = m // slots
    count = len(wanted)
    if group % 16:
        return [
            jnp.stack(
                [
                    lax.dynamic_slice_in_dim(g[:, 0], (where[0] ^ j) * group, group, axis=2)
                    for g in greens
                ],
                axis=1,
            )
            for j in wanted
        ]

    def block(j):
        return pl.BlockSpec((1, 1, 2, group, m), lambda e, s: (e, 0, 0, s[0] ^ j, 0))

    return pl.pallas_call(
        functools.partial(cut_kernel, count),
        name="cut_rows",
        out_shape=[out_like((inner, 2, 2, group, m))] * count,
        grid_spec=pltpu.PrefetchScalarGridSpec(
            num_scalar_prefetch=1,
            grid=(inner,),
            in_specs=[block(j) for j in wanted] * 2,
            out_specs=[pl.BlockSpec((1, 2, 2, group, m), lambda e, s: (e, 0, 0, 0, 0))] * count,
        ),
        compiler_params=pltpu.CompilerParams(vmem_limit_bytes=56 * 2**20),
        cost_estimate=pl.CostEstimate(flops=0, bytes_accessed=16 * inner * count * group * m, transcendentals=0),
    )(where, *([greens[0]] * count), *([greens[1]] * count))


def matrices_kernel(slots, where, coupling, left, right, *held):
    count, _, m, _ = coupling.shape
    group = m // slots
    chip = where[0]
    for o in range(count):
        real, imag = coupling[o, 0].astype(f32), coupling[o, 1].astype(f32)
        real_t, imag_t = real.T.astype(bf16), imag.T.astype(bf16)
        right[o, :m, :m] = real_t
        right[o, :m, m:] = -imag_t
        right[o, m:, :m] = imag_t
        right[o, m:, m:] = real_t
        if held:
            held[0][0], held[0][1] = real, imag
            source = held[0]
        else:
            source = coupling.at[o]
        for j in range(slots):
            start = pl.multiple_of((chip ^ j) * group, group)
            real = source[0, pl.ds(start, group), :].astype(bf16)
            imag = source[1, pl.ds(start, group), :].astype(bf16)
            low = j * group
            left[o, low : low + group, :m] = real
            left[o, low : low + group, m:] = -imag
            left[o, m + low : m + low + group, :m] = imag
            left[o, m + low : m + low + group, m:] = real


def coupling_matrices(where, coulomb, slots):
    count, _, m, _ = coulomb.shape
    vmem = pl.BlockSpec(memory_space=pltpu.VMEM)
    held = [] if (m // slots) % 16 == 0 else [pltpu.VMEM((2, m, m), f32)]
    return pl.pallas_call(
        functools.partial(matrices_kernel, slots),
        name="coupling",
        out_shape=[out_like((count, 2 * m, 2 * m))] * 2,
        in_specs=[pl.BlockSpec(memory_space=pltpu.SMEM), vmem],
        out_specs=[vmem, vmem],
        scratch_shapes=held,
        compiler_params=pltpu.CompilerParams(vmem_limit_bytes=20 * 2**20),
        cost_estimate=pl.CostEstimate(flops=0, bytes_accessed=20 * coulomb.size, transcendentals=0),
    )(where, coulomb)


def pack_kernel(pieces, extra, *refs):
    for k in range(pieces):
        refs[pieces + extra][k] = refs[k][...]


def pack(pieces, block=None, index=None, after=()):
    count = len(pieces)
    block = block or pieces[0].shape
    index = index or (0,) * len(block)
    size = math.prod(block)
    return pl.pallas_call(
        functools.partial(pack_kernel, count, len(after)),
        name="pack",
        out_shape=out_like((count,) + block),
        grid=(1,),
        in_specs=[pl.BlockSpec(block, lambda i: index)] * count
        + [pl.BlockSpec(memory_space=pl.ANY)] * len(after),
        out_specs=pl.BlockSpec((count,) + block, lambda i: (0,) * (1 + len(block))),
        compiler_params=pltpu.CompilerParams(vmem_limit_bytes=16 * 2**20),
        cost_estimate=pl.CostEstimate(flops=0, bytes_accessed=4 * count * size, transcendentals=0),
    )(*pieces, *after)


def screen_kernel(slots, each, final, where, left_ref, right_ref, *rest):
    odd = where[2]
    neighbours = (2 - 2 * odd, 2 * odd) if final else (1,)
    count = len(neighbours)
    per_source = 2 if final else slots
    sources, rest = rest[: per_source * count], rest[per_source * count :]
    if final:
        start_ref, rest = rest[0], rest[1:]
    outs, (pol, left) = rest[:-2], rest[-2:]
    rows, m = sources[0].shape[2:]
    chip = where[0]
    for n in range(count):
        near, far = sources[per_source * n], sources[per_source * n + 1 : per_source * (n + 1)]
        for j in range(slots):
            for part in range(2):
                start = pl.multiple_of(part * m + (chip ^ j) * rows, rows)
                for i in range(each):
                    if j == 0:
                        piece = near[i, part]
                    else:
                        piece = far[0][j - 1, i, part] if final else far[j - 1][i, part]
                    pol[n, i, pl.ds(start, rows), :] = piece.astype(pol.dtype)
    for n, o in enumerate(neighbours):
        both = jnp.concatenate([pol[n, i].astype(bf16) for i in range(each)], axis=1)
        product = jnp.dot(left_ref[o], both, preferred_element_type=f32).astype(bf16)
        for i in range(each):
            for part in range(2):
                left[i, :, (2 * n + part) * m : (2 * n + part + 1) * m] = product[
                    part * m : (part + 1) * m, i * m : (i + 1) * m
                ]
    for i in range(each):
        result = start_ref[i] if final else None
        for n, o in enumerate(neighbours):
            term = jnp.dot(
                left[i, :, 2 * n * m : 2 * (n + 1) * m],
                right_ref[o],
                preferred_element_type=f32,
            )
            result = term if result is None else result + term
        if not final:
            outs[0][i] = result
            continue
        result = result.astype(bf16)
        for j in range(slots):
            for part in range(2):
                outs[j][i, part] = result[j * rows : (j + 1) * rows, part * m : (part + 1) * m]


def screen(where, left_matrix, right_matrix, sources, slots, start=None):
    each, _, rows, m = sources[0].shape
    count = 1 if start is None else 2
    vmem = pl.BlockSpec(memory_space=pltpu.VMEM)
    flops = 16 * each * count * m * m * m
    moved = 4 * each * m * m * (count + 1) + 2 * (left_matrix.size + right_matrix.size)
    hold = bf16 if rows % 16 == 0 else f32
    final = start is not None
    if final:
        shapes = [out_like((each, 2, rows, m))] * slots
    else:
        shapes = [jax.ShapeDtypeStruct((each, m, 2 * m), f32)]
    operands = list(sources) + ([start] if final else [])
    found = pl.pallas_call(
        functools.partial(screen_kernel, slots, each, final),
        name="screen",
        out_shape=shapes,
        in_specs=[pl.BlockSpec(memory_space=pltpu.SMEM)] + [vmem] * (2 + len(operands)),
        out_specs=[vmem] * len(shapes),
        scratch_shapes=[
            pltpu.VMEM((count, each, 2 * m, m), hold),
            pltpu.VMEM((each, m, 2 * count * m), bf16),
        ],
        compiler_params=pltpu.CompilerParams(vmem_limit_bytes=28 * 2**20),
        cost_estimate=pl.CostEstimate(flops=flops, bytes_accessed=moved, transcendentals=0),
    )(where, left_matrix, right_matrix, *operands)
    return found if final else found[0]


def collect_kernel(slots, parts, where, *rest):
    own, other = rest[: slots * parts], rest[slots * parts : -2]
    less, great = rest[-2:]
    core = where[1]
    rows = own[0].shape[3]
    for j in range(slots):

        @pl.when(pl.program_id(0) == j)
        def _(j=j):
            for h in range(parts):
                mine, theirs = own[h * slots + j][0], other[h][j]
                at = slice(h * rows, (h + 1) * rows)
                less[:, 0, :, at] = jnp.where(core == 0, mine, theirs)
                great[:, 0, :, at] = jnp.where(core == 0, theirs, mine)


def collect(where, own, other):
    parts, slots = len(own), len(own[0])
    _, inner, _, rows, m = own[0][0].shape
    shape = (inner, 1, 2, m, m)
    if rows % 16:
        target = jnp.zeros((2,) + shape, bf16)
        for h in range(parts):
            for j in range(slots):
                pair = jnp.stack([own[h][j][0], other[h][j]])
                pair = jnp.where(where[1] == 0, pair, pair[::-1])[:, :, None]
                start = ((where[0] ^ j) * parts + h) * rows
                target = lax.dynamic_update_slice_in_dim(target, pair, start, axis=4)
        return target[0], target[1]
    flat = [piece for pieces in own for piece in pieces]
    specs = [pl.BlockSpec((1, inner, 2, rows, m), lambda i, s: (0, 0, 0, 0, 0))] * len(flat)
    specs += [pl.BlockSpec((slots, inner, 2, rows, m), lambda i, s: (0, 0, 0, 0, 0))] * parts
    target = pl.BlockSpec((inner, 1, 2, rows * parts, m), lambda i, s: (0, 0, 0, s[0] ^ i, 0))
    return pl.pallas_call(
        functools.partial(collect_kernel, slots, parts),
        name="collect",
        out_shape=[out_like(shape)] * 2,
        grid_spec=pltpu.PrefetchScalarGridSpec(
            num_scalar_prefetch=1,
            grid=(slots,),
            in_specs=specs,
            out_specs=[target] * 2,
        ),
        compiler_params=pltpu.CompilerParams(vmem_limit_bytes=20 * 2**20),
        cost_estimate=pl.CostEstimate(
            flops=0, bytes_accessed=16 * inner * m * m, transcendentals=0
        ),
    )(where, *flat, *other)


def local(lesser_green, greater_green, coulomb_blocks):
    pieces = lax.axis_size("energy")
    slots = pieces // 2
    inner, _, _, m, _ = lesser_green.shape
    group = m // slots
    parts = next((n for n in (3, 2) if group % (16 * n) == 0), 1)
    rows = group // parts
    chunks = 2
    index = lax.axis_index("energy")
    where = jnp.stack([index // 2, index % 2, lax.axis_index("blk") % 2]).astype(jnp.int32)
    others = range(1, slots)

    both = (lesser_green, greater_green)
    found = cut(where, both, slots, list(others))
    greens = [swap(found[j - 1], 2 * j) for j in others]
    greens = [*cut(where, both, slots, [0]), *greens]
    left, right = coupling_matrices(where, coulomb_blocks[0], slots)

    middle = (slots + 1) // 2
    mine = [pack(group) for group in (greens[:middle], greens[middle:])]
    sib = [swap(piece, 1) for piece in mine]

    pol, near, after = [], [], []
    for c in range(chunks):
        found = correlate(where, mine, sib, chunks, c, after)
        after = [found[0]]
        pol.append([swap(found[j], 2 * j) for j in others])
        near.append([trade(found[0], 0), found[0], trade(found[0], 1)])

    starts = [screen(where, left, right, [near[c][1], *pol[c]], slots) for c in range(chunks)]

    screens = []
    after = [piece for triple in near for piece in (triple[0], triple[2])] + [near[-1][1]]
    for c in range(chunks):
        far = pack(pol[c], after=after)
        crossed = [near[c][0], trade(far, 0), near[c][2], trade(far, 1)]
        after = [far, starts[0]]
        found = screen(where, left, right, crossed, slots, starts[c])
        screens.append([found[0]] + [swap(found[j], 2 * j) for j in others])

    own, other = [], []
    for h in range(parts):
        found = self_energy(where, mine, sib, screens, h, rows)
        own.append([found[0]] + [swap(found[j], 2 * j) for j in others])
        other.append(swap(jnp.stack([piece[1] for piece in own[h]]), 1))
    return tuple(collect(where, own, other))


def solution(mesh):
    return jax.shard_map(
        local,
        mesh=mesh,
        in_specs=(
            P("energy", "blk", None, None, None),
            P("energy", "blk", None, None, None),
            P("blk", None, None, None, None),
        ),
        out_specs=(P("energy", "blk", None, None, None), P("energy", "blk", None, None, None)),
        check_vma=False,
    )
```
